32 devices in a mesh: fsdp: 8 (over z, x), rep: 4 (over y, core).
Axes of the slice: x: 2, y: 2, z: 4, core: 2. Of those that a mesh axis runs over, the one named last changes fastest.
Arguments:
- tokens: bfloat16 [24576, 960], P(('fsdp', 'rep')), may hold values from -6 to 6
- lengths: int32 [64, 3], P(('fsdp', 'rep')), may hold values from 1 to 288, 384 in all within a row
- attn_gain: bfloat16 [960], P('fsdp'), may hold values from 0.5 to 1.5
- w_query: bfloat16 [960, 960], P('fsdp', 'rep'), may hold values from -0.1875 to 0.1875
- w_key: bfloat16 [960, 320], P('fsdp', 'rep'), may hold values from -0.1875 to 0.1875
- w_value: bfloat16 [960, 320], P('fsdp', 'rep'), may hold values from -0.1875 to 0.1875
- w_output: bfloat16 [960, 960], P('fsdp', 'rep'), may hold values from -1.5 to 1.5
- mlp_gain: bfloat16 [960], P('fsdp'), may hold values from 0.5 to 1.5
- w_gate: bfloat16 [960, 2560], P('fsdp', 'rep'), may hold values from -0.1875 to 0.1875
- w_up: bfloat16 [960, 2560], P('fsdp', 'rep'), may hold values from -0.1875 to 0.1875
- w_down: bfloat16 [2560, 960], P('fsdp', 'rep'), may hold values from -0.125 to 0.125
- cotangent: bfloat16 [24576, 960], P(('fsdp', 'rep')), may hold values from -6 to 6
Outputs:
- output: bfloat16 [24576, 960], P(('fsdp', 'rep'))
- token_grad: bfloat16 [24576, 960], P(('fsdp', 'rep'))
- grad_attn_gain: float32 [960], P('fsdp')
- grad_query: float32 [960, 960], P('fsdp', 'rep')
- grad_key: float32 [960, 320], P('fsdp', 'rep')
- grad_value: float32 [960, 320], P('fsdp', 'rep')
- grad_output: float32 [960, 960], P('fsdp', 'rep')
- grad_mlp_gain: float32 [960], P('fsdp')
- grad_gate: float32 [960, 2560], P('fsdp', 'rep')
- grad_up: float32 [960, 2560], P('fsdp', 'rep')
- grad_down: float32 [2560, 960], P('fsdp', 'rep')
The draws below stay inside these ranges and needn't reach their ends.
Inputs may be any that keep to these rules, and one draw needn't show every extreme that they name: Each row lists the lengths of the 3 sequences of one micro-batch; they sum to 384, and in every row the longest is exactly 288.
All inputs are finite; a program needn't handle non-finite values.
Results may differ from the reference program's by a relative error of at most 0.015.
Values may be sent and summed in bfloat16 or wider, within the bound.
No kernel may reach another device: no remote copies, remote signals or barrier semaphores. Data moves between devices by JAX's collectives and lax.ppermute only.
A program may use at most 192 MiB of HBM per device.

```python
import math
import jax
import jax.numpy as jnp
import numpy as np
from jax import lax

D = 960
FF = 2560
HEADS = 15
KV_HEADS = 5
HEAD = 64
MB_TOK = 384
SEGS = 3
LONGEST = 288
GROUP = 3
QW = 960
KVW = 320
MBATCHES = 64
TOKENS = 24576


def strengthened(values, own_key, source, target, blocks, factor):
    def block_of(axis_at):
        return (jnp.arange(values.shape[axis_at]) // (values.shape[axis_at] // blocks)).reshape((-1,) + (1,) * (values.ndim - 1 - axis_at))

    first = jax.random.permutation(own_key, blocks)[block_of(target)]
    other_side = (block_of(target) + blocks // 2) % blocks
    return jnp.where((block_of(source) == first) | (block_of(source) == other_side), factor * values, values)


def block_scale(rng, extent, shards, low, high):
    def one(dim, blocks):
        draws = jax.random.uniform(jax.random.fold_in(jax.random.fold_in(rng, 6), dim), (blocks,), jnp.float32, low / len(shards), high / len(shards))
        return jnp.repeat(jnp.exp(draws), extent[dim] // blocks).reshape((-1,) + (1,) * (len(extent) - dim - 1))

    gain = one(*shards[0])
    for cut in shards[1:]:
        gain = gain * one(*cut)
    return gain


def profile(number_of, total, limit, slope):
    loads = [(1 << 20) // math.isqrt(rank ** slope) + 1 for rank in range(2, number_of + 1)]
    surplus, counts = total - limit - (number_of - 1), [1] * (number_of - 1)
    while surplus > 0:
        candidates = [i for i in range(number_of - 1) if counts[i] < limit]
        mass, left = sum([loads[i] for i in candidates]), surplus
        for i in candidates:
            addition = min(limit - counts[i], max(1, left * loads[i] // mass), surplus)
            counts[i] = counts[i] + addition
            surplus = surplus - addition
    return np.array([limit] + counts)


def uneven(own_key, number_of, total, bound, lean):
    if number_of == 2:
        one = jax.random.randint(own_key, (), max(1, total - bound), min(bound, total - 1) + 1)
        return jnp.stack([one, total - one])
    sizes = jnp.asarray(profile(number_of, total, bound, lean), jnp.int32)
    couples = (number_of - 1) // 2
    source_of, sink = sizes[1:1 + 2 * couples:2], sizes[2:2 + 2 * couples:2]
    slack = jnp.minimum(source_of - 1, bound - sink)
    shifted = jax.random.randint(jax.random.fold_in(own_key, 1), (couples,), 0, 1 << 20) % (slack + 1)
    sizes = sizes.at[1:1 + 2 * couples:2].set(source_of - shifted).at[2:2 + 2 * couples:2].set(sink + shifted)
    return sizes[jax.random.permutation(jax.random.fold_in(own_key, 2), number_of)]


def gaussian(own_key, dims, scale, most, shards=(), kind=jnp.bfloat16):
    gain = block_scale(own_key, dims, shards, -0.22, 0.18) if shards else 1.0
    array = jax.random.normal(own_key, dims, jnp.float32) * scale * gain
    return jnp.minimum(jnp.maximum(array, -most), most).astype(kind)


def gaussian_with(stream_key, shape, deviation, limit, shards, heavy, kind=jnp.bfloat16):
    array = deviation * jax.random.normal(stream_key, shape, jnp.float32)
    if shards:
        array = array * block_scale(stream_key, shape, shards, -0.22, 0.18)
    return jnp.clip(strengthened(array, jax.random.fold_in(stream_key, 3), *heavy), -limit, limit).astype(kind)


def setup_inputs(seed: int = 0) -> dict:
    streams_of = jax.random.split(jax.random.key(seed), 13)
    tokens = gaussian(streams_of[0], (TOKENS, D), 1.0, 6.0, ((0, 32),))
    lengths = jax.vmap(lambda own: uneven(own, SEGS, MB_TOK, LONGEST, 2))(jax.random.split(streams_of[1], MBATCHES)).reshape((MBATCHES, SEGS)).astype(jnp.int32)
    attn_gain = jnp.clip(1.0 + 0.1 * jax.random.normal(streams_of[2], (D,), jnp.float32), 0.5, 1.5).astype(jnp.bfloat16)
    w_query = gaussian(streams_of[3], (D, QW), D ** -0.5, 0.1875, ((0, 8), (1, 4)))
    w_key = gaussian(streams_of[4], (D, KVW), D ** -0.5, 0.1875, ((0, 8), (1, 4)))
    w_value = gaussian(streams_of[5], (D, KVW), D ** -0.5, 0.1875, ((0, 8), (1, 4)))
    w_output = gaussian(streams_of[6], (QW, D), (D // 64) ** -0.5, 1.5, ((0, 8), (1, 4)))
    mlp_gain = jnp.clip(1.0 + 0.1 * jax.random.normal(streams_of[7], (D,), jnp.float32), 0.5, 1.5).astype(jnp.bfloat16)
    w_gate = gaussian(streams_of[8], (D, FF), D ** -0.5, 0.1875, ((0, 8), (1, 4)))
    w_up = gaussian(streams_of[9], (D, FF), D ** -0.5, 0.1875, ((0, 8), (1, 4)))
    w_down = gaussian(streams_of[10], (FF, D), FF ** -0.5, 0.125, ((0, 8), (1, 4)))
    cotangent = gaussian_with(streams_of[11], (TOKENS, D), 1.0, 6.0, ((0, 32),), (0, 1, 32, 2.75))
    return {"tokens": tokens, "lengths": lengths, "attn_gain": attn_gain, "w_query": w_query, "w_key": w_key, "w_value": w_value, "w_output": w_output, "mlp_gain": mlp_gain, "w_gate": w_gate, "w_up": w_up, "w_down": w_down, "cotangent": cotangent}


@jax.custom_vjp
def low(v):
    return lax.optimization_barrier(v.astype(jnp.bfloat16)).astype(jnp.float32)

@jax.custom_vjp
def low_back(v):
    return v

def low_keep(v):
    return (low(v), None)

def low_pass(kept, grad):
    return (grad,)

def back_keep(v):
    return (v, None)

def back_low(kept, grad):
    return (low(grad),)
low.defvjp(low_keep, low_pass)
low_back.defvjp(back_keep, back_low)
norm_epsilon = 1e-05
rope_base = 100000.0
masked_value = -1e+30

def layout(length_row):
    seq_sizes = length_row.astype(jnp.int32)
    starts = jnp.cumsum(seq_sizes) - seq_sizes
    places = jnp.arange(MB_TOK, dtype=jnp.int32)
    inside = ((places[:, None] >= starts[None, :]) & (places[:, None] < (starts + seq_sizes)[None, :])).astype(jnp.int32)
    segment = lax.optimization_barrier(jnp.sum(inside * jnp.arange(SEGS, dtype=jnp.int32)[None, :], axis=1))
    position = places - lax.optimization_barrier(jnp.sum(inside * starts[None, :], axis=1))
    return (segment, position)

def visible(segment):
    places = jnp.arange(MB_TOK, dtype=jnp.int32)
    return (segment[:, None] == segment[None, :]) & (places[None, :] <= places[:, None])

def rope_tables(position):
    half_width = HEAD // 2
    exponent = jnp.arange(half_width, dtype=jnp.float32) * (2.0 / HEAD)
    inverse = jnp.power(rope_base, -exponent)
    angles = position.astype(jnp.float32)[..., None] * inverse
    return (jnp.cos(angles), jnp.sin(angles))

def rotate(values, cosine_table, sine_table):
    half_width = values.shape[-1] // 2
    first_half = values[..., :half_width]
    second_half = values[..., half_width:]
    cosine_rows = cosine_table[..., None, :]
    sine_rows = sine_table[..., None, :]
    return jnp.concatenate([first_half * cosine_rows - second_half * sine_rows, second_half * cosine_rows + first_half * sine_rows], axis=-1)

def rms_norm(values, gain_row):
    scale_rows = lax.rsqrt(lax.optimization_barrier(jnp.mean(values * values, axis=-1, keepdims=True)) + norm_epsilon)
    return values * scale_rows * gain_row

def product(left, right):
    return jnp.dot(left, right, precision=lax.Precision.HIGHEST)

def forward(block_in, segment, position, attn_gain, w_query, w_key, w_value, w_output, mlp_gain, w_gate, w_up, w_down):
    cosine_table, sine_table = rope_tables(position)
    normed = low(rms_norm(block_in, attn_gain))
    query_lin = low_back(product(normed, w_query)).reshape(MB_TOK, HEADS, HEAD)
    key_lin = low_back(product(normed, w_key)).reshape(MB_TOK, KV_HEADS, HEAD)
    value_rows = low(low_back(product(normed, w_value))).reshape(MB_TOK, KV_HEADS, HEAD)
    query_rot = low(rotate(query_lin, cosine_table, sine_table)).reshape(MB_TOK, KV_HEADS, GROUP, HEAD)
    key_rot = low(rotate(key_lin, cosine_table, sine_table))
    scores = jnp.einsum('qkgd,pkd->kgqp', query_rot, key_rot, precision=lax.Precision.HIGHEST)
    scores = low_back(scores * HEAD ** (-0.5))
    scores = jnp.where(visible(segment)[None, None], scores, masked_value)
    probs_low = low(jax.nn.softmax(scores, axis=-1))
    mixed = jnp.einsum('kgqp,pkd->qkgd', probs_low, value_rows, precision=lax.Precision.HIGHEST)
    mixed = low(low_back(mixed.reshape(MB_TOK, QW)))
    middle = block_in + low_back(product(mixed, w_output))
    normed_two = low(rms_norm(middle, mlp_gain))
    gate_lin = low_back(product(normed_two, w_gate))
    up_lin = low_back(product(normed_two, w_up))
    hidden = low(jax.nn.silu(gate_lin) * up_lin)
    return middle + low_back(product(hidden, w_down))

def reference(tokens, lengths, attn_gain, w_query, w_key, w_value, w_output, mlp_gain, w_gate, w_up, w_down, cotangent):
    weights_f = tuple((weight.astype(jnp.float32) for weight in (attn_gain, w_query, w_key, w_value, w_output, mlp_gain, w_gate, w_up, w_down)))
    token_blocks = tokens.astype(jnp.float32).reshape(MBATCHES, MB_TOK, D)
    cot_blocks = cotangent.astype(jnp.float32).reshape(MBATCHES, MB_TOK, D)

    def one_block(running, block_items):
        block_in, length_row, cot_block = block_items
        segment, position = layout(length_row)

        def apply_block(block_rows, *layer_weights):
            return forward(block_rows, segment, position, *layer_weights)
        result, pullback = jax.vjp(apply_block, block_in, *weights_f)
        gradients = pullback(cot_block)
        running = tuple((before + addend for before, addend in zip(running, gradients[1:])))
        return (running, (result.astype(jnp.bfloat16), gradients[0].astype(jnp.bfloat16)))
    start_totals = tuple((jnp.zeros(weight.shape, jnp.float32) for weight in weights_f))
    totals, (outputs, token_grads) = lax.scan(one_block, start_totals, (token_blocks, lengths, cot_blocks))
    return (outputs.reshape(TOKENS, D), token_grads.reshape(TOKENS, D), totals[0], totals[1], totals[2], totals[3], totals[4], totals[5], totals[6], totals[7], totals[8])
```

```python
import jax
import jax.numpy as jnp
from jax import lax
from jax.experimental import pallas as pl
from jax.experimental.pallas import tpu as pltpu
from jax.sharding import PartitionSpec as P

D = 960
FF = 2560
HEADS = 15
KV_HEADS = 5
HEAD = 64
MB_TOK = 384
SEGS = 3
GROUP = 3
QW = 960
KVW = 320

SLOTS = 8
REPS = 4
USED = 120
SLOT = 128
WIDE = SLOTS * SLOT
PACK = 640
HALF_PACK = 320
ROWS_A = 64
VMEM_BYTES = 60 * 1024 * 1024

norm_epsilon = 1e-05
rope_base = 100000.0
masked_value = -1e30

f32 = jnp.float32
bf16 = jnp.bfloat16


def layout(length_row):
    starts = jnp.cumsum(length_row) - length_row
    places = jnp.arange(MB_TOK, dtype=jnp.int32)
    inside = (
        (places[:, None] >= starts[None, :]) & (places[:, None] < (starts + length_row)[None, :])
    ).astype(jnp.int32)
    segment = jnp.sum(inside * jnp.arange(SEGS, dtype=jnp.int32)[None, :], axis=1)
    position = places - jnp.sum(inside * starts[None, :], axis=1)
    return (segment, position)


def rope_tables(position):
    half_width = HEAD // 2
    exponent = jnp.arange(half_width, dtype=f32) * (2.0 / HEAD)
    inverse = jnp.power(rope_base, -exponent)
    angles = position.astype(f32)[:, None] * inverse
    cosines, sines = (jnp.cos(angles), jnp.sin(angles))
    return (
        jnp.concatenate([cosines] * 4, axis=1),
        jnp.concatenate([-sines, sines, -sines, sines], axis=1),
    )


def slot_of(eighth):
    return (eighth & 1) * 4 + (eighth >> 1)


def eighth_of(slot):
    return (slot & 3) * 2 + (slot >> 2)


def feature_lanes(eighth_here):
    lanes = jnp.arange(WIDE, dtype=jnp.int32)
    eighth = eighth_of(lanes // SLOT) ^ eighth_here
    return jnp.where(lanes % SLOT < USED, eighth * USED + lanes % SLOT, -1)


def one_hot(rows, wanted):
    return (jnp.arange(rows, dtype=jnp.int32)[:, None] == wanted[None, :]).astype(bf16)


def placing(eighth_here, quarter_here):
    features = feature_lanes(eighth_here)
    spread = one_hot(WIDE, features)
    columns = jnp.arange(WIDE, dtype=jnp.int32)
    query_from = jnp.where(
        columns < QW, ((columns // 240) ^ quarter_here) * 256 + columns % 240, -1
    )
    key_columns = jnp.arange(384, dtype=jnp.int32)
    key_from = ((key_columns // 80) ^ quarter_here) * 384 + key_columns % 80
    key_value_from = jnp.concatenate(
        [
            jnp.where(key_columns < KVW, key_from + 112, -1),
            jnp.where(key_columns < KVW, key_from + 192, -1),
        ]
    )
    output_from = jnp.where(
        features >= 0, ((features // 240) ^ quarter_here) * 256 + 16 + features % 240, -1
    )
    return (
        spread,
        one_hot(1024, query_from),
        one_hot(1536, key_value_from),
        one_hot(1024, output_from),
    )


def dot_nn(left, right):
    return lax.dot_general(left, right, (((1,), (0,)), ((), ())), preferred_element_type=f32)


def dot_nt(left, right):
    return lax.dot_general(left, right, (((1,), (1,)), ((), ())), preferred_element_type=f32)


def dot_tn(left, right):
    return lax.dot_general(left, right, (((0,), (0,)), ((), ())), preferred_element_type=f32)


def lane_index(shape):
    return lax.broadcasted_iota(jnp.int32, shape, len(shape) - 1)


def swapped(values):
    first = (lane_index(values.shape) & 63) < 32
    return jnp.where(first, pltpu.roll(values, 96, 1), pltpu.roll(values, 32, 1))


def turned(values, cosines, sines):
    return values * cosines + swapped(values) * sines


def both_halves(values, odd):
    low = lane_index(values.shape) < 64
    moved = pltpu.roll(values, 64, 1)
    return jnp.where(low, moved, values) if odd else jnp.where(low, values, moved)


def only_half(values, odd):
    low = lane_index(values.shape) < 64
    return jnp.where(low != bool(odd), values, jnp.zeros_like(values))


def gain_row(attn_ref, which):
    rows = [attn_ref[0, s, 112:128, 0:SLOT].astype(f32)[8 + which : 9 + which] for s in range(SLOTS)]
    return jnp.concatenate(rows, axis=1)


def probs_at(part):
    return (0, 128, 384)[part]


def attn_forward_kernel(
    inputs,
    spread,
    query_from,
    key_value_from,
    output_from,
    cosines,
    sines,
    segment_rows,
    segment_columns,
    a0,
    a1,
    a2,
    a3,
    b0,
    b1,
    b2,
    b3,
    normed_out,
    query_out,
    key_out,
    value_out,
    probs_out,
    mixed_out,
    middle_out,
    normed_two_out,
    w_query,
    w_key_value,
    w_output,
    gains_out,
    attn_all,
    heads_out,
    mixed_heads,
    bias,
    sems,
):
    @pl.when(pl.program_id(0) == 0)
    def _():
        copies = []
        for quarter, source in enumerate((a0, a1, a2, a3)):
            copies.append((source, attn_all.at[quarter, :, 0:ROWS_A, :]))
        for place, source in enumerate((b0, b1, b2, b3)):
            side, core = (place >> 1, place & 1)
            for y in range(2):
                copies.append(
                    (
                        source.at[y * 4 : y * 4 + 4],
                        attn_all.at[y * 2 + core, side * 4 : side * 4 + 4, ROWS_A : 2 * ROWS_A, :],
                    )
                )
        started = [
            pltpu.make_async_copy(source, target, sems.at[n])
            for n, (source, target) in enumerate(copies)
        ]
        for copy in started:
            copy.start()
        for copy in started:
            copy.wait()

        def columns(low, high):
            return jnp.concatenate(
                [
                    attn_all[quarter, :, :, low:high].reshape(WIDE, high - low)
                    for quarter in range(REPS)
                ],
                axis=1,
            )

        w_query[...] = dot_nn(columns(0, 256), query_from[...]).astype(bf16)
        w_key_value[...] = dot_nn(columns(128, 512), key_value_from[...]).astype(bf16)
        w_output[...] = dot_nn(columns(384, 640), output_from[...]).astype(bf16)
        gains_out[0:1, :] = gain_row(attn_all, 0)
        gains_out[1:2, :] = gain_row(attn_all, 1)

    values = inputs[...].astype(f32)
    gain_one = gains_out[0:1, :]
    gain_two = gains_out[1:2, :]
    scale = lax.rsqrt(jnp.sum(values * values, axis=1, keepdims=True) * (1.0 / D) + norm_epsilon)
    normed = (values * scale * gain_one).astype(bf16)
    normed_out[...] = normed
    cosine, sine = (cosines[...], sines[...])
    query_lin = dot_nn(normed, w_query[...])
    for c in range(8):
        at = slice(c * 128, c * 128 + 128)
        query_out[:, at] = turned(query_lin[:, at], cosine, sine).astype(bf16)
    key_value = dot_nn(normed, w_key_value[...])
    for c in range(3):
        key_part = turned(key_value[:, c * 128 : c * 128 + 128], cosine, sine)
        value_part = key_value[:, 384 + c * 128 : 384 + c * 128 + 128]
        for odd in range(2 if c < 2 else 1):
            at = slice((2 * c + odd) * 128, (2 * c + odd) * 128 + 128)
            key_out[:, at] = both_halves(key_part, odd).astype(bf16)
            value_out[:, at] = both_halves(value_part, odd).astype(bf16)

    query_place = lax.broadcasted_iota(jnp.int32, (MB_TOK, MB_TOK), 0)
    key_place = lax.broadcasted_iota(jnp.int32, (MB_TOK, MB_TOK), 1)
    seen = (segment_rows[...] == segment_columns[0]) & (key_place <= query_place)
    bias[...] = jnp.where(seen, 0.0, masked_value)
    for j in range(KV_HEADS):
        at = slice(j * 128, j * 128 + 128)
        for part in range(3):
            keys = 128 * (part + 1)
            rows = slice(part * 128, part * 128 + 128)
            queries = jnp.concatenate(
                [
                    only_half(query_out[rows, (h // 2) * 128 : (h // 2) * 128 + 128], h % 2)
                    for h in range(3 * j, 3 * j + 3)
                ],
                axis=0,
            )
            scores = dot_nt(queries, key_out[0:keys, at]) * HEAD**-0.5
            hidden_part = bias[rows, 0:keys]
            scores = scores + jnp.concatenate([hidden_part] * GROUP, axis=0)
            peak = jnp.max(scores, axis=1, keepdims=True)
            weights = jnp.exp(scores - peak)
            total = jnp.sum(weights, axis=1, keepdims=True)
            probs = (weights * (1.0 / total)).astype(bf16)
            probs_out[0, j, :, probs_at(part) : probs_at(part) + keys] = probs
            gathered = dot_nn(probs, value_out[0:keys, at])
            for g in range(GROUP):
                heads_out[3 * j + g, rows, :] = gathered[g * 128 : g * 128 + 128]
    low = lane_index((MB_TOK, 128)) < 64
    for c in range(8):
        upper = heads_out[2 * c + 1] if 2 * c + 1 < HEADS else jnp.zeros((MB_TOK, 128), f32)
        mixed_heads[:, c * 128 : c * 128 + 128] = jnp.where(low, heads_out[2 * c], upper).astype(bf16)
    mixed = dot_nn(mixed_heads[...], spread[...]).astype(bf16)
    mixed_out[...] = mixed
    middle = values + dot_nn(mixed, w_output[...])
    middle_out[...] = middle
    scale_two = lax.rsqrt(
        jnp.sum(middle * middle, axis=1, keepdims=True) * (1.0 / D) + norm_epsilon
    )
    normed_two_out[...] = (middle * scale_two * gain_two).astype(bf16)


def whole_block(shape):
    return pl.BlockSpec(
        shape, lambda *ids: (0,) * len(shape), pipeline_mode=pl.Buffered(buffer_count=1)
    )


def anywhere():
    return pl.BlockSpec(memory_space=pl.ANY)


def attn_forward(inputs, places, tables, segments, first_parts, second_parts):
    tokens = inputs.shape[0]
    count = tokens // MB_TOK

    def per_batch(columns):
        return pl.BlockSpec((MB_TOK, columns), lambda i: (i, 0))

    outs = [
        jax.ShapeDtypeStruct((tokens, WIDE), bf16),
        jax.ShapeDtypeStruct((tokens, WIDE), bf16),
        jax.ShapeDtypeStruct((tokens, PACK), bf16),
        jax.ShapeDtypeStruct((tokens, PACK), bf16),
        jax.ShapeDtypeStruct((count, KV_HEADS, MB_TOK, 768), bf16),
        jax.ShapeDtypeStruct((tokens, WIDE), bf16),
        jax.ShapeDtypeStruct((tokens, WIDE), f32),
        jax.ShapeDtypeStruct((tokens, WIDE), bf16),
        jax.ShapeDtypeStruct((WIDE, 1024), bf16),
        jax.ShapeDtypeStruct((WIDE, 768), bf16),
        jax.ShapeDtypeStruct((WIDE, WIDE), bf16),
        jax.ShapeDtypeStruct((8, WIDE), f32),
    ]
    return pl.pallas_call(
        attn_forward_kernel,
        grid=(count,),
        in_specs=[per_batch(WIDE)]
        + [whole_block(place.shape) for place in places]
        + [
            per_batch(128),
            per_batch(128),
            per_batch(1),
            pl.BlockSpec((1, 1, MB_TOK), lambda i: (i, 0, 0)),
        ]
        + [anywhere()] * 8,
        out_specs=[
            per_batch(WIDE),
            per_batch(WIDE),
            per_batch(PACK),
            per_batch(PACK),
            pl.BlockSpec((1, KV_HEADS, MB_TOK, 768), lambda i: (i, 0, 0, 0)),
            per_batch(WIDE),
            per_batch(WIDE),
            per_batch(WIDE),
            whole_block((WIDE, 1024)),
            whole_block((WIDE, 768)),
            whole_block((WIDE, WIDE)),
            whole_block((8, WIDE)),
        ],
        out_shape=outs,
        scratch_shapes=[
            pltpu.VMEM((REPS, SLOTS, SLOT, PACK), bf16),
            pltpu.VMEM((HEADS, MB_TOK, 128), f32),
            pltpu.VMEM((MB_TOK, WIDE), bf16),
            pltpu.VMEM((MB_TOK, MB_TOK), f32),
            pltpu.SemaphoreType.DMA((12,)),
        ],
        compiler_params=pltpu.CompilerParams(vmem_limit_bytes=VMEM_BYTES),
        cost_estimate=pl.CostEstimate(
            flops=24_000_000_000, bytes_accessed=40_000_000, transcendentals=4_000_000
        ),
        name="attn_forward",
    )(
        inputs,
        *places,
        *tables,
        segments.reshape(tokens, 1),
        segments.reshape(count, 1, MB_TOK),
        *first_parts,
        *second_parts,
    )


def rolled(values):
    return pltpu.roll(values.astype(f32), HALF_PACK, 1)


def left_right(left, right):
    first = lane_index(left.shape) < HALF_PACK
    left, right = (left.astype(f32), right.astype(f32))
    return (
        jnp.where(first, left, pltpu.roll(right, HALF_PACK, 1)).astype(bf16),
        jnp.where(first, pltpu.roll(left, HALF_PACK, 1), right).astype(bf16),
    )


def mlp_kernel(
    here,
    normed,
    cotangent,
    cotangent_turned,
    g0,
    g1,
    g2,
    g3,
    d0,
    d1,
    d2,
    d3,
    out,
    d_normed,
    grads_zero,
    grads_one,
    down_zero,
    down_one,
    w_pair,
    down_raw,
    w_down,
    normed_turned,
    hidden_all,
    d_gate_all,
    d_up_all,
    grad_pair,
    grad_down,
    down_made,
    sem_pair,
    sem_down,
    sem_grad,
    sem_grad_down,
):
    step = pl.program_id(0)
    eighth_here, quarter_here = (here[0], here[1])
    side_here = eighth_here & 1
    slot = step & 1

    def pair_copies(at, to, core):
        return [
            pltpu.make_async_copy(
                (g0, g1, g2, g3)[side * 2 + core].at[pl.ds((at >> 1) * 4, 4)],
                w_pair.at[to, side * 4 : side * 4 + 4],
                sem_pair.at[to, side],
            )
            for side in range(2)
        ]

    def down_place(at, side):
        return side * 4 + ((at ^ quarter_here) ^ (eighth_here >> 1))

    def down_copies(at, to):
        return [
            pltpu.make_async_copy(
                (d0, d1, d2, d3)[quarter].at[down_place(at, side)],
                down_raw.at[to, side, quarter],
                sem_down.at[to, side, quarter],
            )
            for side in range(2)
            for quarter in range(REPS)
        ]

    def fetch(at, to):
        for core in range(2):

            @pl.when((at & 1) == core)
            def _():
                for copy in pair_copies(at, to, core):
                    copy.start()

        for copy in down_copies(at, to):
            copy.start()

    def grad_copies(at, to, core):
        return [
            pltpu.make_async_copy(
                grad_pair.at[to, side * 4 : side * 4 + 4],
                (grads_zero, grads_one)[core].at[side, pl.ds((at >> 1) * 4, 4)],
                sem_grad.at[to, side],
            )
            for side in range(2)
        ]

    def grad_down_copies(at, to):
        return [
            pltpu.make_async_copy(
                down_made.at[to, side, quarter],
                (down_zero, down_one)[quarter & 1].at[quarter >> 1, down_place(at, side)],
                sem_grad_down.at[to, side, quarter],
            )
            for side in range(2)
            for quarter in range(REPS)
        ]

    def settle(at, to):
        for copy in grad_copies(at, to, 0) + grad_down_copies(at, to):
            copy.wait()

    @pl.when(step == 0)
    def _():
        fetch(step, slot)
        normed_turned[...] = normed[...].T
        out[...] = jnp.zeros_like(out)
        d_normed[...] = jnp.zeros_like(d_normed)

    for copy in pair_copies(step, slot, 0) + down_copies(step, slot):
        copy.wait()

    @pl.when(step + 1 < REPS)
    def _():
        fetch(step + 1, 1 - slot)

    def rows_of(quarter, which):
        eighth = (quarter ^ quarter_here) * 2 + which
        return pl.multiple_of(slot_of(eighth ^ eighth_here) * SLOT, SLOT)

    for quarter in range(REPS):
        lefts, rights = left_right(
            down_raw[slot, side_here, quarter], down_raw[slot, 1 - side_here, quarter]
        )
        w_down[pl.ds(rows_of(quarter, 0), SLOT), :] = lefts
        w_down[pl.ds(rows_of(quarter, 1), SLOT), :] = rights

    tokens = normed.shape[0]
    w_gate = w_pair[slot, :, 0:SLOT, :].reshape(WIDE, PACK)
    w_up = w_pair[slot, :, SLOT : 2 * SLOT, :].reshape(WIDE, PACK)

    def one_tile(t, carry):
        rows = pl.ds(pl.multiple_of(t * 256, 256), 256)
        gate = dot_nn(normed[rows, :], w_gate)
        up = dot_nn(normed[rows, :], w_up)
        d_hidden = dot_nn(cotangent[rows, :], w_down[...])
        sigmoid = 1.0 / (1.0 + jnp.exp(-gate))
        silu = gate * sigmoid
        hidden = (silu * up).astype(bf16)
        d_gate = (d_hidden * up * sigmoid * (1.0 + gate * (1.0 - sigmoid))).astype(bf16)
        d_up = (d_hidden * silu).astype(bf16)
        hidden_all[rows, :] = hidden
        d_gate_all[rows, :] = d_gate
        d_up_all[rows, :] = d_up
        out[rows, :] += dot_nt(hidden, w_down[...])
        d_normed[rows, :] += dot_nt(d_gate, w_gate) + dot_nt(d_up, w_up)
        return carry

    lax.fori_loop(0, tokens // 256, one_tile, 0)

    @pl.when(step >= 2)
    def _():
        settle(step - 2, slot)

    def grad_tile(t, carry):
        rows = pl.ds(pl.multiple_of(t * 256, 256), 256)
        two = pl.ds(t * 2, 2)
        gate_part = dot_nn(normed_turned[rows, :], d_gate_all[...]).astype(bf16)
        grad_pair[slot, two, 0:SLOT, :] = gate_part.reshape(2, SLOT, PACK)
        up_part = dot_nn(normed_turned[rows, :], d_up_all[...]).astype(bf16)
        grad_pair[slot, two, SLOT : 2 * SLOT, :] = up_part.reshape(2, SLOT, PACK)
        grad_down[rows, :] = dot_nn(cotangent_turned[rows, :], hidden_all[...])
        return carry

    lax.fori_loop(0, WIDE // 256, grad_tile, 0)
    for quarter in range(REPS):
        lefts, rights = left_right(
            grad_down[pl.ds(rows_of(quarter, 0), SLOT), :],
            grad_down[pl.ds(rows_of(quarter, 1), SLOT), :],
        )
        down_made[slot, side_here, quarter] = lefts
        down_made[slot, 1 - side_here, quarter] = rights
    for core in range(2):

        @pl.when((step & 1) == core)
        def _():
            for copy in grad_copies(step, slot, core):
                copy.start()

    for copy in grad_down_copies(step, slot):
        copy.start()

    @pl.when(step == REPS - 1)
    def _():
        settle(step - 1, 1 - slot)
        settle(step, slot)


def mlp(here, normed, cotangent, cotangent_turned, pair_parts, down_parts):
    tokens = normed.shape[0]
    pair_grads = jax.ShapeDtypeStruct((2, SLOTS, 2 * SLOT, PACK), bf16)
    down_grads = jax.ShapeDtypeStruct((2, SLOTS, SLOT, PACK), bf16)
    return pl.pallas_call(
        mlp_kernel,
        grid=(REPS,),
        in_specs=[
            pl.BlockSpec(memory_space=pltpu.SMEM),
            whole_block((tokens, WIDE)),
            whole_block((tokens, WIDE)),
            whole_block((WIDE, tokens)),
        ]
        + [anywhere()] * 8,
        out_specs=[whole_block((tokens, WIDE)), whole_block((tokens, WIDE))] + [anywhere()] * 4,
        out_shape=[
            jax.ShapeDtypeStruct((tokens, WIDE), f32),
            jax.ShapeDtypeStruct((tokens, WIDE), f32),
            pair_grads,
            pair_grads,
            down_grads,
            down_grads,
        ],
        scratch_shapes=[
            pltpu.VMEM((2, SLOTS, 2 * SLOT, PACK), bf16),
            pltpu.VMEM((2, 2, REPS, SLOT, PACK), bf16),
            pltpu.VMEM((WIDE, PACK), bf16),
            pltpu.VMEM((WIDE, tokens), bf16),
            pltpu.VMEM((tokens, PACK), bf16),
            pltpu.VMEM((tokens, PACK), bf16),
            pltpu.VMEM((tokens, PACK), bf16),
            pltpu.VMEM((2, SLOTS, 2 * SLOT, PACK), bf16),
            pltpu.VMEM((WIDE, PACK), f32),
            pltpu.VMEM((2, 2, REPS, SLOT, PACK), bf16),
            pltpu.SemaphoreType.DMA((2, 2)),
            pltpu.SemaphoreType.DMA((2, 2, REPS)),
            pltpu.SemaphoreType.DMA((2, 2)),
            pltpu.SemaphoreType.DMA((2, 2, REPS)),
        ],
        compiler_params=pltpu.CompilerParams(vmem_limit_bytes=VMEM_BYTES),
        cost_estimate=pl.CostEstimate(
            flops=44_000_000_000, bytes_accessed=44_000_000, transcendentals=2_000_000
        ),
        name="mlp",
    )(here, normed, cotangent, cotangent_turned, *pair_parts, *down_parts)


def attn_backward_kernel(
    cotangent,
    middle,
    d_normed_two,
    inputs,
    query_rot,
    key_both,
    value_both,
    probs_in,
    cosines,
    sines,
    normed,
    mixed,
    gains,
    spread,
    query_from,
    key_value_from,
    output_from,
    w_query,
    w_key_value,
    w_output,
    token_grad,
    one_zero,
    one_one,
    two_zero,
    two_one,
    d_mixed_heads,
    head_parts,
    key_parts,
    value_parts,
    d_heads,
    wire_in,
    wire_out,
    gain_sums,
):
    step = pl.program_id(0)
    batches = pl.num_programs(0) - 1

    @pl.when(step < batches)
    def _():
        gain_one = gains[0:1, :]
        gain_two = gains[1:2, :]
        mid = middle[...]
        upstream = d_normed_two[...]
        scale_two = lax.rsqrt(jnp.sum(mid * mid, axis=1, keepdims=True) * (1.0 / D) + norm_epsilon)
        weighted = upstream * gain_two
        inner = jnp.sum(weighted * mid, axis=1, keepdims=True) * (1.0 / D)
        term_two = jnp.sum(upstream * mid * scale_two, axis=0, keepdims=True)
        d_middle = (
            cotangent[...].astype(f32)
            + scale_two * weighted
            - mid * scale_two * scale_two * scale_two * inner
        )
        d_branch = d_middle.astype(bf16)
        d_mixed = dot_nt(d_branch, w_output[...]).astype(bf16)
        d_mixed_heads[...] = dot_nt(d_mixed, spread[...]).astype(bf16)
        for j in range(KV_HEADS):
            at = slice(j * 128, j * 128 + 128)
            for part in (2, 1, 0):
                keys = 128 * (part + 1)
                rows = slice(part * 128, part * 128 + 128)

                def three(ref):
                    return jnp.concatenate(
                        [
                            only_half(ref[rows, (h // 2) * 128 : (h // 2) * 128 + 128], h % 2)
                            for h in range(3 * j, 3 * j + 3)
                        ],
                        axis=0,
                    )

                queries = three(query_rot)
                d_mix = three(d_mixed_heads)
                probs = probs_in[0, j, :, probs_at(part) : probs_at(part) + keys]
                probs_f = probs.astype(f32)
                d_probs = dot_nt(d_mix, value_both[0:keys, at])
                product = probs_f * d_probs
                d_scores = product - probs_f * jnp.sum(product, axis=1, keepdims=True)
                d_scores = d_scores.astype(bf16)
                d_query = dot_nn(d_scores, key_both[0:keys, at])
                for g in range(GROUP):
                    head_parts[3 * j + g, rows, :] = d_query[g * 128 : g * 128 + 128]
                d_key = dot_tn(d_scores, queries)
                d_value = dot_tn(probs, d_mix)
                if part == 2:
                    key_parts[j] = d_key
                    value_parts[j] = d_value
                else:
                    key_parts[j, 0:keys, :] += d_key
                    value_parts[j, 0:keys, :] += d_value

        low = lane_index((MB_TOK, 128)) < 64
        cosine, sine = (cosines[...], sines[...])
        empty = jnp.zeros((MB_TOK, 128), f32)
        for c in range(8):
            upper = head_parts[2 * c + 1] if 2 * c + 1 < HEADS else empty
            joined = jnp.where(low, head_parts[2 * c], upper) * HEAD**-0.5
            d_heads[:, c * 128 : c * 128 + 128] = turned(joined, cosine, -sine).astype(bf16)

        def summed(ref, j):
            return ref[j] + pltpu.roll(ref[j], 64, 1)

        for c in range(3):
            for place, ref in ((1024, key_parts), (1408, value_parts)):
                upper = summed(ref, 2 * c + 1) if 2 * c + 1 < KV_HEADS else empty
                joined = jnp.where(low, summed(ref, 2 * c), upper)
                if place == 1024:
                    joined = turned(joined * HEAD**-0.5, cosine, -sine)
                d_heads[:, place + c * 128 : place + c * 128 + 128] = joined.astype(bf16)
        d_query_low = d_heads[:, 0:1024]
        d_key_value_low = d_heads[:, 1024:1792]
        rows = pl.ds(pl.multiple_of(step * MB_TOK, MB_TOK), MB_TOK)
        query_wire = dot_nt(d_query_low, query_from[...])
        key_value_wire = dot_nt(d_key_value_low, key_value_from[...])
        output_wire = dot_nt(d_branch, output_from[...]).astype(bf16)
        for quarter in range(REPS):
            base = quarter * 512
            from_query = query_wire[:, quarter * 256 : quarter * 256 + 256]
            from_key = key_value_wire[:, quarter * 384 : quarter * 384 + 384]
            wire_in[rows, base : base + 128] = from_query[:, 0:128].astype(bf16)
            wire_in[rows, base + 128 : base + 256] = (
                from_query[:, 128:256] + from_key[:, 0:128]
            ).astype(bf16)
            wire_in[rows, base + 256 : base + 512] = from_key[:, 128:384].astype(bf16)
        wire_out[rows, :] = output_wire
        d_normed = dot_nt(d_query_low, w_query[...]) + dot_nt(d_key_value_low, w_key_value[...])
        values = inputs[...].astype(f32)
        scale = lax.rsqrt(
            jnp.sum(values * values, axis=1, keepdims=True) * (1.0 / D) + norm_epsilon
        )
        weighted = d_normed * gain_one
        inner = jnp.sum(weighted * values, axis=1, keepdims=True) * (1.0 / D)
        term_one = jnp.sum(d_normed * values * scale, axis=0, keepdims=True)
        total = d_middle + scale * weighted - values * scale * scale * scale * inner
        token_grad[...] = dot_nt(total.astype(bf16), spread[0:D, :]).astype(bf16)

        @pl.when(step == 0)
        def _():
            gain_sums[...] = jnp.zeros_like(gain_sums)

        gain_sums[0:1, :] += term_one
        gain_sums[1:2, :] += term_two

    @pl.when(step == batches)
    def _():
        normed_turned = normed[...].T
        mixed_turned = mixed[...].T
        row = lax.broadcasted_iota(jnp.int32, (SLOTS, 16, SLOT), 1)
        gain_rows = jnp.zeros((SLOTS, 16, SLOT), f32)
        for which in range(2):
            spots = [
                gain_sums[which : which + 1, s * SLOT : s * SLOT + SLOT].reshape(1, 1, SLOT)
                for s in range(SLOTS)
            ]
            gain_rows = jnp.where(row == 8 + which, jnp.concatenate(spots, axis=0), gain_rows)
        for quarter in range(REPS):
            first = dot_nn(normed_turned, wire_in[:, quarter * 512 : quarter * 512 + 512])
            second = dot_nn(mixed_turned, wire_out[:, quarter * 256 : quarter * 256 + 256])
            block = jnp.concatenate(
                [first[:, 0:384], first[:, 384:512] + second[:, 0:128], second[:, 128:256]], axis=1
            ).reshape(SLOTS, SLOT, PACK)
            y, core = (quarter >> 1, quarter & 1)
            low_rows = block[:, 0:ROWS_A, :].astype(bf16)
            high_rows = block[:, ROWS_A:SLOT, :].astype(bf16)
            (one_zero, one_one)[core][y, :, :, :] = low_rows
            target = (two_zero, two_one)[core]
            tail = (block[:, 112:SLOT, 0:SLOT] + gain_rows).astype(bf16)
            for side in range(2):
                slots = slice(side * 4, side * 4 + 4)
                target[side, y * 4 : y * 4 + 4, :, :] = high_rows[slots]
                target[side, y * 4 : y * 4 + 4, 48:64, 0:SLOT] = tail[slots]


def attn_backward(
    cotangent,
    middle,
    d_normed_two,
    inputs,
    query_rot,
    key_both,
    value_both,
    probs,
    tables,
    normed,
    mixed,
    gains,
    places,
    weights,
):
    tokens = inputs.shape[0]
    count = tokens // MB_TOK

    def per_batch(columns):
        return pl.BlockSpec((MB_TOK, columns), lambda i: (jnp.minimum(i, count - 1), 0))

    half = jax.ShapeDtypeStruct((2, SLOTS, ROWS_A, PACK), bf16)
    return pl.pallas_call(
        attn_backward_kernel,
        grid=(count + 1,),
        in_specs=[
            per_batch(WIDE),
            per_batch(WIDE),
            per_batch(WIDE),
            per_batch(WIDE),
            per_batch(WIDE),
            per_batch(PACK),
            per_batch(PACK),
            pl.BlockSpec(
                (1, KV_HEADS, MB_TOK, 768), lambda i: (jnp.minimum(i, count - 1), 0, 0, 0)
            ),
            per_batch(128),
            per_batch(128),
            whole_block((tokens, WIDE)),
            whole_block((tokens, WIDE)),
            whole_block((8, WIDE)),
        ]
        + [whole_block(place.shape) for place in places]
        + [whole_block(weight.shape) for weight in weights],
        out_specs=[per_batch(D)] + [whole_block(half.shape)] * 4,
        out_shape=[jax.ShapeDtypeStruct((tokens, D), bf16), half, half, half, half],
        scratch_shapes=[
            pltpu.VMEM((MB_TOK, WIDE), bf16),
            pltpu.VMEM((HEADS, MB_TOK, 128), f32),
            pltpu.VMEM((KV_HEADS, MB_TOK, 128), f32),
            pltpu.VMEM((KV_HEADS, MB_TOK, 128), f32),
            pltpu.VMEM((MB_TOK, 1792), bf16),
            pltpu.VMEM((tokens, REPS * 512), bf16),
            pltpu.VMEM((tokens, REPS * 256), bf16),
            pltpu.VMEM((8, WIDE), f32),
        ],
        compiler_params=pltpu.CompilerParams(vmem_limit_bytes=VMEM_BYTES),
        cost_estimate=pl.CostEstimate(
            flops=40_000_000_000, bytes_accessed=50_000_000, transcendentals=0
        ),
        name="attn_backward",
    )(
        cotangent,
        middle,
        d_normed_two,
        inputs,
        query_rot,
        key_both,
        value_both,
        probs,
        *tables,
        normed,
        mixed,
        gains,
        *places,
        *weights,
    )


Z_NEAR = ("fsdp", 1)
Z_FAR = ("fsdp", 2)
X_SIDE = ("fsdp", 0)
Y_SIDE = ("rep", 1)
CORE = ("rep", 0)


def swap_with(values, step):
    axis, bit = step
    count = lax.axis_size(axis)
    return lax.ppermute(values, axis, [(i, i ^ (1 << bit)) for i in range(count)])


def gather_parts(block, side_first):
    two = jnp.stack([block, swap_with(block, Z_NEAR)])
    four = jnp.concatenate([two, swap_with(two, Z_FAR)])
    first, second = (X_SIDE, Y_SIDE) if side_first else (Y_SIDE, X_SIDE)
    eight = jnp.concatenate([four, swap_with(four, first)])
    across = swap_with(eight, second)
    return (eight, swap_with(eight, CORE), across, swap_with(across, CORE))


def added(left, right):
    return (left.astype(f32) + right.astype(f32)).astype(bf16)


def scatter_parts(kept, sent, side_first):
    first, second = (X_SIDE, Y_SIDE) if side_first else (Y_SIDE, X_SIDE)
    came = swap_with(sent, CORE)
    came_next = swap_with(added(kept[1], came[1]), second)
    eight = added(kept[0], came[0])
    came = swap_with(added(eight[4:8], came_next[4:8]), first)
    four = added(eight[0:4], came_next[0:4])
    came_next = swap_with(added(four[2:4], came[2:4]), Z_FAR)
    two = added(four[0:2], came[0:2])
    came = swap_with(added(two[1], came_next[1]), Z_NEAR)
    return two[0].astype(f32) + came_next[0].astype(f32) + came.astype(f32)


def split_parts(blocks, side_first):
    rows, columns = blocks.shape[2:]
    grid = blocks.reshape(4, 2, 2, 2, rows, columns)
    parts = []
    for second in range(2):
        for core in range(2):
            if side_first:
                part = grid[:, :, second, core].transpose(1, 0, 2, 3)
            else:
                part = grid[:, second, :, core].transpose(1, 0, 2, 3)
            parts.append(part.reshape(SLOTS, rows, columns))
    return parts


def join_parts(kept, sent, side_first):
    rows, columns = kept.shape[2:]
    grid = jnp.stack([kept, sent]).reshape(2, 2, 2, 4, rows, columns)
    grid = grid.transpose(3, 2, 1, 0, 4, 5) if side_first else grid.transpose(3, 1, 2, 0, 4, 5)
    return grid.reshape(SLOTS, REPS, rows, columns)


def attn_block(w_query, w_key, w_value, w_output, attn_gain, mlp_gain):
    matrices = jnp.concatenate([w_query, w_key, w_value, w_output], axis=1)
    gains = jnp.stack([attn_gain, mlp_gain])
    gains = jnp.pad(gains, ((0, SLOT - USED - 2), (0, PACK - USED)))
    return jnp.concatenate([matrices, gains], axis=0)


def pair_block(w_gate, w_up):
    taller = ((0, SLOT - USED), (0, 0))
    return jnp.concatenate([jnp.pad(w_gate, taller), jnp.pad(w_up, taller)], axis=0)


def down_block(w_down):
    halves = w_down.T.reshape(2, USED, HALF_PACK)
    halves = jnp.concatenate([halves[0], halves[1]], axis=1)
    return jnp.pad(halves, ((0, SLOT - USED), (0, 0)))


def down_of(block):
    halves = jnp.stack([block[:USED, :HALF_PACK], block[:USED, HALF_PACK:]])
    return halves.reshape(2 * USED, HALF_PACK).T


def whole(shard):
    return lax.all_gather(lax.all_gather(shard, "rep", axis=1, tiled=True), "fsdp", axis=0, tiled=True)


def cut(matrix, eighth, quarter):
    rows, columns = (matrix.shape[0] // SLOTS, matrix.shape[1] // REPS)
    return matrix[
        eighth * rows : eighth * rows + rows, quarter * columns : quarter * columns + columns
    ]


def every_block(make):
    return jnp.stack(
        [jnp.stack([make(e, q) for q in range(REPS)]) for e in range(SLOTS)]
    )


def owned(blocks):
    eighths, quarters, rows, columns = blocks.shape
    matrix = blocks.transpose(0, 2, 1, 3).reshape(eighths * rows, quarters * columns)
    part = lax.psum_scatter(matrix, "fsdp", scatter_dimension=0, tiled=True)
    return lax.psum_scatter(part, "rep", scatter_dimension=1, tiled=True).astype(f32)


def per_device(
    tokens,
    lengths,
    attn_gain,
    w_query,
    w_key,
    w_value,
    w_output,
    mlp_gain,
    w_gate,
    w_up,
    w_down,
    cotangent,
):
    paired = lax.axis_size("fsdp") == SLOTS and lax.axis_size("rep") == REPS
    if paired:
        eighth_here = lax.axis_index("fsdp").astype(jnp.int32)
        quarter_here = lax.axis_index("rep").astype(jnp.int32)
        attn_pack = attn_block(w_query, w_key, w_value, w_output, attn_gain, mlp_gain)
        first_parts = gather_parts(attn_pack[:ROWS_A], True)
        second_parts = gather_parts(attn_pack[ROWS_A:], False)
        pair_parts = gather_parts(pair_block(w_gate, w_up), False)
        down_parts = gather_parts(down_block(w_down), True)
    else:
        eighth_here = jnp.int32(0)
        quarter_here = jnp.int32(0)
        gain_one, gain_two = (
            lax.all_gather(attn_gain, "fsdp", axis=0, tiled=True).reshape(SLOTS, USED),
            lax.all_gather(mlp_gain, "fsdp", axis=0, tiled=True).reshape(SLOTS, USED),
        )
        mats = [whole(w) for w in (w_query, w_key, w_value, w_output, w_gate, w_up, w_down)]
        attn_blocks = every_block(
            lambda e, q: attn_block(*[cut(m, e, q) for m in mats[:4]], gain_one[e], gain_two[e])
        )
        first_parts = split_parts(attn_blocks[:, :, :ROWS_A], True)
        second_parts = split_parts(attn_blocks[:, :, ROWS_A:], False)
        pair_parts = split_parts(
            every_block(lambda e, q: pair_block(cut(mats[4], e, q), cut(mats[5], e, q))), False
        )
        down_parts = split_parts(every_block(lambda e, q: down_block(cut(mats[6], e, q))), True)
    here = jnp.stack([eighth_here, quarter_here])
    places = placing(eighth_here, quarter_here)
    spread = places[0]
    segments, positions = jax.vmap(layout)(lengths)
    tables = rope_tables(positions.reshape(-1))
    inputs = jnp.dot(tokens, spread[:D], preferred_element_type=f32).astype(bf16)
    upstream = jnp.dot(cotangent, spread[:D], preferred_element_type=f32).astype(bf16)
    (
        normed,
        query_rot,
        key_both,
        value_both,
        probs,
        mixed,
        middle,
        normed_two,
        *weights,
        gains,
    ) = attn_forward(inputs, places, tables, segments, first_parts, second_parts)
    mlp_out, d_normed_two, pair_kept, pair_sent, down_kept, down_sent = mlp(
        here, normed_two, upstream, upstream.T, pair_parts, down_parts
    )
    output = jnp.dot(
        (middle + mlp_out).astype(bf16), spread[:D].T, preferred_element_type=f32
    ).astype(bf16)
    token_grad, one_kept, one_sent, two_kept, two_sent = attn_backward(
        upstream,
        middle,
        d_normed_two,
        inputs,
        query_rot,
        key_both,
        value_both,
        probs,
        tables,
        normed,
        mixed,
        gains,
        places,
        weights,
    )
    if paired:
        down_sum = scatter_parts(down_kept, down_sent, True)
        pair_sum = scatter_parts(pair_kept, pair_sent, False)
        first_sum = scatter_parts(one_kept, one_sent, True)
        second_sum = scatter_parts(two_kept, two_sent, False)
        attn_sum = jnp.concatenate([first_sum, second_sum], axis=0)
        gain_sums = (attn_sum[USED, :USED], attn_sum[USED + 1, :USED])
        attn_sum = attn_sum[:USED]
        grads = [
            attn_sum[:, 0:240],
            attn_sum[:, 240:320],
            attn_sum[:, 320:400],
            attn_sum[:, 400:640],
            pair_sum[:USED],
            pair_sum[SLOT : SLOT + USED],
            down_of(down_sum),
        ]
    else:
        attn_blocks = jnp.concatenate(
            [join_parts(one_kept, one_sent, True), join_parts(two_kept, two_sent, False)], axis=2
        )
        gain_sums = tuple(
            lax.psum(
                lax.psum_scatter(
                    attn_blocks[:, 0, USED + which, :USED].astype(f32).reshape(D),
                    "fsdp",
                    scatter_dimension=0,
                    tiled=True,
                ),
                "rep",
            )
            for which in range(2)
        )
        attn_blocks = attn_blocks[:, :, :USED]
        pair_blocks = join_parts(pair_kept, pair_sent, False)
        down_blocks = join_parts(down_kept, down_sent, True)
        grads = [
            owned(attn_blocks[..., 0:240]),
            owned(attn_blocks[..., 240:320]),
            owned(attn_blocks[..., 320:400]),
            owned(attn_blocks[..., 400:640]),
            owned(pair_blocks[:, :, :USED]),
            owned(pair_blocks[:, :, SLOT : SLOT + USED]),
            owned(jax.vmap(jax.vmap(down_of))(down_blocks)),
        ]
    return (
        output,
        token_grad,
        gain_sums[0],
        grads[0],
        grads[1],
        grads[2],
        grads[3],
        gain_sums[1],
        grads[4],
        grads[5],
        grads[6],
    )


def solution(mesh):
    placed = (
        P(("fsdp", "rep"), None),
        P(("fsdp", "rep"), None),
        P("fsdp"),
        P("fsdp", "rep"),
        P("fsdp", "rep"),
        P("fsdp", "rep"),
        P("fsdp", "rep"),
        P("fsdp"),
        P("fsdp", "rep"),
        P("fsdp", "rep"),
        P("fsdp", "rep"),
        P(("fsdp", "rep"), None),
    )
    return jax.shard_map(
        per_device,
        mesh=mesh,
        in_specs=placed,
        out_specs=(
            P(("fsdp", "rep"), None),
            P(("fsdp", "rep"), None),
            P("fsdp"),
            P("fsdp", "rep"),
            P("fsdp", "rep"),
            P("fsdp", "rep"),
            P("fsdp", "rep"),
            P("fsdp"),
            P("fsdp", "rep"),
            P("fsdp", "rep"),
            P("fsdp", "rep"),
        ),
        check_vma=False,
    )
```

```python
import jax
import jax.numpy as jnp
from jax import lax
from jax.experimental import pallas as pl
from jax.experimental.pallas import tpu as pltpu
from jax.sharding import PartitionSpec as P

D = 960
FF = 2560
HEADS = 15
KV_HEADS = 5
HEAD = 64
MB_TOK = 384
SEGS = 3
GROUP = 3
QW = 960
KVW = 320

SLOTS = 8
REPS = 4
USED = 120
SLOT = 128
WIDE = SLOTS * SLOT
PACK = 640
HALF_PACK = 320
ROWS_A = 64
VMEM_BYTES = 60 * 1024 * 1024

norm_epsilon = 1e-05
rope_base = 100000.0
masked_value = -1e30

f32 = jnp.float32
bf16 = jnp.bfloat16


def layout(length_row):
    starts = jnp.cumsum(length_row) - length_row
    places = jnp.arange(MB_TOK, dtype=jnp.int32)
    inside = (
        (places[:, None] >= starts[None, :]) & (places[:, None] < (starts + length_row)[None, :])
    ).astype(jnp.int32)
    segment = jnp.sum(inside * jnp.arange(SEGS, dtype=jnp.int32)[None, :], axis=1)
    position = places - jnp.sum(inside * starts[None, :], axis=1)
    return (segment, position)


def rope_tables(position):
    half_width = HEAD // 2
    exponent = jnp.arange(half_width, dtype=f32) * (2.0 / HEAD)
    inverse = jnp.power(rope_base, -exponent)
    angles = position.astype(f32)[:, None] * inverse
    cosines, sines = (jnp.cos(angles), jnp.sin(angles))
    return (
        jnp.concatenate([cosines] * 4, axis=1),
        jnp.concatenate([-sines, sines, -sines, sines], axis=1),
    )


def slot_of(eighth):
    return (eighth & 1) * 4 + (eighth >> 1)


def eighth_of(slot):
    return (slot & 3) * 2 + (slot >> 2)


def feature_lanes(eighth_here):
    lanes = jnp.arange(WIDE, dtype=jnp.int32)
    eighth = eighth_of(lanes // SLOT) ^ eighth_here
    return jnp.where(lanes % SLOT < USED, eighth * USED + lanes % SLOT, -1)


def one_hot(rows, wanted):
    return (jnp.arange(rows, dtype=jnp.int32)[:, None] == wanted[None, :]).astype(bf16)


def placing(eighth_here, quarter_here):
    features = feature_lanes(eighth_here)
    spread = one_hot(WIDE, features)
    columns = jnp.arange(WIDE, dtype=jnp.int32)
    query_from = jnp.where(
        columns < QW, ((columns // 240) ^ quarter_here) * 256 + columns % 240, -1
    )
    key_columns = jnp.arange(384, dtype=jnp.int32)
    key_from = ((key_columns // 80) ^ quarter_here) * 384 + key_columns % 80
    key_value_from = jnp.concatenate(
        [
            jnp.where(key_columns < KVW, key_from + 112, -1),
            jnp.where(key_columns < KVW, key_from + 192, -1),
        ]
    )
    output_from = jnp.where(
        features >= 0, ((features // 240) ^ quarter_here) * 256 + 16 + features % 240, -1
    )
    return (
        spread,
        one_hot(1024, query_from),
        one_hot(1536, key_value_from),
        one_hot(1024, output_from),
    )


def dot_nn(left, right):
    return lax.dot_general(left, right, (((1,), (0,)), ((), ())), preferred_element_type=f32)


def dot_nt(left, right):
    return lax.dot_general(left, right, (((1,), (1,)), ((), ())), preferred_element_type=f32)


def dot_tn(left, right):
    return lax.dot_general(left, right, (((0,), (0,)), ((), ())), preferred_element_type=f32)


def lane_index(shape):
    return lax.broadcasted_iota(jnp.int32, shape, len(shape) - 1)


def swapped(values):
    first = (lane_index(values.shape) & 63) < 32
    return jnp.where(first, pltpu.roll(values, 96, 1), pltpu.roll(values, 32, 1))


def turned(values, cosines, sines):
    return values * cosines + swapped(values) * sines


def both_halves(values, odd):
    low = lane_index(values.shape) < 64
    moved = pltpu.roll(values, 64, 1)
    return jnp.where(low, moved, values) if odd else jnp.where(low, values, moved)


def only_half(values, odd):
    low = lane_index(values.shape) < 64
    return jnp.where(low != bool(odd), values, jnp.zeros_like(values))


def gain_row(attn_ref, which):
    rows = [attn_ref[0, s, 112:128, 0:SLOT].astype(f32)[8 + which : 9 + which] for s in range(SLOTS)]
    return jnp.concatenate(rows, axis=1)


def probs_at(part):
    return (0, 128, 384)[part]


def attn_forward_kernel(
    inputs,
    spread,
    query_from,
    key_value_from,
    output_from,
    cosines,
    sines,
    segment_rows,
    segment_columns,
    a0,
    a1,
    a2,
    a3,
    b0,
    b1,
    b2,
    b3,
    normed_out,
    query_out,
    key_out,
    value_out,
    probs_out,
    mixed_out,
    middle_out,
    normed_two_out,
    w_query,
    w_key_value,
    w_output,
    gains_out,
    attn_all,
    heads_out,
    mixed_heads,
    bias,
    sems,
):
    @pl.when(pl.program_id(0) == 0)
    def _():
        copies = []
        for quarter, source in enumerate((a0, a1, a2, a3)):
            copies.append((source, attn_all.at[quarter, :, 0:ROWS_A, :]))
        for place, source in enumerate((b0, b1, b2, b3)):
            side, core = (place >> 1, place & 1)
            for y in range(2):
                copies.append(
                    (
                        source.at[y * 4 : y * 4 + 4],
                        attn_all.at[y * 2 + core, side * 4 : side * 4 + 4, ROWS_A : 2 * ROWS_A, :],
                    )
                )
        started = [
            pltpu.make_async_copy(source, target, sems.at[n])
            for n, (source, target) in enumerate(copies)
        ]
        for copy in started:
            copy.start()
        for copy in started:
            copy.wait()

        def columns(low, high):
            return jnp.concatenate(
                [
                    attn_all[quarter, :, :, low:high].reshape(WIDE, high - low)
                    for quarter in range(REPS)
                ],
                axis=1,
            )

        w_query[...] = dot_nn(columns(0, 256), query_from[...]).astype(bf16)
        w_key_value[...] = dot_nn(columns(128, 512), key_value_from[...]).astype(bf16)
        w_output[...] = dot_nn(columns(384, 640), output_from[...]).astype(bf16)
        gains_out[0:1, :] = gain_row(attn_all, 0)
        gains_out[1:2, :] = gain_row(attn_all, 1)

    values = inputs[...].astype(f32)
    gain_one = gains_out[0:1, :]
    gain_two = gains_out[1:2, :]
    scale = lax.rsqrt(jnp.sum(values * values, axis=1, keepdims=True) * (1.0 / D) + norm_epsilon)
    normed = (values * scale * gain_one).astype(bf16)
    normed_out[...] = normed
    cosine, sine = (cosines[...], sines[...])
    query_lin = dot_nn(normed, w_query[...])
    for c in range(8):
        at = slice(c * 128, c * 128 + 128)
        query_out[:, at] = turned(query_lin[:, at], cosine, sine).astype(bf16)
    key_value = dot_nn(normed, w_key_value[...])
    for c in range(3):
        key_part = turned(key_value[:, c * 128 : c * 128 + 128], cosine, sine)
        value_part = key_value[:, 384 + c * 128 : 384 + c * 128 + 128]
        for odd in range(2 if c < 2 else 1):
            at = slice((2 * c + odd) * 128, (2 * c + odd) * 128 + 128)
            key_out[:, at] = both_halves(key_part, odd).astype(bf16)
            value_out[:, at] = both_halves(value_part, odd).astype(bf16)

    query_place = lax.broadcasted_iota(jnp.int32, (MB_TOK, MB_TOK), 0)
    key_place = lax.broadcasted_iota(jnp.int32, (MB_TOK, MB_TOK), 1)
    seen = (segment_rows[...] == segment_columns[0]) & (key_place <= query_place)
    bias[...] = jnp.where(seen, 0.0, masked_value)
    for j in range(KV_HEADS):
        at = slice(j * 128, j * 128 + 128)
        for part in range(3):
            keys = 128 * (part + 1)
            rows = slice(part * 128, part * 128 + 128)
            queries = jnp.concatenate(
                [
                    only_half(query_out[rows, (h // 2) * 128 : (h // 2) * 128 + 128], h % 2)
                    for h in range(3 * j, 3 * j + 3)
                ],
                axis=0,
            )
            scores = dot_nt(queries, key_out[0:keys, at]) * HEAD**-0.5
            hidden_part = bias[rows, 0:keys]
            scores = scores + jnp.concatenate([hidden_part] * GROUP, axis=0)
            peak = jnp.max(scores, axis=1, keepdims=True)
            weights = jnp.exp(scores - peak)
            total = jnp.sum(weights, axis=1, keepdims=True)
            probs = (weights * (1.0 / total)).astype(bf16)
            probs_out[0, j, :, probs_at(part) : probs_at(part) + keys] = probs
            gathered = dot_nn(probs, value_out[0:keys, at])
            for g in range(GROUP):
                heads_out[3 * j + g, rows, :] = gathered[g * 128 : g * 128 + 128]
    low = lane_index((MB_TOK, 128)) < 64
    for c in range(8):
        upper = heads_out[2 * c + 1] if 2 * c + 1 < HEADS else jnp.zeros((MB_TOK, 128), f32)
        mixed_heads[:, c * 128 : c * 128 + 128] = jnp.where(low, heads_out[2 * c], upper).astype(bf16)
    mixed = dot_nn(mixed_heads[...], spread[...]).astype(bf16)
    mixed_out[...] = mixed
    middle = values + dot_nn(mixed, w_output[...])
    middle_out[...] = middle
    scale_two = lax.rsqrt(
        jnp.sum(middle * middle, axis=1, keepdims=True) * (1.0 / D) + norm_epsilon
    )
    normed_two_out[...] = (middle * scale_two * gain_two).astype(bf16)


def whole_block(shape):
    return pl.BlockSpec(
        shape, lambda *ids: (0,) * len(shape), pipeline_mode=pl.Buffered(buffer_count=1)
    )


def anywhere():
    return pl.BlockSpec(memory_space=pl.ANY)


def attn_forward(inputs, places, tables, segments, first_parts, second_parts):
    tokens = inputs.shape[0]
    count = tokens // MB_TOK

    def per_batch(columns):
        return pl.BlockSpec((MB_TOK, columns), lambda i: (i, 0))

    outs = [
        jax.ShapeDtypeStruct((tokens, WIDE), bf16),
        jax.ShapeDtypeStruct((tokens, WIDE), bf16),
        jax.ShapeDtypeStruct((tokens, PACK), bf16),
        jax.ShapeDtypeStruct((tokens, PACK), bf16),
        jax.ShapeDtypeStruct((count, KV_HEADS, MB_TOK, 768), bf16),
        jax.ShapeDtypeStruct((tokens, WIDE), bf16),
        jax.ShapeDtypeStruct((tokens, WIDE), f32),
        jax.ShapeDtypeStruct((tokens, WIDE), bf16),
        jax.ShapeDtypeStruct((WIDE, 1024), bf16),
        jax.ShapeDtypeStruct((WIDE, 768), bf16),
        jax.ShapeDtypeStruct((WIDE, WIDE), bf16),
        jax.ShapeDtypeStruct((8, WIDE), f32),
    ]
    return pl.pallas_call(
        attn_forward_kernel,
        grid=(count,),
        in_specs=[per_batch(WIDE)]
        + [whole_block(place.shape) for place in places]
        + [
            per_batch(128),
            per_batch(128),
            per_batch(1),
            pl.BlockSpec((1, 1, MB_TOK), lambda i: (i, 0, 0)),
        ]
        + [anywhere()] * 8,
        out_specs=[
            per_batch(WIDE),
            per_batch(WIDE),
            per_batch(PACK),
            per_batch(PACK),
            pl.BlockSpec((1, KV_HEADS, MB_TOK, 768), lambda i: (i, 0, 0, 0)),
            per_batch(WIDE),
            per_batch(WIDE),
            per_batch(WIDE),
            whole_block((WIDE, 1024)),
            whole_block((WIDE, 768)),
            whole_block((WIDE, WIDE)),
            whole_block((8, WIDE)),
        ],
        out_shape=outs,
        scratch_shapes=[
            pltpu.VMEM((REPS, SLOTS, SLOT, PACK), bf16),
            pltpu.VMEM((HEADS, MB_TOK, 128), f32),
            pltpu.VMEM((MB_TOK, WIDE), bf16),
            pltpu.VMEM((MB_TOK, MB_TOK), f32),
            pltpu.SemaphoreType.DMA((12,)),
        ],
        compiler_params=pltpu.CompilerParams(vmem_limit_bytes=VMEM_BYTES),
        cost_estimate=pl.CostEstimate(
            flops=24_000_000_000, bytes_accessed=40_000_000, transcendentals=4_000_000
        ),
        name="attn_forward",
    )(
        inputs,
        *places,
        *tables,
        segments.reshape(tokens, 1),
        segments.reshape(count, 1, MB_TOK),
        *first_parts,
        *second_parts,
    )


def left_right(left, right):
    first = lane_index(left.shape) < HALF_PACK
    left, right = (left.astype(f32), right.astype(f32))
    return (
        jnp.where(first, left, pltpu.roll(right, HALF_PACK, 1)).astype(bf16),
        jnp.where(first, pltpu.roll(left, HALF_PACK, 1), right).astype(bf16),
    )


def pair_fetches(first_parts, second_parts, at, w_gate, w_up, sems):
    found = []
    for core in range(2):
        lanes = slice(core * PACK, core * PACK + PACK)
        found.append((first_parts[at * 2 + core].at[:, 0:SLOT, :], w_gate.at[:, :, lanes]))
        for side in range(2):
            found.append(
                (
                    second_parts[side * 2 + core].at[at * 4 : at * 4 + 4, 0:SLOT, :],
                    w_up.at[side * 4 : side * 4 + 4, :, lanes],
                )
            )
    return [
        pltpu.make_async_copy(source, target, sems.at[n])
        for n, (source, target) in enumerate(found)
    ]


def mlp_activations_kernel(
    here,
    normed,
    cotangent,
    g0,
    g1,
    g2,
    g3,
    u0,
    u1,
    u2,
    u3,
    hidden_out,
    d_gate_out,
    d_up_out,
    down_out,
    w_gate,
    w_up,
    down_raw,
    sem_pair,
    sem_down,
):
    step = pl.program_id(0)
    eighth_here, quarter_here = (here[0], here[1])
    side_here = eighth_here & 1
    slot = step & 1
    first_parts, second_parts = ((g0, g1, g2, g3), (u0, u1, u2, u3))

    def down_copies(at, to):
        found = []
        for core in range(2):
            plane = ((2 * at + core) ^ quarter_here) ^ (eighth_here >> 1)
            for side in range(2):
                for quarter in range(REPS):
                    target = down_raw.at[to, core, side, quarter]
                    y, inner = (quarter >> 1, quarter & 1)
                    found.append(
                        (
                            first_parts[quarter].at[side * 4 + plane, SLOT : SLOT + ROWS_A],
                            target.at[0:ROWS_A],
                        )
                    )
                    found.append(
                        (
                            second_parts[side * 2 + inner].at[y * 4 + plane, SLOT : SLOT + ROWS_A],
                            target.at[ROWS_A : 2 * ROWS_A],
                        )
                    )
        return [
            pltpu.make_async_copy(source, target, sem_down.at[to, n])
            for n, (source, target) in enumerate(found)
        ]

    def pair_copies(at, to):
        return pair_fetches(
            first_parts, second_parts, at, w_gate.at[to], w_up.at[to], sem_pair.at[to]
        )

    @pl.when(step == 0)
    def _():
        for at in range(2):
            for copy in pair_copies(at, at) + down_copies(at, at):
                copy.start()

    for at in range(2):

        @pl.when(step == at)
        def _():
            for copy in pair_copies(at, at) + down_copies(at, at):
                copy.wait()

    def rows_of(quarter, which):
        eighth = (quarter ^ quarter_here) * 2 + which
        return pl.multiple_of(slot_of(eighth ^ eighth_here) * SLOT, SLOT)

    for core in range(2):
        lanes = slice(core * PACK, core * PACK + PACK)
        for quarter in range(REPS):
            lefts, rights = left_right(
                down_raw[slot, core, side_here, quarter],
                down_raw[slot, core, 1 - side_here, quarter],
            )
            down_out[0, pl.ds(rows_of(quarter, 0), SLOT), lanes] = lefts
            down_out[0, pl.ds(rows_of(quarter, 1), SLOT), lanes] = rights

    gate_weights = w_gate[slot].reshape(WIDE, 2 * PACK)
    up_weights = w_up[slot].reshape(WIDE, 2 * PACK)

    def one_tile(t, carry):
        rows = pl.ds(pl.multiple_of(t * 256, 256), 256)
        gate = dot_nn(normed[rows, :], gate_weights)
        up = dot_nn(normed[rows, :], up_weights)
        d_hidden = dot_nn(cotangent[rows, :], down_out[0])
        sigmoid = 1.0 / (1.0 + jnp.exp(-gate))
        silu = gate * sigmoid
        hidden_out[0, rows, :] = (silu * up).astype(bf16)
        d_gate_out[0, rows, :] = (
            d_hidden * up * sigmoid * (1.0 + gate * (1.0 - sigmoid))
        ).astype(bf16)
        d_up_out[0, rows, :] = (d_hidden * silu).astype(bf16)
        return carry

    lax.fori_loop(0, normed.shape[0] // 256, one_tile, 0)


def chunk_block(rows, columns):
    return pl.BlockSpec((1, rows, columns), lambda i: (i, 0, 0))


def mlp_activations(here, normed, cotangent, first_parts, second_parts):
    tokens = normed.shape[0]
    rows = jax.ShapeDtypeStruct((2, tokens, 2 * PACK), bf16)
    return pl.pallas_call(
        mlp_activations_kernel,
        grid=(2,),
        in_specs=[
            pl.BlockSpec(memory_space=pltpu.SMEM),
            whole_block((tokens, WIDE)),
            whole_block((tokens, WIDE)),
        ]
        + [anywhere()] * 8,
        out_specs=[chunk_block(tokens, 2 * PACK)] * 3 + [chunk_block(WIDE, 2 * PACK)],
        out_shape=[rows, rows, rows, jax.ShapeDtypeStruct((2, WIDE, 2 * PACK), bf16)],
        scratch_shapes=[
            pltpu.VMEM((2, SLOTS, SLOT, 2 * PACK), bf16),
            pltpu.VMEM((2, SLOTS, SLOT, 2 * PACK), bf16),
            pltpu.VMEM((2, 2, 2, REPS, SLOT, PACK), bf16),
            pltpu.SemaphoreType.DMA((2, 6)),
            pltpu.SemaphoreType.DMA((2, 32)),
        ],
        compiler_params=pltpu.CompilerParams(vmem_limit_bytes=VMEM_BYTES),
        cost_estimate=pl.CostEstimate(
            flops=15_000_000_000, bytes_accessed=35_000_000, transcendentals=2_000_000
        ),
        name="mlp_activations",
    )(here, normed, cotangent, *first_parts, *second_parts)


def mlp_grads_kernel(
    here,
    normed,
    cotangent_turned,
    hidden,
    d_gate,
    d_up,
    first_zero,
    first_one,
    second_zero,
    second_one,
    normed_turned,
    grad_gate,
    grad_up,
    grad_down,
    down_made,
    sem_pair,
    sem_down,
):
    step = pl.program_id(0)
    eighth_here, quarter_here = (here[0], here[1])
    side_here = eighth_here & 1
    slot = step & 1
    firsts, seconds = ((first_zero, first_one), (second_zero, second_one))

    def copies(at, to):
        found = []
        for core in range(2):
            found.append((grad_gate.at[to, core], firsts[core].at[at, :, 0:SLOT, :], sem_pair))
            for side in range(2):
                found.append(
                    (
                        grad_up.at[to, core, side * 4 : side * 4 + 4],
                        seconds[core].at[side, at * 4 : at * 4 + 4, 0:SLOT, :],
                        sem_pair,
                    )
                )
        for core in range(2):
            plane = ((2 * at + core) ^ quarter_here) ^ (eighth_here >> 1)
            for side in range(2):
                for quarter in range(REPS):
                    source = down_made.at[to, core, side, quarter]
                    y, inner = (quarter >> 1, quarter & 1)
                    found.append(
                        (
                            source.at[0:ROWS_A],
                            firsts[inner].at[y, side * 4 + plane, SLOT : SLOT + ROWS_A],
                            sem_down,
                        )
                    )
                    found.append(
                        (
                            source.at[ROWS_A : 2 * ROWS_A],
                            seconds[inner].at[side, y * 4 + plane, SLOT : SLOT + ROWS_A],
                            sem_down,
                        )
                    )
        return [
            pltpu.make_async_copy(source, target, sems.at[to, n])
            for n, (source, target, sems) in enumerate(found)
        ]

    @pl.when(step == 0)
    def _():
        normed_turned[...] = normed[...].T

    def grad_tile(t, carry):
        rows = pl.ds(pl.multiple_of(t * 256, 256), 256)
        two = pl.ds(t * 2, 2)
        gate_part = dot_nn(normed_turned[rows, :], d_gate[0]).astype(bf16)
        up_part = dot_nn(normed_turned[rows, :], d_up[0]).astype(bf16)
        for core in range(2):
            lanes = slice(core * PACK, core * PACK + PACK)
            grad_gate[slot, core, two] = gate_part[:, lanes].reshape(2, SLOT, PACK)
            grad_up[slot, core, two] = up_part[:, lanes].reshape(2, SLOT, PACK)
        grad_down[rows, :] = dot_nn(cotangent_turned[rows, :], hidden[0])
        return carry

    lax.fori_loop(0, WIDE // 256, grad_tile, 0)

    def rows_of(quarter, which):
        eighth = (quarter ^ quarter_here) * 2 + which
        return pl.multiple_of(slot_of(eighth ^ eighth_here) * SLOT, SLOT)

    for core in range(2):
        lanes = slice(core * PACK, core * PACK + PACK)
        for quarter in range(REPS):
            lefts, rights = left_right(
                grad_down[pl.ds(rows_of(quarter, 0), SLOT), lanes],
                grad_down[pl.ds(rows_of(quarter, 1), SLOT), lanes],
            )
            down_made[slot, core, side_here, quarter] = lefts
            down_made[slot, core, 1 - side_here, quarter] = rights
    for at in range(2):

        @pl.when(step == at)
        def _():
            for copy in copies(at, at):
                copy.start()

    @pl.when(step == 1)
    def _():
        for at in range(2):
            for copy in copies(at, at):
                copy.wait()


def mlp_grads(here, normed, cotangent_turned, hidden, d_gate, d_up):
    tokens = normed.shape[0]
    part = jax.ShapeDtypeStruct((2, SLOTS, SLOT + ROWS_A, PACK), bf16)
    return pl.pallas_call(
        mlp_grads_kernel,
        grid=(2,),
        in_specs=[
            pl.BlockSpec(memory_space=pltpu.SMEM),
            whole_block((tokens, WIDE)),
            whole_block((WIDE, tokens)),
        ]
        + [chunk_block(tokens, 2 * PACK)] * 3,
        out_specs=[anywhere()] * 4,
        out_shape=[part] * 4,
        scratch_shapes=[
            pltpu.VMEM((WIDE, tokens), bf16),
            pltpu.VMEM((2, 2, SLOTS, SLOT, PACK), bf16),
            pltpu.VMEM((2, 2, SLOTS, SLOT, PACK), bf16),
            pltpu.VMEM((WIDE, 2 * PACK), f32),
            pltpu.VMEM((2, 2, 2, REPS, SLOT, PACK), bf16),
            pltpu.SemaphoreType.DMA((2, 38)),
            pltpu.SemaphoreType.DMA((2, 38)),
        ],
        compiler_params=pltpu.CompilerParams(vmem_limit_bytes=VMEM_BYTES),
        cost_estimate=pl.CostEstimate(
            flops=15_000_000_000, bytes_accessed=35_000_000, transcendentals=0
        ),
        name="mlp_grads",
    )(here, normed, cotangent_turned, hidden, d_gate, d_up)


def mlp_outputs_kernel(
    hidden,
    d_gate,
    d_up,
    w_down,
    g0,
    g1,
    g2,
    g3,
    u0,
    u1,
    u2,
    u3,
    out,
    d_normed,
    w_gate,
    w_up,
    sem_pair,
):
    step = pl.program_id(0)
    slot = step & 1

    def pair_copies(at):
        return pair_fetches(
            (g0, g1, g2, g3), (u0, u1, u2, u3), at, w_gate.at[at], w_up.at[at], sem_pair.at[at]
        )

    @pl.when(step == 0)
    def _():
        for at in range(2):
            for copy in pair_copies(at):
                copy.start()

    for at in range(2):

        @pl.when(step == at)
        def _():
            for copy in pair_copies(at):
                copy.wait()

    gate_weights = w_gate[slot].reshape(WIDE, 2 * PACK)
    up_weights = w_up[slot].reshape(WIDE, 2 * PACK)

    def products(rows):
        return (
            dot_nt(hidden[0, rows, :], w_down[0]),
            dot_nt(d_gate[0, rows, :], gate_weights) + dot_nt(d_up[0, rows, :], up_weights),
        )

    def tile_rows(t):
        return pl.ds(pl.multiple_of(t * 256, 256), 256)

    def first_tile(t, carry):
        rows = tile_rows(t)
        out[rows, :], d_normed[rows, :] = products(rows)
        return carry

    def second_tile(t, carry):
        rows = tile_rows(t)
        more_out, more_normed = products(rows)
        out[rows, :] += more_out
        d_normed[rows, :] += more_normed
        return carry

    tiles = out.shape[0] // 256

    @pl.when(step == 0)
    def _():
        lax.fori_loop(0, tiles, first_tile, 0)

    @pl.when(step == 1)
    def _():
        lax.fori_loop(0, tiles, second_tile, 0)


def mlp_outputs(hidden, d_gate, d_up, w_down, first_parts, second_parts):
    tokens = hidden.shape[1]
    return pl.pallas_call(
        mlp_outputs_kernel,
        grid=(2,),
        in_specs=[chunk_block(tokens, 2 * PACK)] * 3
        + [chunk_block(WIDE, 2 * PACK)]
        + [anywhere()] * 8,
        out_specs=[whole_block((tokens, WIDE)), whole_block((tokens, WIDE))],
        out_shape=[jax.ShapeDtypeStruct((tokens, WIDE), f32)] * 2,
        scratch_shapes=[
            pltpu.VMEM((2, SLOTS, SLOT, 2 * PACK), bf16),
            pltpu.VMEM((2, SLOTS, SLOT, 2 * PACK), bf16),
            pltpu.SemaphoreType.DMA((2, 6)),
        ],
        compiler_params=pltpu.CompilerParams(vmem_limit_bytes=VMEM_BYTES),
        cost_estimate=pl.CostEstimate(
            flops=15_000_000_000, bytes_accessed=35_000_000, transcendentals=0
        ),
        name="mlp_outputs",
    )(hidden, d_gate, d_up, w_down, *first_parts, *second_parts)


def attn_backward_kernel(
    cotangent,
    middle,
    d_normed_two,
    inputs,
    query_rot,
    key_both,
    value_both,
    probs_in,
    cosines,
    sines,
    gains,
    spread,
    query_from,
    key_value_from,
    output_from,
    w_query,
    w_key_value,
    w_output,
    token_grad,
    wire_in,
    wire_out,
    gain_sums,
    d_mixed_heads,
    head_parts,
    key_parts,
    value_parts,
    d_heads,
):
    step = pl.program_id(0)

    def one_batch():
        gain_one = gains[0:1, :]
        gain_two = gains[1:2, :]
        mid = middle[...]
        upstream = d_normed_two[...]
        scale_two = lax.rsqrt(jnp.sum(mid * mid, axis=1, keepdims=True) * (1.0 / D) + norm_epsilon)
        weighted = upstream * gain_two
        inner = jnp.sum(weighted * mid, axis=1, keepdims=True) * (1.0 / D)
        term_two = jnp.sum(upstream * mid * scale_two, axis=0, keepdims=True)
        d_middle = (
            cotangent[...].astype(f32)
            + scale_two * weighted
            - mid * scale_two * scale_two * scale_two * inner
        )
        d_branch = d_middle.astype(bf16)
        d_mixed = dot_nt(d_branch, w_output[...]).astype(bf16)
        d_mixed_heads[...] = dot_nt(d_mixed, spread[...]).astype(bf16)
        for j in range(KV_HEADS):
            at = slice(j * 128, j * 128 + 128)
            for part in (2, 1, 0):
                keys = 128 * (part + 1)
                rows = slice(part * 128, part * 128 + 128)

                def three(ref):
                    return jnp.concatenate(
                        [
                            only_half(ref[rows, (h // 2) * 128 : (h // 2) * 128 + 128], h % 2)
                            for h in range(3 * j, 3 * j + 3)
                        ],
                        axis=0,
                    )

                queries = three(query_rot)
                d_mix = three(d_mixed_heads)
                probs = probs_in[0, j, :, probs_at(part) : probs_at(part) + keys]
                probs_f = probs.astype(f32)
                d_probs = dot_nt(d_mix, value_both[0:keys, at])
                product = probs_f * d_probs
                d_scores = product - probs_f * jnp.sum(product, axis=1, keepdims=True)
                d_scores = d_scores.astype(bf16)
                d_query = dot_nn(d_scores, key_both[0:keys, at])
                for g in range(GROUP):
                    head_parts[3 * j + g, rows, :] = d_query[g * 128 : g * 128 + 128]
                d_key = dot_tn(d_scores, queries)
                d_value = dot_tn(probs, d_mix)
                if part == 2:
                    key_parts[j] = d_key
                    value_parts[j] = d_value
                else:
                    key_parts[j, 0:keys, :] += d_key
                    value_parts[j, 0:keys, :] += d_value

        low = lane_index((MB_TOK, 128)) < 64
        cosine, sine = (cosines[...], sines[...])
        empty = jnp.zeros((MB_TOK, 128), f32)
        for c in range(8):
            upper = head_parts[2 * c + 1] if 2 * c + 1 < HEADS else empty
            joined = jnp.where(low, head_parts[2 * c], upper) * HEAD**-0.5
            d_heads[:, c * 128 : c * 128 + 128] = turned(joined, cosine, -sine).astype(bf16)

        def summed(ref, j):
            return ref[j] + pltpu.roll(ref[j], 64, 1)

        for c in range(3):
            for place, ref in ((1024, key_parts), (1408, value_parts)):
                upper = summed(ref, 2 * c + 1) if 2 * c + 1 < KV_HEADS else empty
                joined = jnp.where(low, summed(ref, 2 * c), upper)
                if place == 1024:
                    joined = turned(joined * HEAD**-0.5, cosine, -sine)
                d_heads[:, place + c * 128 : place + c * 128 + 128] = joined.astype(bf16)
        d_query_low = d_heads[:, 0:1024]
        d_key_value_low = d_heads[:, 1024:1792]
        query_wire = dot_nt(d_query_low, query_from[...])
        key_value_wire = dot_nt(d_key_value_low, key_value_from[...])
        output_wire = dot_nt(d_branch, output_from[...]).astype(bf16)
        for quarter in range(REPS):
            base = quarter * 512
            from_query = query_wire[:, quarter * 256 : quarter * 256 + 256]
            from_key = key_value_wire[:, quarter * 384 : quarter * 384 + 384]
            wire_in[:, base : base + 128] = from_query[:, 0:128].astype(bf16)
            wire_in[:, base + 128 : base + 256] = (
                from_query[:, 128:256] + from_key[:, 0:128]
            ).astype(bf16)
            wire_in[:, base + 256 : base + 512] = from_key[:, 128:384].astype(bf16)
        wire_out[...] = output_wire
        d_normed = dot_nt(d_query_low, w_query[...]) + dot_nt(d_key_value_low, w_key_value[...])
        values = inputs[...].astype(f32)
        scale = lax.rsqrt(
            jnp.sum(values * values, axis=1, keepdims=True) * (1.0 / D) + norm_epsilon
        )
        weighted = d_normed * gain_one
        inner = jnp.sum(weighted * values, axis=1, keepdims=True) * (1.0 / D)
        term_one = jnp.sum(d_normed * values * scale, axis=0, keepdims=True)
        total = d_middle + scale * weighted - values * scale * scale * scale * inner
        token_grad[...] = dot_nt(total.astype(bf16), spread[0:D, :]).astype(bf16)

        @pl.when(step == 0)
        def _():
            gain_sums[...] = jnp.zeros_like(gain_sums)

        gain_sums[0:1, :] += term_one
        gain_sums[1:2, :] += term_two

    one_batch()


def attn_grads_kernel(
    normed, mixed, wire_in, wire_out, gain_sums, one_zero, one_one, two_zero, two_one
):
    normed_turned = normed[...].T
    mixed_turned = mixed[...].T
    row = lax.broadcasted_iota(jnp.int32, (SLOTS, 16, SLOT), 1)
    gain_rows = jnp.zeros((SLOTS, 16, SLOT), f32)
    for which in range(2):
        spots = [
            gain_sums[which : which + 1, s * SLOT : s * SLOT + SLOT].reshape(1, 1, SLOT)
            for s in range(SLOTS)
        ]
        gain_rows = jnp.where(row == 8 + which, jnp.concatenate(spots, axis=0), gain_rows)
    for quarter in range(REPS):
        first = dot_nn(normed_turned, wire_in[:, quarter * 512 : quarter * 512 + 512])
        second = dot_nn(mixed_turned, wire_out[:, quarter * 256 : quarter * 256 + 256])
        block = jnp.concatenate(
            [first[:, 0:384], first[:, 384:512] + second[:, 0:128], second[:, 128:256]], axis=1
        ).reshape(SLOTS, SLOT, PACK)
        y, core = (quarter >> 1, quarter & 1)
        low_rows = block[:, 0:ROWS_A, :].astype(bf16)
        high_rows = block[:, ROWS_A:SLOT, :].astype(bf16)
        (one_zero, one_one)[core][y, :, :, :] = low_rows
        target = (two_zero, two_one)[core]
        tail = (block[:, 112:SLOT, 0:SLOT] + gain_rows).astype(bf16)
        for side in range(2):
            slots = slice(side * 4, side * 4 + 4)
            target[side, y * 4 : y * 4 + 4, :, :] = high_rows[slots]
            target[side, y * 4 : y * 4 + 4, 48:64, 0:SLOT] = tail[slots]


def attn_backward(
    cotangent,
    middle,
    d_normed_two,
    inputs,
    query_rot,
    key_both,
    value_both,
    probs,
    tables,
    gains,
    places,
    weights,
):
    tokens = inputs.shape[0]
    count = tokens // MB_TOK

    def per_batch(columns):
        return pl.BlockSpec((MB_TOK, columns), lambda i: (i, 0))

    return pl.pallas_call(
        attn_backward_kernel,
        grid=(count,),
        in_specs=[
            per_batch(WIDE),
            per_batch(WIDE),
            per_batch(WIDE),
            per_batch(WIDE),
            per_batch(WIDE),
            per_batch(PACK),
            per_batch(PACK),
            pl.BlockSpec((1, KV_HEADS, MB_TOK, 768), lambda i: (i, 0, 0, 0)),
            per_batch(128),
            per_batch(128),
            whole_block((8, WIDE)),
        ]
        + [whole_block(place.shape) for place in places]
        + [whole_block(weight.shape) for weight in weights],
        out_specs=[
            per_batch(D),
            per_batch(REPS * 512),
            per_batch(REPS * 256),
            whole_block((8, WIDE)),
        ],
        out_shape=[
            jax.ShapeDtypeStruct((tokens, D), bf16),
            jax.ShapeDtypeStruct((tokens, REPS * 512), bf16),
            jax.ShapeDtypeStruct((tokens, REPS * 256), bf16),
            jax.ShapeDtypeStruct((8, WIDE), f32),
        ],
        scratch_shapes=[
            pltpu.VMEM((MB_TOK, WIDE), bf16),
            pltpu.VMEM((HEADS, MB_TOK, 128), f32),
            pltpu.VMEM((KV_HEADS, MB_TOK, 128), f32),
            pltpu.VMEM((KV_HEADS, MB_TOK, 128), f32),
            pltpu.VMEM((MB_TOK, 1792), bf16),
        ],
        compiler_params=pltpu.CompilerParams(vmem_limit_bytes=VMEM_BYTES),
        cost_estimate=pl.CostEstimate(
            flops=32_000_000_000, bytes_accessed=40_000_000, transcendentals=0
        ),
        name="attn_backward",
    )(
        cotangent,
        middle,
        d_normed_two,
        inputs,
        query_rot,
        key_both,
        value_both,
        probs,
        *tables,
        gains,
        *places,
        *weights,
    )


def attn_grads(normed, mixed, wire_in, wire_out, gain_sums):
    half = jax.ShapeDtypeStruct((2, SLOTS, ROWS_A, PACK), bf16)
    arrays = (normed, mixed, wire_in, wire_out, gain_sums)
    return pl.pallas_call(
        attn_grads_kernel,
        grid=(1,),
        in_specs=[whole_block(array.shape) for array in arrays],
        out_specs=[whole_block(half.shape)] * 4,
        out_shape=[half] * 4,
        compiler_params=pltpu.CompilerParams(vmem_limit_bytes=VMEM_BYTES),
        cost_estimate=pl.CostEstimate(
            flops=8_000_000_000, bytes_accessed=14_000_000, transcendentals=0
        ),
        name="attn_grads",
    )(*arrays)


X_SIDE = ("fsdp", 1)
Y_SIDE = ("rep", 2)
CORE = ("rep", 1)


def swap_with(values, step):
    axis, mask = step
    count = lax.axis_size(axis)
    return lax.ppermute(values, axis, [(i, i ^ mask) for i in range(count)])


def after(values, *done):
    return lax.optimization_barrier((values, done))[0]


def along_z(block):
    return jnp.stack([block] + [swap_with(block, ("fsdp", 2 * k)) for k in range(1, 4)])


def sides_of(side_first):
    return (X_SIDE, Y_SIDE) if side_first else (Y_SIDE, X_SIDE)


def along_first(four, side_first):
    return jnp.concatenate([four, swap_with(four, sides_of(side_first)[0])])


def along_second(eight, side_first):
    return swap_with(eight, sides_of(side_first)[1])


def along_core(eight, across):
    return (eight, swap_with(eight, CORE), across, swap_with(across, CORE))


def added(left, right):
    return (left.astype(f32) + right.astype(f32)).astype(bf16)


class Reduction:
    def __init__(self, kept, sent, side_first):
        self.kept = kept
        self.sent = sent
        self.first, self.second = sides_of(side_first)

    def over_core(self):
        came = swap_with(self.sent, CORE)
        self.out = added(self.kept[1], came[1])
        self.eight = added(self.kept[0], came[0])

    def over_second(self):
        came = swap_with(self.out, self.second)
        self.out = added(self.eight[4:8], came[4:8])
        self.four = added(self.eight[0:4], came[0:4])

    def over_first(self):
        came = swap_with(self.out, self.first)
        self.blocks = [added(self.four[k], came[k]) for k in range(4)]

    def over_z(self):
        came = [swap_with(self.blocks[k], ("fsdp", 2 * k)) for k in range(1, 4)]
        return sum((block.astype(f32) for block in came), self.blocks[0].astype(f32))


def split_parts(blocks, side_first):
    rows, columns = blocks.shape[2:]
    grid = blocks.reshape(4, 2, 2, 2, rows, columns)
    parts = []
    for second in range(2):
        for core in range(2):
            if side_first:
                part = grid[:, :, second, core].transpose(1, 0, 2, 3)
            else:
                part = grid[:, second, :, core].transpose(1, 0, 2, 3)
            parts.append(part.reshape(SLOTS, rows, columns))
    return parts


def join_parts(kept, sent, side_first):
    rows, columns = kept.shape[2:]
    grid = jnp.stack([kept, sent]).reshape(2, 2, 2, 4, rows, columns)
    grid = grid.transpose(3, 2, 1, 0, 4, 5) if side_first else grid.transpose(3, 1, 2, 0, 4, 5)
    return grid.reshape(SLOTS, REPS, rows, columns)


def attn_block(w_query, w_key, w_value, w_output, attn_gain, mlp_gain):
    matrices = jnp.concatenate([w_query, w_key, w_value, w_output], axis=1)
    gains = jnp.stack([attn_gain, mlp_gain])
    gains = jnp.pad(gains, ((0, SLOT - USED - 2), (0, PACK - USED)))
    return jnp.concatenate([matrices, gains], axis=0)


def down_block(w_down):
    halves = w_down.T.reshape(2, USED, HALF_PACK)
    halves = jnp.concatenate([halves[0], halves[1]], axis=1)
    return jnp.pad(halves, ((0, SLOT - USED), (0, 0)))


def mlp_blocks(w_gate, w_up, w_down):
    taller = ((0, SLOT - USED), (0, 0))
    down = down_block(w_down)
    return (
        jnp.concatenate([jnp.pad(w_gate, taller), down[:ROWS_A]], axis=0),
        jnp.concatenate([jnp.pad(w_up, taller), down[ROWS_A:]], axis=0),
    )


def down_of(block):
    halves = jnp.stack([block[:USED, :HALF_PACK], block[:USED, HALF_PACK:]])
    return halves.reshape(2 * USED, HALF_PACK).T


def whole(shard):
    return lax.all_gather(lax.all_gather(shard, "rep", axis=1, tiled=True), "fsdp", axis=0, tiled=True)


def cut(matrix, eighth, quarter):
    rows, columns = (matrix.shape[0] // SLOTS, matrix.shape[1] // REPS)
    return matrix[
        eighth * rows : eighth * rows + rows, quarter * columns : quarter * columns + columns
    ]


def every_block(make):
    return jnp.stack(
        [jnp.stack([make(e, q) for q in range(REPS)]) for e in range(SLOTS)]
    )


def owned(blocks):
    eighths, quarters, rows, columns = blocks.shape
    matrix = blocks.transpose(0, 2, 1, 3).reshape(eighths * rows, quarters * columns)
    part = lax.psum_scatter(matrix, "fsdp", scatter_dimension=0, tiled=True)
    return lax.psum_scatter(part, "rep", scatter_dimension=1, tiled=True).astype(f32)


def per_device(
    tokens,
    lengths,
    attn_gain,
    w_query,
    w_key,
    w_value,
    w_output,
    mlp_gain,
    w_gate,
    w_up,
    w_down,
    cotangent,
):
    paired = lax.axis_size("fsdp") == SLOTS and lax.axis_size("rep") == REPS
    if paired:
        eighth_here = lax.axis_index("fsdp").astype(jnp.int32)
        quarter_here = lax.axis_index("rep").astype(jnp.int32)
        attn_pack = attn_block(w_query, w_key, w_value, w_output, attn_gain, mlp_gain)
        mlp_first, mlp_second = mlp_blocks(w_gate, w_up, w_down)
        one, two = (along_z(attn_pack[:ROWS_A]), along_z(attn_pack[ROWS_A:]))
        mlp_first, mlp_second = after((mlp_first, mlp_second), one, two)
        three, four = (along_z(mlp_first), along_z(mlp_second))
        one, two = (along_first(one, True), along_first(two, False))
        one_across, two_across = (along_second(one, True), along_second(two, False))
        first_parts = along_core(one, one_across)
        second_parts = along_core(two, two_across)
        three, four = after((three, four), one_across, two_across)
        three, four = (along_first(three, True), along_first(four, False))
        first_parts, second_parts = after((first_parts, second_parts), three, four)
        three_across, four_across = (along_second(three, True), along_second(four, False))
        mlp_first_parts = along_core(three, three_across)
        mlp_second_parts = along_core(four, four_across)
    else:
        eighth_here = jnp.int32(0)
        quarter_here = jnp.int32(0)
        gain_one, gain_two = (
            lax.all_gather(attn_gain, "fsdp", axis=0, tiled=True).reshape(SLOTS, USED),
            lax.all_gather(mlp_gain, "fsdp", axis=0, tiled=True).reshape(SLOTS, USED),
        )
        mats = [whole(w) for w in (w_query, w_key, w_value, w_output, w_gate, w_up, w_down)]
        attn_blocks = every_block(
            lambda e, q: attn_block(*[cut(m, e, q) for m in mats[:4]], gain_one[e], gain_two[e])
        )
        first_parts = split_parts(attn_blocks[:, :, :ROWS_A], True)
        second_parts = split_parts(attn_blocks[:, :, ROWS_A:], False)
        mlp_each = [
            [
                mlp_blocks(cut(mats[4], e, q), cut(mats[5], e, q), cut(mats[6], e, q))
                for q in range(REPS)
            ]
            for e in range(SLOTS)
        ]
        mlp_first_parts = split_parts(every_block(lambda e, q: mlp_each[e][q][0]), True)
        mlp_second_parts = split_parts(every_block(lambda e, q: mlp_each[e][q][1]), False)
    here = jnp.stack([eighth_here, quarter_here])
    places = placing(eighth_here, quarter_here)
    spread = places[0]
    segments, positions = jax.vmap(layout)(lengths)
    tables = rope_tables(positions.reshape(-1))
    inputs = jnp.dot(tokens, spread[:D], preferred_element_type=f32).astype(bf16)
    upstream = jnp.dot(cotangent, spread[:D], preferred_element_type=f32).astype(bf16)
    upstream_turned = upstream.T
    (
        normed,
        query_rot,
        key_both,
        value_both,
        probs,
        mixed,
        middle,
        normed_two,
        *weights,
        gains,
    ) = attn_forward(inputs, places, tables, segments, first_parts, second_parts)
    hidden, d_gate, d_up, w_down_all = mlp_activations(
        here, normed_two, upstream, mlp_first_parts, mlp_second_parts
    )
    three_kept, three_sent, four_kept, four_sent = mlp_grads(
        here, normed_two, upstream_turned, hidden, d_gate, d_up
    )
    three = Reduction(three_kept, three_sent, True)
    four = Reduction(four_kept, four_sent, False)
    hidden, d_gate, d_up = after((hidden, d_gate, d_up), three_kept, four_kept)
    mlp_out, d_normed_two = mlp_outputs(
        hidden, d_gate, d_up, w_down_all, mlp_first_parts, mlp_second_parts
    )
    if paired:
        three.over_core()
        four.over_core()
        d_normed_two = after(d_normed_two, three.out, four.out)
    token_grad, wire_in, wire_out, gain_parts = attn_backward(
        upstream,
        middle,
        d_normed_two,
        inputs,
        query_rot,
        key_both,
        value_both,
        probs,
        tables,
        gains,
        places,
        weights,
    )
    if paired:
        three.over_second()
        four.over_second()
        wire_in = after(wire_in, three.out, four.out)
    one_kept, one_sent, two_kept, two_sent = attn_grads(
        normed, mixed, wire_in, wire_out, gain_parts
    )
    output = jnp.dot(
        (middle + mlp_out).astype(bf16), spread[:D].T, preferred_element_type=f32
    ).astype(bf16)
    if paired:
        one = Reduction(one_kept, one_sent, True)
        two = Reduction(two_kept, two_sent, False)
        one.over_core()
        two.over_core()
        three.over_first()
        four.over_first()
        one.over_second()
        two.over_second()
        three_sum = three.over_z()
        four_sum = four.over_z()
        one.over_first()
        two.over_first()
        first_sum = one.over_z()
        second_sum = two.over_z()
        attn_sum = jnp.concatenate([first_sum, second_sum], axis=0)
        gain_sums = (attn_sum[USED, :USED], attn_sum[USED + 1, :USED])
        attn_sum = attn_sum[:USED]
        grads = [
            attn_sum[:, 0:240],
            attn_sum[:, 240:320],
            attn_sum[:, 320:400],
            attn_sum[:, 400:640],
            three_sum[:USED],
            four_sum[:USED],
            down_of(jnp.concatenate([three_sum[SLOT:], four_sum[SLOT:]], axis=0)),
        ]
    else:
        attn_blocks = jnp.concatenate(
            [join_parts(one_kept, one_sent, True), join_parts(two_kept, two_sent, False)], axis=2
        )
        gain_sums = tuple(
            lax.psum(
                lax.psum_scatter(
                    attn_blocks[:, 0, USED + which, :USED].astype(f32).reshape(D),
                    "fsdp",
                    scatter_dimension=0,
                    tiled=True,
                ),
                "rep",
            )
            for which in range(2)
        )
        attn_blocks = attn_blocks[:, :, :USED]
        three_blocks = join_parts(three_kept, three_sent, True)
        four_blocks = join_parts(four_kept, four_sent, False)
        down_blocks = jnp.concatenate([three_blocks[:, :, SLOT:], four_blocks[:, :, SLOT:]], axis=2)
        grads = [
            owned(attn_blocks[..., 0:240]),
            owned(attn_blocks[..., 240:320]),
            owned(attn_blocks[..., 320:400]),
            owned(attn_blocks[..., 400:640]),
            owned(three_blocks[:, :, :USED]),
            owned(four_blocks[:, :, :USED]),
            owned(jax.vmap(jax.vmap(down_of))(down_blocks)),
        ]
    return (
        output,
        token_grad,
        gain_sums[0],
        grads[0],
        grads[1],
        grads[2],
        grads[3],
        gain_sums[1],
        grads[4],
        grads[5],
        grads[6],
    )


def solution(mesh):
    placed = (
        P(("fsdp", "rep"), None),
        P(("fsdp", "rep"), None),
        P("fsdp"),
        P("fsdp", "rep"),
        P("fsdp", "rep"),
        P("fsdp", "rep"),
        P("fsdp", "rep"),
        P("fsdp"),
        P("fsdp", "rep"),
        P("fsdp", "rep"),
        P("fsdp", "rep"),
        P(("fsdp", "rep"), None),
    )
    return jax.shard_map(
        per_device,
        mesh=mesh,
        in_specs=placed,
        out_specs=(
            P(("fsdp", "rep"), None),
            P(("fsdp", "rep"), None),
            P("fsdp"),
            P("fsdp", "rep"),
            P("fsdp", "rep"),
            P("fsdp", "rep"),
            P("fsdp", "rep"),
            P("fsdp"),
            P("fsdp", "rep"),
            P("fsdp", "rep"),
            P("fsdp", "rep"),
        ),
        check_vma=False,
    )
```

```python
import jax
import jax.numpy as jnp
from jax import lax
from jax.experimental import pallas as pl
from jax.experimental.pallas import tpu as pltpu
from jax.sharding import PartitionSpec as P

D = 960
FF = 2560
HEADS = 15
KV_HEADS = 5
HEAD = 64
MB_TOK = 384
SEGS = 3
GROUP = 3
QW = 960
KVW = 320

SLOTS = 8
REPS = 4
USED = 120
SLOT = 128
WIDE = SLOTS * SLOT
PACK = 640
HALF_PACK = 320
ROWS_A = 64
ROWS_M = 96
REST = SLOT - ROWS_M
VMEM_BYTES = 60 * 1024 * 1024

norm_epsilon = 1e-05
rope_base = 100000.0
masked_value = -1e30

f32 = jnp.float32
bf16 = jnp.bfloat16


def layout(length_row):
    starts = jnp.cumsum(length_row) - length_row
    places = jnp.arange(MB_TOK, dtype=jnp.int32)
    inside = (
        (places[:, None] >= starts[None, :]) & (places[:, None] < (starts + length_row)[None, :])
    ).astype(jnp.int32)
    segment = jnp.sum(inside * jnp.arange(SEGS, dtype=jnp.int32)[None, :], axis=1)
    position = places - jnp.sum(inside * starts[None, :], axis=1)
    return (segment, position)


def rope_tables(position):
    half_width = HEAD // 2
    exponent = jnp.arange(half_width, dtype=f32) * (2.0 / HEAD)
    inverse = jnp.power(rope_base, -exponent)
    angles = position.astype(f32)[:, None] * inverse
    cosines, sines = (jnp.cos(angles), jnp.sin(angles))
    return (
        jnp.concatenate([cosines] * 4, axis=1),
        jnp.concatenate([-sines, sines, -sines, sines], axis=1),
    )


def slot_of(eighth):
    return (eighth & 1) * 4 + (eighth >> 1)


def eighth_of(slot):
    return (slot & 3) * 2 + (slot >> 2)


def feature_lanes(eighth_here):
    lanes = jnp.arange(WIDE, dtype=jnp.int32)
    eighth = eighth_of(lanes // SLOT) ^ eighth_here
    return jnp.where(lanes % SLOT < USED, eighth * USED + lanes % SLOT, -1)


def one_hot(rows, wanted):
    return (jnp.arange(rows, dtype=jnp.int32)[:, None] == wanted[None, :]).astype(bf16)


def placing(eighth_here, quarter_here):
    features = feature_lanes(eighth_here)
    spread = one_hot(WIDE, features)
    columns = jnp.arange(WIDE, dtype=jnp.int32)
    query_from = jnp.where(
        columns < QW, ((columns // 240) ^ quarter_here) * 256 + columns % 240, -1
    )
    key_columns = jnp.arange(384, dtype=jnp.int32)
    key_from = ((key_columns // 80) ^ quarter_here) * 384 + key_columns % 80
    key_value_from = jnp.concatenate(
        [
            jnp.where(key_columns < KVW, key_from + 112, -1),
            jnp.where(key_columns < KVW, key_from + 192, -1),
        ]
    )
    output_from = jnp.where(
        features >= 0, ((features // 240) ^ quarter_here) * 256 + 16 + features % 240, -1
    )
    return (
        spread,
        one_hot(1024, query_from),
        one_hot(1536, key_value_from),
        one_hot(1024, output_from),
    )


def dot_nn(left, right):
    return lax.dot_general(left, right, (((1,), (0,)), ((), ())), preferred_element_type=f32)


def dot_nt(left, right):
    return lax.dot_general(left, right, (((1,), (1,)), ((), ())), preferred_element_type=f32)


def dot_tn(left, right):
    return lax.dot_general(left, right, (((0,), (0,)), ((), ())), preferred_element_type=f32)


def lane_index(shape):
    return lax.broadcasted_iota(jnp.int32, shape, len(shape) - 1)


def swapped(values):
    first = (lane_index(values.shape) & 63) < 32
    return jnp.where(first, pltpu.roll(values, 96, 1), pltpu.roll(values, 32, 1))


def turned(values, cosines, sines):
    return values * cosines + swapped(values) * sines


def both_halves(values, odd):
    low = lane_index(values.shape) < 64
    moved = pltpu.roll(values, 64, 1)
    return jnp.where(low, moved, values) if odd else jnp.where(low, values, moved)


def only_half(values, odd):
    low = lane_index(values.shape) < 64
    return jnp.where(low != bool(odd), values, jnp.zeros_like(values))


def gain_row(attn_ref, which):
    rows = [attn_ref[0, s, 112:128, 0:SLOT].astype(f32)[8 + which : 9 + which] for s in range(SLOTS)]
    return jnp.concatenate(rows, axis=1)


def probs_at(part):
    return (0, 128, 384)[part]


def attn_weights_kernel(
    query_from,
    key_value_from,
    output_from,
    a0,
    a1,
    a2,
    a3,
    b0,
    b1,
    b2,
    b3,
    w_query,
    w_key_value,
    w_output,
    gains_out,
    attn_all,
    sems,
):
    copies = []
    for quarter, source in enumerate((a0, a1, a2, a3)):
        copies.append((source, attn_all.at[quarter, :, 0:ROWS_A, :]))
    for place, source in enumerate((b0, b1, b2, b3)):
        side, core = (place >> 1, place & 1)
        for y in range(2):
            copies.append(
                (
                    source.at[y * 4 : y * 4 + 4],
                    attn_all.at[y * 2 + core, side * 4 : side * 4 + 4, ROWS_A : 2 * ROWS_A, :],
                )
            )
    started = [
        pltpu.make_async_copy(source, target, sems.at[n])
        for n, (source, target) in enumerate(copies)
    ]
    for copy in started:
        copy.start()
    for copy in started:
        copy.wait()

    def columns(low, high):
        return jnp.concatenate(
            [
                attn_all[quarter, :, :, low:high].reshape(WIDE, high - low)
                for quarter in range(REPS)
            ],
            axis=1,
        )

    w_query[...] = dot_nn(columns(0, 256), query_from[...]).astype(bf16)
    w_key_value[...] = dot_nn(columns(128, 512), key_value_from[...]).astype(bf16)
    w_output[...] = dot_nn(columns(384, 640), output_from[...]).astype(bf16)
    gains_out[0:1, :] = gain_row(attn_all, 0)
    gains_out[1:2, :] = gain_row(attn_all, 1)


def attn_forward_kernel(
    inputs,
    spread,
    w_query,
    w_key_value,
    w_output,
    gains,
    cosines,
    sines,
    segment_rows,
    segment_columns,
    normed_out,
    query_out,
    key_out,
    value_out,
    probs_out,
    mixed_out,
    middle_out,
    normed_two_out,
    heads_out,
    mixed_heads,
    bias,
):
    values = inputs[...].astype(f32)
    gain_one = gains[0:1, :]
    gain_two = gains[1:2, :]
    scale = lax.rsqrt(jnp.sum(values * values, axis=1, keepdims=True) * (1.0 / D) + norm_epsilon)
    normed = (values * scale * gain_one).astype(bf16)
    normed_out[...] = normed
    cosine, sine = (cosines[...], sines[...])
    query_lin = dot_nn(normed, w_query[...])
    for c in range(8):
        at = slice(c * 128, c * 128 + 128)
        query_out[:, at] = turned(query_lin[:, at], cosine, sine).astype(bf16)
    key_value = dot_nn(normed, w_key_value[...])
    for c in range(3):
        key_part = turned(key_value[:, c * 128 : c * 128 + 128], cosine, sine)
        value_part = key_value[:, 384 + c * 128 : 384 + c * 128 + 128]
        for odd in range(2 if c < 2 else 1):
            at = slice((2 * c + odd) * 128, (2 * c + odd) * 128 + 128)
            key_out[:, at] = both_halves(key_part, odd).astype(bf16)
            value_out[:, at] = both_halves(value_part, odd).astype(bf16)

    query_place = lax.broadcasted_iota(jnp.int32, (MB_TOK, MB_TOK), 0)
    key_place = lax.broadcasted_iota(jnp.int32, (MB_TOK, MB_TOK), 1)
    seen = (segment_rows[...] == segment_columns[0]) & (key_place <= query_place)
    bias[...] = jnp.where(seen, 0.0, masked_value)
    for j in range(KV_HEADS):
        at = slice(j * 128, j * 128 + 128)
        for part in range(3):
            keys = 128 * (part + 1)
            rows = slice(part * 128, part * 128 + 128)
            queries = jnp.concatenate(
                [
                    only_half(query_out[rows, (h // 2) * 128 : (h // 2) * 128 + 128], h % 2)
                    for h in range(3 * j, 3 * j + 3)
                ],
                axis=0,
            )
            scores = dot_nt(queries, key_out[0:keys, at]) * HEAD**-0.5
            hidden_part = bias[rows, 0:keys]
            scores = scores + jnp.concatenate([hidden_part] * GROUP, axis=0)
            peak = jnp.max(scores, axis=1, keepdims=True)
            weights = jnp.exp(scores - peak)
            total = jnp.sum(weights, axis=1, keepdims=True)
            probs = (weights * (1.0 / total)).astype(bf16)
            probs_out[j, :, probs_at(part) : probs_at(part) + keys] = probs
            gathered = dot_nn(probs, value_out[0:keys, at])
            for g in range(GROUP):
                heads_out[3 * j + g, rows, :] = gathered[g * 128 : g * 128 + 128]
    low = lane_index((MB_TOK, 128)) < 64
    for c in range(8):
        upper = heads_out[2 * c + 1] if 2 * c + 1 < HEADS else jnp.zeros((MB_TOK, 128), f32)
        mixed_heads[:, c * 128 : c * 128 + 128] = jnp.where(low, heads_out[2 * c], upper).astype(bf16)
    mixed = dot_nn(mixed_heads[...], spread[...]).astype(bf16)
    mixed_out[...] = mixed
    middle = values + dot_nn(mixed, w_output[...])
    middle_out[...] = middle
    scale_two = lax.rsqrt(
        jnp.sum(middle * middle, axis=1, keepdims=True) * (1.0 / D) + norm_epsilon
    )
    normed_two_out[...] = (middle * scale_two * gain_two).astype(bf16)


def whole_block(shape):
    return pl.BlockSpec(
        shape, lambda *ids: (0,) * len(shape), pipeline_mode=pl.Buffered(buffer_count=1)
    )


def anywhere():
    return pl.BlockSpec(memory_space=pl.ANY)


def batch_block(batch, columns):
    return pl.BlockSpec((MB_TOK, columns), lambda i: (batch, 0))


def attn_weights(places, first_parts, second_parts):
    outs = [(WIDE, 1024, bf16), (WIDE, 768, bf16), (WIDE, WIDE, bf16), (8, WIDE, f32)]
    return pl.pallas_call(
        attn_weights_kernel,
        grid=(1,),
        in_specs=[whole_block(place.shape) for place in places] + [anywhere()] * 8,
        out_specs=[whole_block(out[:2]) for out in outs],
        out_shape=[jax.ShapeDtypeStruct(out[:2], out[2]) for out in outs],
        scratch_shapes=[
            pltpu.VMEM((REPS, SLOTS, SLOT, PACK), bf16),
            pltpu.SemaphoreType.DMA((12,)),
        ],
        compiler_params=pltpu.CompilerParams(vmem_limit_bytes=VMEM_BYTES),
        cost_estimate=pl.CostEstimate(
            flops=8_000_000_000, bytes_accessed=16_000_000, transcendentals=0
        ),
        name="attn_weights",
    )(*places, *first_parts, *second_parts)


def attn_forward(batch, inputs, spread, weights, gains, tables, segments):
    count = inputs.shape[0] // MB_TOK
    whole_in = (spread, *weights, gains)
    outs = [
        ((MB_TOK, WIDE), bf16),
        ((MB_TOK, WIDE), bf16),
        ((MB_TOK, PACK), bf16),
        ((MB_TOK, PACK), bf16),
        ((KV_HEADS, MB_TOK, 768), bf16),
        ((MB_TOK, WIDE), bf16),
        ((MB_TOK, WIDE), f32),
        ((MB_TOK, WIDE), bf16),
    ]
    return pl.pallas_call(
        attn_forward_kernel,
        grid=(1,),
        in_specs=[batch_block(batch, WIDE)]
        + [whole_block(array.shape) for array in whole_in]
        + [
            batch_block(batch, 128),
            batch_block(batch, 128),
            batch_block(batch, 1),
            pl.BlockSpec((1, 1, MB_TOK), lambda i: (batch, 0, 0)),
        ],
        out_specs=[whole_block(out[0]) for out in outs],
        out_shape=[jax.ShapeDtypeStruct(*out) for out in outs],
        scratch_shapes=[
            pltpu.VMEM((HEADS, MB_TOK, 128), f32),
            pltpu.VMEM((MB_TOK, WIDE), bf16),
            pltpu.VMEM((MB_TOK, MB_TOK), f32),
        ],
        compiler_params=pltpu.CompilerParams(vmem_limit_bytes=VMEM_BYTES),
        cost_estimate=pl.CostEstimate(
            flops=8_000_000_000, bytes_accessed=16_000_000, transcendentals=2_000_000
        ),
        name="attn_forward",
    )(
        inputs,
        *whole_in,
        *tables,
        segments.reshape(-1, 1),
        segments.reshape(count, 1, MB_TOK),
    )


def left_right(left, right):
    first = lane_index(left.shape) < HALF_PACK
    left, right = (left.astype(f32), right.astype(f32))
    return (
        jnp.where(first, left, pltpu.roll(right, HALF_PACK, 1)).astype(bf16),
        jnp.where(first, pltpu.roll(left, HALF_PACK, 1), right).astype(bf16),
    )


def pair_fetches(parts, at, w_gate, w_up, sems):
    found = []
    for group, target in enumerate((w_gate, w_up)):
        firsts, seconds = (parts[8 * group : 8 * group + 4], parts[8 * group + 4 : 8 * group + 8])
        for core in range(2):
            lanes = slice(core * PACK, core * PACK + PACK)
            found.append((firsts[at * 2 + core], target.at[:, 0:ROWS_M, lanes]))
            for side in range(2):
                found.append(
                    (
                        seconds[side * 2 + core].at[at * 4 : at * 4 + 4, 0:REST, :],
                        target.at[side * 4 : side * 4 + 4, ROWS_M:SLOT, lanes],
                    )
                )
    return [
        pltpu.make_async_copy(source, target, sems.at[n])
        for n, (source, target) in enumerate(found)
    ]


def mlp_kernel(here, *refs, count):
    normed = refs[:count]
    cotangent, cotangent_turned = refs[count : count + 2]
    parts = refs[count + 2 : count + 18]
    hidden, d_gate, d_up, down_out = refs[count + 18 : count + 22]
    grads = refs[count + 22 : count + 30]
    (
        w_gate,
        w_up,
        down_raw,
        normed_turned,
        grad_gate,
        grad_up,
        grad_down,
        down_made,
        sem_pair,
        sem_down,
        sem_out,
    ) = refs[count + 30 :]
    step = pl.program_id(0)
    eighth_here, quarter_here = (here[0], here[1])
    side_here = eighth_here & 1

    def plane_of(at, core):
        return ((2 * at + core) ^ quarter_here) ^ (eighth_here >> 1)

    def fetches(at):
        found = []
        for core in range(2):
            for side in range(2):
                for quarter in range(REPS):
                    y, inner = (quarter >> 1, quarter & 1)
                    for group in range(2):
                        found.append(
                            (
                                parts[8 * group + 4 + side * 2 + inner].at[
                                    y * 4 + plane_of(at, core), REST:ROWS_M
                                ],
                                down_raw.at[
                                    core, side, quarter, group * ROWS_A : group * ROWS_A + ROWS_A
                                ],
                            )
                        )
        return pair_fetches(parts, at, w_gate, w_up, sem_pair) + [
            pltpu.make_async_copy(source, target, sem_down.at[n])
            for n, (source, target) in enumerate(found)
        ]

    def results(at):
        found = []
        for group, source in enumerate((grad_gate, grad_up)):
            firsts, seconds = (grads[4 * group : 4 * group + 2], grads[4 * group + 2 : 4 * group + 4])
            for core in range(2):
                found.append((source.at[core, :, 0:ROWS_M], firsts[core].at[at]))
                for side in range(2):
                    found.append(
                        (
                            source.at[core, side * 4 : side * 4 + 4, ROWS_M:SLOT],
                            seconds[core].at[side, at * 4 : at * 4 + 4, 0:REST],
                        )
                    )
                    for quarter in range(REPS):
                        y, inner = (quarter >> 1, quarter & 1)
                        found.append(
                            (
                                down_made.at[
                                    core, side, quarter, group * ROWS_A : group * ROWS_A + ROWS_A
                                ],
                                seconds[inner].at[
                                    side, y * 4 + plane_of(at, core), REST:ROWS_M
                                ],
                            )
                        )
        return [
            pltpu.make_async_copy(source, target, sem_out.at[n])
            for n, (source, target) in enumerate(found)
        ]

    def rows_of(quarter, which):
        eighth = (quarter ^ quarter_here) * 2 + which
        return pl.multiple_of(slot_of(eighth ^ eighth_here) * SLOT, SLOT)

    @pl.when(step == 0)
    def _():
        for copy in fetches(0):
            copy.start()
        for batch in range(count):
            normed_turned[:, batch * MB_TOK : batch * MB_TOK + MB_TOK] = normed[batch][...].T
        for copy in fetches(0):
            copy.wait()

    @pl.when(step == 1)
    def _():
        for copy in fetches(1):
            copy.wait()

    for core in range(2):
        lanes = slice(core * PACK, core * PACK + PACK)
        for quarter in range(REPS):
            lefts, rights = left_right(
                down_raw[core, side_here, quarter], down_raw[core, 1 - side_here, quarter]
            )
            down_out[0, pl.ds(rows_of(quarter, 0), SLOT), lanes] = lefts
            down_out[0, pl.ds(rows_of(quarter, 1), SLOT), lanes] = rights

    gate_weights = w_gate[...].reshape(WIDE, 2 * PACK)
    up_weights = w_up[...].reshape(WIDE, 2 * PACK)
    for batch in range(count):
        rows = slice(batch * MB_TOK, batch * MB_TOK + MB_TOK)
        gate = dot_nn(normed[batch][...], gate_weights)
        up = dot_nn(normed[batch][...], up_weights)
        d_hidden = dot_nn(cotangent[rows, :], down_out[0])
        sigmoid = 1.0 / (1.0 + jnp.exp(-gate))
        silu = gate * sigmoid
        hidden[0, rows, :] = (silu * up).astype(bf16)
        d_gate[0, rows, :] = (d_hidden * up * sigmoid * (1.0 + gate * (1.0 - sigmoid))).astype(bf16)
        d_up[0, rows, :] = (d_hidden * silu).astype(bf16)

    @pl.when(step == 0)
    def _():
        for copy in fetches(1):
            copy.start()

    @pl.when(step == 1)
    def _():
        for copy in results(0):
            copy.wait()

    for half in range(2):
        rows = slice(half * 512, half * 512 + 512)
        four = slice(half * 4, half * 4 + 4)
        gate_part = dot_nn(normed_turned[rows, :], d_gate[0]).astype(bf16)
        up_part = dot_nn(normed_turned[rows, :], d_up[0]).astype(bf16)
        for core in range(2):
            lanes = slice(core * PACK, core * PACK + PACK)
            grad_gate[core, four] = gate_part[:, lanes].reshape(4, SLOT, PACK)
            grad_up[core, four] = up_part[:, lanes].reshape(4, SLOT, PACK)
        grad_down[rows, :] = dot_nn(cotangent_turned[rows, :], hidden[0])
    for core in range(2):
        lanes = slice(core * PACK, core * PACK + PACK)
        for quarter in range(REPS):
            lefts, rights = left_right(
                grad_down[pl.ds(rows_of(quarter, 0), SLOT), lanes],
                grad_down[pl.ds(rows_of(quarter, 1), SLOT), lanes],
            )
            down_made[core, side_here, quarter] = lefts
            down_made[core, 1 - side_here, quarter] = rights
    for at in range(2):

        @pl.when(step == at)
        def _():
            for copy in results(at):
                copy.start()

    @pl.when(step == 1)
    def _():
        for copy in results(1):
            copy.wait()


def chunk_block(rows, columns):
    return pl.BlockSpec((1, rows, columns), lambda i: (i, 0, 0))


def mlp(here, normed, cotangent, cotangent_turned, parts):
    count = len(normed)
    tokens = cotangent.shape[0]
    rows = jax.ShapeDtypeStruct((2, tokens, 2 * PACK), bf16)
    part = jax.ShapeDtypeStruct((2, SLOTS, ROWS_M, PACK), bf16)
    outs = pl.pallas_call(
        lambda *refs: mlp_kernel(*refs, count=count),
        grid=(2,),
        in_specs=[pl.BlockSpec(memory_space=pltpu.SMEM)]
        + [whole_block((MB_TOK, WIDE))] * count
        + [whole_block((tokens, WIDE)), whole_block((WIDE, tokens))]
        + [anywhere()] * 16,
        out_specs=[chunk_block(tokens, 2 * PACK)] * 3
        + [chunk_block(WIDE, 2 * PACK)]
        + [anywhere()] * 8,
        out_shape=[rows, rows, rows, jax.ShapeDtypeStruct((2, WIDE, 2 * PACK), bf16)] + [part] * 8,
        scratch_shapes=[
            pltpu.VMEM((SLOTS, SLOT, 2 * PACK), bf16),
            pltpu.VMEM((SLOTS, SLOT, 2 * PACK), bf16),
            pltpu.VMEM((2, 2, REPS, SLOT, PACK), bf16),
            pltpu.VMEM((WIDE, tokens), bf16),
            pltpu.VMEM((2, SLOTS, SLOT, PACK), bf16),
            pltpu.VMEM((2, SLOTS, SLOT, PACK), bf16),
            pltpu.VMEM((WIDE, 2 * PACK), f32),
            pltpu.VMEM((2, 2, REPS, SLOT, PACK), bf16),
            pltpu.SemaphoreType.DMA((12,)),
            pltpu.SemaphoreType.DMA((32,)),
            pltpu.SemaphoreType.DMA((44,)),
        ],
        compiler_params=pltpu.CompilerParams(vmem_limit_bytes=VMEM_BYTES),
        cost_estimate=pl.CostEstimate(
            flops=30_000_000_000, bytes_accessed=50_000_000, transcendentals=2_000_000
        ),
        name="mlp",
    )(here, *normed, cotangent, cotangent_turned, *parts)
    return (outs[:4], outs[4:])


def mlp_outputs_kernel(hidden, d_gate, d_up, w_down, *refs, count):
    parts = refs[:16]
    outs, d_normed = (refs[16 : 16 + count], refs[16 + count : 16 + 2 * count])
    w_gate, w_up, sem_pair = refs[16 + 2 * count :]
    step = pl.program_id(0)

    def fetches(at):
        return pair_fetches(parts, at, w_gate.at[at], w_up.at[at], sem_pair.at[at])

    @pl.when(step == 0)
    def _():
        for at in range(2):
            for copy in fetches(at):
                copy.start()

    for at in range(2):

        @pl.when(step == at)
        def _():
            for copy in fetches(at):
                copy.wait()
            gate_weights = w_gate[at].reshape(WIDE, 2 * PACK)
            up_weights = w_up[at].reshape(WIDE, 2 * PACK)
            for batch in range(count):
                rows = slice(batch * MB_TOK, batch * MB_TOK + MB_TOK)
                out_part = dot_nt(hidden[0, rows, :], w_down[0])
                normed_part = dot_nt(d_gate[0, rows, :], gate_weights) + dot_nt(
                    d_up[0, rows, :], up_weights
                )
                if at == 0:
                    outs[batch][...] = out_part
                    d_normed[batch][...] = normed_part
                else:
                    outs[batch][...] += out_part
                    d_normed[batch][...] += normed_part


def mlp_outputs(hidden, d_gate, d_up, w_down, parts):
    tokens = hidden.shape[1]
    count = tokens // MB_TOK
    outs = pl.pallas_call(
        lambda *refs: mlp_outputs_kernel(*refs, count=count),
        grid=(2,),
        in_specs=[chunk_block(tokens, 2 * PACK)] * 3
        + [chunk_block(WIDE, 2 * PACK)]
        + [anywhere()] * 16,
        out_specs=[whole_block((MB_TOK, WIDE))] * (2 * count),
        out_shape=[jax.ShapeDtypeStruct((MB_TOK, WIDE), f32)] * (2 * count),
        scratch_shapes=[
            pltpu.VMEM((2, SLOTS, SLOT, 2 * PACK), bf16),
            pltpu.VMEM((2, SLOTS, SLOT, 2 * PACK), bf16),
            pltpu.SemaphoreType.DMA((2, 12)),
        ],
        compiler_params=pltpu.CompilerParams(vmem_limit_bytes=VMEM_BYTES),
        cost_estimate=pl.CostEstimate(
            flops=15_000_000_000, bytes_accessed=35_000_000, transcendentals=0
        ),
        name="mlp_outputs",
    )(hidden, d_gate, d_up, w_down, *parts)
    return (outs[:count], outs[count:])


def attn_backward_kernel(
    cotangent,
    middle,
    d_normed_two,
    inputs,
    query_rot,
    key_both,
    value_both,
    probs_in,
    cosines,
    sines,
    gains,
    spread,
    query_from,
    key_value_from,
    output_from,
    w_query,
    w_key_value,
    w_output,
    token_grad,
    wire_in,
    wire_out,
    gain_sums,
    d_mixed_heads,
    head_parts,
    key_parts,
    value_parts,
    d_heads,
):
    gain_one = gains[0:1, :]
    gain_two = gains[1:2, :]
    mid = middle[...]
    upstream = d_normed_two[...]
    scale_two = lax.rsqrt(jnp.sum(mid * mid, axis=1, keepdims=True) * (1.0 / D) + norm_epsilon)
    weighted = upstream * gain_two
    inner = jnp.sum(weighted * mid, axis=1, keepdims=True) * (1.0 / D)
    term_two = jnp.sum(upstream * mid * scale_two, axis=0, keepdims=True)
    d_middle = (
        cotangent[...].astype(f32)
        + scale_two * weighted
        - mid * scale_two * scale_two * scale_two * inner
    )
    d_branch = d_middle.astype(bf16)
    d_mixed = dot_nt(d_branch, w_output[...]).astype(bf16)
    d_mixed_heads[...] = dot_nt(d_mixed, spread[...]).astype(bf16)
    for j in range(KV_HEADS):
        at = slice(j * 128, j * 128 + 128)
        for part in (2, 1, 0):
            keys = 128 * (part + 1)
            rows = slice(part * 128, part * 128 + 128)

            def three(ref):
                return jnp.concatenate(
                    [
                        only_half(ref[rows, (h // 2) * 128 : (h // 2) * 128 + 128], h % 2)
                        for h in range(3 * j, 3 * j + 3)
                    ],
                    axis=0,
                )

            queries = three(query_rot)
            d_mix = three(d_mixed_heads)
            probs = probs_in[j, :, probs_at(part) : probs_at(part) + keys]
            probs_f = probs.astype(f32)
            d_probs = dot_nt(d_mix, value_both[0:keys, at])
            product = probs_f * d_probs
            d_scores = product - probs_f * jnp.sum(product, axis=1, keepdims=True)
            d_scores = d_scores.astype(bf16)
            d_query = dot_nn(d_scores, key_both[0:keys, at])
            for g in range(GROUP):
                head_parts[3 * j + g, rows, :] = d_query[g * 128 : g * 128 + 128]
            d_key = dot_tn(d_scores, queries)
            d_value = dot_tn(probs, d_mix)
            if part == 2:
                key_parts[j] = d_key
                value_parts[j] = d_value
            else:
                key_parts[j, 0:keys, :] += d_key
                value_parts[j, 0:keys, :] += d_value

    low = lane_index((MB_TOK, 128)) < 64
    cosine, sine = (cosines[...], sines[...])
    empty = jnp.zeros((MB_TOK, 128), f32)
    for c in range(8):
        upper = head_parts[2 * c + 1] if 2 * c + 1 < HEADS else empty
        joined = jnp.where(low, head_parts[2 * c], upper) * HEAD**-0.5
        d_heads[:, c * 128 : c * 128 + 128] = turned(joined, cosine, -sine).astype(bf16)

    def summed(ref, j):
        return ref[j] + pltpu.roll(ref[j], 64, 1)

    for c in range(3):
        for place, ref in ((1024, key_parts), (1408, value_parts)):
            upper = summed(ref, 2 * c + 1) if 2 * c + 1 < KV_HEADS else empty
            joined = jnp.where(low, summed(ref, 2 * c), upper)
            if place == 1024:
                joined = turned(joined * HEAD**-0.5, cosine, -sine)
            d_heads[:, place + c * 128 : place + c * 128 + 128] = joined.astype(bf16)
    d_query_low = d_heads[:, 0:1024]
    d_key_value_low = d_heads[:, 1024:1792]
    query_wire = dot_nt(d_query_low, query_from[...])
    key_value_wire = dot_nt(d_key_value_low, key_value_from[...])
    output_wire = dot_nt(d_branch, output_from[...]).astype(bf16)
    for quarter in range(REPS):
        base = quarter * 512
        from_query = query_wire[:, quarter * 256 : quarter * 256 + 256]
        from_key = key_value_wire[:, quarter * 384 : quarter * 384 + 384]
        wire_in[:, base : base + 128] = from_query[:, 0:128].astype(bf16)
        wire_in[:, base + 128 : base + 256] = (
            from_query[:, 128:256] + from_key[:, 0:128]
        ).astype(bf16)
        wire_in[:, base + 256 : base + 512] = from_key[:, 128:384].astype(bf16)
    wire_out[...] = output_wire
    d_normed = dot_nt(d_query_low, w_query[...]) + dot_nt(d_key_value_low, w_key_value[...])
    values = inputs[...].astype(f32)
    scale = lax.rsqrt(
        jnp.sum(values * values, axis=1, keepdims=True) * (1.0 / D) + norm_epsilon
    )
    weighted = d_normed * gain_one
    inner = jnp.sum(weighted * values, axis=1, keepdims=True) * (1.0 / D)
    term_one = jnp.sum(d_normed * values * scale, axis=0, keepdims=True)
    total = d_middle + scale * weighted - values * scale * scale * scale * inner
    token_grad[...] = total.astype(bf16)

    gain_sums[0:1, :] = term_one
    gain_sums[1:2, :] = term_two


def attn_grads_kernel(*refs, count):
    normed, mixed, wires_in, wires_out, gain_parts = [
        refs[n * count : n * count + count] for n in range(5)
    ]
    one_zero, one_one, two_zero, two_one = refs[5 * count : 5 * count + 4]
    gain_sums = sum(part[0:8, :] for part in gain_parts)

    def stacked(parts):
        return jnp.concatenate([part[...] for part in parts], axis=0)

    normed_turned = stacked(normed).T
    mixed_turned = stacked(mixed).T
    wire_in, wire_out = (stacked(wires_in), stacked(wires_out))
    row = lax.broadcasted_iota(jnp.int32, (SLOTS, 16, SLOT), 1)
    gain_rows = jnp.zeros((SLOTS, 16, SLOT), f32)
    for which in range(2):
        spots = [
            gain_sums[which : which + 1, s * SLOT : s * SLOT + SLOT].reshape(1, 1, SLOT)
            for s in range(SLOTS)
        ]
        gain_rows = jnp.where(row == 8 + which, jnp.concatenate(spots, axis=0), gain_rows)
    for quarter in range(REPS):
        first = dot_nn(normed_turned, wire_in[:, quarter * 512 : quarter * 512 + 512])
        second = dot_nn(mixed_turned, wire_out[:, quarter * 256 : quarter * 256 + 256])
        block = jnp.concatenate(
            [first[:, 0:384], first[:, 384:512] + second[:, 0:128], second[:, 128:256]], axis=1
        ).reshape(SLOTS, SLOT, PACK)
        y, core = (quarter >> 1, quarter & 1)
        low_rows = block[:, 0:ROWS_A, :].astype(bf16)
        high_rows = block[:, ROWS_A:SLOT, :].astype(bf16)
        (one_zero, one_one)[core][y, :, :, :] = low_rows
        target = (two_zero, two_one)[core]
        tail = (block[:, 112:SLOT, 0:SLOT] + gain_rows).astype(bf16)
        for side in range(2):
            slots = slice(side * 4, side * 4 + 4)
            target[side, y * 4 : y * 4 + 4, :, :] = high_rows[slots]
            target[side, y * 4 : y * 4 + 4, 48:64, 0:SLOT] = tail[slots]


def attn_backward(
    batch,
    cotangent,
    middle,
    d_normed_two,
    inputs,
    query_rot,
    key_both,
    value_both,
    probs,
    tables,
    gains,
    places,
    weights,
):
    one = [middle, d_normed_two]
    own = [query_rot, key_both, value_both, probs]
    rest = [gains, *places, *weights]
    outs = [
        ((MB_TOK, WIDE), bf16),
        ((MB_TOK, REPS * 512), bf16),
        ((MB_TOK, REPS * 256), bf16),
        ((8, WIDE), f32),
    ]
    return pl.pallas_call(
        attn_backward_kernel,
        grid=(1,),
        in_specs=[batch_block(batch, WIDE)]
        + [whole_block(array.shape) for array in one]
        + [batch_block(batch, WIDE)]
        + [whole_block(array.shape) for array in own]
        + [batch_block(batch, 128)] * 2
        + [whole_block(array.shape) for array in rest],
        out_specs=[whole_block(out[0]) for out in outs],
        out_shape=[jax.ShapeDtypeStruct(*out) for out in outs],
        scratch_shapes=[
            pltpu.VMEM((MB_TOK, WIDE), bf16),
            pltpu.VMEM((HEADS, MB_TOK, 128), f32),
            pltpu.VMEM((KV_HEADS, MB_TOK, 128), f32),
            pltpu.VMEM((KV_HEADS, MB_TOK, 128), f32),
            pltpu.VMEM((MB_TOK, 1792), bf16),
        ],
        compiler_params=pltpu.CompilerParams(vmem_limit_bytes=VMEM_BYTES),
        cost_estimate=pl.CostEstimate(
            flops=16_000_000_000, bytes_accessed=20_000_000, transcendentals=0
        ),
        name="attn_backward",
    )(cotangent, *one, inputs, *own, *tables, *rest)


def attn_grads(normed, mixed, wires_in, wires_out, gain_parts):
    count = len(normed)
    half = jax.ShapeDtypeStruct((2, SLOTS, ROWS_A, PACK), bf16)
    arrays = (*normed, *mixed, *wires_in, *wires_out, *gain_parts)
    return pl.pallas_call(
        lambda *refs: attn_grads_kernel(*refs, count=count),
        grid=(1,),
        in_specs=[whole_block(array.shape) for array in arrays],
        out_specs=[whole_block(half.shape)] * 4,
        out_shape=[half] * 4,
        compiler_params=pltpu.CompilerParams(vmem_limit_bytes=VMEM_BYTES),
        cost_estimate=pl.CostEstimate(
            flops=8_000_000_000, bytes_accessed=14_000_000, transcendentals=0
        ),
        name="attn_grads",
    )(*arrays)


X_SIDE = ("fsdp", 1)
Y_SIDE = ("rep", 2)
CORE = ("rep", 1)


def swap_with(values, step):
    axis, mask = step
    count = lax.axis_size(axis)
    return lax.ppermute(values, axis, [(i, i ^ mask) for i in range(count)])


def after(values, *done):
    return lax.optimization_barrier((values, done))[0]


def along_z(block):
    return jnp.stack([block] + [swap_with(block, ("fsdp", 2 * k)) for k in range(1, 4)])


def sides_of(side_first):
    return (X_SIDE, Y_SIDE) if side_first else (Y_SIDE, X_SIDE)


def along_first(four, side_first):
    return jnp.concatenate([four, swap_with(four, sides_of(side_first)[0])])


def along_second(eight, side_first):
    return swap_with(eight, sides_of(side_first)[1])


def along_core(eight, across):
    return (eight, swap_with(eight, CORE), across, swap_with(across, CORE))


def added(left, right):
    return (left.astype(f32) + right.astype(f32)).astype(bf16)


class Reduction:
    def __init__(self, kept, sent, side_first):
        self.kept = kept
        self.sent = sent
        self.first, self.second = sides_of(side_first)

    def parts(self):
        return (self.kept, self.sent)

    def over_core(self):
        self.came = swap_with(self.sent, CORE)
        self.out = added(self.kept[1], self.came[1])

    def over_second(self):
        came = swap_with(self.out, self.second)
        kept, before = after((self.kept[0], self.came[0]), came)
        eight = added(kept, before)
        self.out = added(eight[4:8], came[4:8])
        self.four = added(eight[0:4], came[0:4])

    def over_first(self):
        came = swap_with(self.out, self.first)
        self.blocks = [added(self.four[k], came[k]) for k in range(4)]


def over_z(one, two):
    blocks = [jnp.concatenate([one.blocks[k], two.blocks[k]], axis=0) for k in range(4)]
    came = [swap_with(blocks[k], ("fsdp", 2 * k)) for k in range(1, 4)]
    return sum((block.astype(f32) for block in came), blocks[0].astype(f32))


def split_parts(blocks, side_first):
    rows, columns = blocks.shape[2:]
    grid = blocks.reshape(4, 2, 2, 2, rows, columns)
    parts = []
    for second in range(2):
        for core in range(2):
            if side_first:
                part = grid[:, :, second, core].transpose(1, 0, 2, 3)
            else:
                part = grid[:, second, :, core].transpose(1, 0, 2, 3)
            parts.append(part.reshape(SLOTS, rows, columns))
    return parts


def join_parts(kept, sent, side_first):
    rows, columns = kept.shape[2:]
    grid = jnp.stack([kept, sent]).reshape(2, 2, 2, 4, rows, columns)
    grid = grid.transpose(3, 2, 1, 0, 4, 5) if side_first else grid.transpose(3, 1, 2, 0, 4, 5)
    return grid.reshape(SLOTS, REPS, rows, columns)


def attn_block(w_query, w_key, w_value, w_output, attn_gain, mlp_gain):
    matrices = jnp.concatenate([w_query, w_key, w_value, w_output], axis=1)
    gains = jnp.stack([attn_gain, mlp_gain])
    gains = jnp.pad(gains, ((0, SLOT - USED - 2), (0, PACK - USED)))
    return jnp.concatenate([matrices, gains], axis=0)


def down_block(w_down):
    halves = w_down.T.reshape(2, USED, HALF_PACK)
    halves = jnp.concatenate([halves[0], halves[1]], axis=1)
    return jnp.pad(halves, ((0, SLOT - USED), (0, 0)))


def mlp_blocks(w_gate, w_up, w_down):
    taller = ((0, SLOT - USED), (0, 0))
    down = down_block(w_down)
    return (
        jnp.concatenate([jnp.pad(w_gate, taller), down[:ROWS_A]], axis=0),
        jnp.concatenate([jnp.pad(w_up, taller), down[ROWS_A:]], axis=0),
    )


def down_of(block):
    halves = jnp.stack([block[:USED, :HALF_PACK], block[:USED, HALF_PACK:]])
    return halves.reshape(2 * USED, HALF_PACK).T


def whole(shard):
    return lax.all_gather(lax.all_gather(shard, "rep", axis=1, tiled=True), "fsdp", axis=0, tiled=True)


def cut(matrix, eighth, quarter):
    rows, columns = (matrix.shape[0] // SLOTS, matrix.shape[1] // REPS)
    return matrix[
        eighth * rows : eighth * rows + rows, quarter * columns : quarter * columns + columns
    ]


def every_block(make):
    return jnp.stack(
        [jnp.stack([make(e, q) for q in range(REPS)]) for e in range(SLOTS)]
    )


def owned(blocks):
    eighths, quarters, rows, columns = blocks.shape
    matrix = blocks.transpose(0, 2, 1, 3).reshape(eighths * rows, quarters * columns)
    part = lax.psum_scatter(matrix, "fsdp", scatter_dimension=0, tiled=True)
    return lax.psum_scatter(part, "rep", scatter_dimension=1, tiled=True).astype(f32)


def per_device(
    tokens,
    lengths,
    attn_gain,
    w_query,
    w_key,
    w_value,
    w_output,
    mlp_gain,
    w_gate,
    w_up,
    w_down,
    cotangent,
):
    paired = lax.axis_size("fsdp") == SLOTS and lax.axis_size("rep") == REPS
    if paired:
        eighth_here = lax.axis_index("fsdp").astype(jnp.int32)
        quarter_here = lax.axis_index("rep").astype(jnp.int32)
    else:
        eighth_here = jnp.int32(0)
        quarter_here = jnp.int32(0)
    here = jnp.stack([eighth_here, quarter_here])
    places = placing(eighth_here, quarter_here)
    spread = places[0]
    segments, positions = jax.vmap(layout)(lengths)
    tables = rope_tables(positions.reshape(-1))
    inputs = jnp.dot(tokens, spread[:D], preferred_element_type=f32).astype(bf16)
    upstream = jnp.dot(cotangent, spread[:D], preferred_element_type=f32).astype(bf16)
    upstream_turned = upstream.T
    batches = range(tokens.shape[0] // MB_TOK)
    forward_inputs = [inputs for _ in batches]

    if paired:
        attn_pack = attn_block(w_query, w_key, w_value, w_output, attn_gain, mlp_gain)
        gate_pack, up_pack = mlp_blocks(w_gate, w_up, w_down)
        attn_four = along_z(attn_pack)
        gate_pack = after(gate_pack, attn_four)
        gate_four = along_z(gate_pack)
        up_pack = after(up_pack, gate_four)
        up_four = along_z(up_pack)
        one = along_first(attn_four[:, :ROWS_A], True)
        two = along_first(attn_four[:, ROWS_A:], False)
        one_across, two_across = (along_second(one, True), along_second(two, False))
        attn_parts = (*along_core(one, one_across), *along_core(two, two_across))
        gate_four = after(gate_four, one_across, two_across)
        gate_one = along_first(gate_four[:, :ROWS_M], True)
        gate_two = along_first(gate_four[:, ROWS_M:], False)
        up_one = along_first(up_four[:, :ROWS_M], True)
        up_two = along_first(up_four[:, ROWS_M:], False)
        forward_inputs[0] = after(inputs, gate_one, gate_two, up_four)
        forward_inputs[-1] = after(inputs, up_one, up_two)
        gate_across = (along_second(gate_one, True), along_second(gate_two, False))
        up_across = (along_second(up_one, True), along_second(up_two, False))
    else:
        gain_one, gain_two = (
            lax.all_gather(attn_gain, "fsdp", axis=0, tiled=True).reshape(SLOTS, USED),
            lax.all_gather(mlp_gain, "fsdp", axis=0, tiled=True).reshape(SLOTS, USED),
        )
        mats = [whole(w) for w in (w_query, w_key, w_value, w_output, w_gate, w_up, w_down)]
        attn_blocks = every_block(
            lambda e, q: attn_block(*[cut(m, e, q) for m in mats[:4]], gain_one[e], gain_two[e])
        )
        attn_parts = (
            *split_parts(attn_blocks[:, :, :ROWS_A], True),
            *split_parts(attn_blocks[:, :, ROWS_A:], False),
        )
        mlp_each = [
            [
                mlp_blocks(cut(mats[4], e, q), cut(mats[5], e, q), cut(mats[6], e, q))
                for q in range(REPS)
            ]
            for e in range(SLOTS)
        ]
        mlp_parts = []
        for group in range(2):
            blocks = every_block(lambda e, q: mlp_each[e][q][group])
            mlp_parts += split_parts(blocks[:, :, :ROWS_M], True)
            mlp_parts += split_parts(blocks[:, :, ROWS_M:], False)

    *weights, gains = attn_weights(places[1:], attn_parts[:4], attn_parts[4:])
    made = [
        attn_forward(batch, forward_inputs[batch], spread, weights, gains, tables, segments)
        for batch in batches
    ]
    normed, query_rot, key_both, value_both, probs, mixed, middle, normed_two = zip(*made)
    if paired:
        gate_across = after(gate_across, normed_two[0])
        up_across = after(up_across, normed_two[-1])
        mlp_parts = (
            *along_core(gate_one, gate_across[0]),
            *along_core(gate_two, gate_across[1]),
            *along_core(up_one, up_across[0]),
            *along_core(up_two, up_across[1]),
        )
    (hidden, d_gate, d_up, w_down_all), grads = mlp(
        here, normed_two, upstream, upstream_turned, mlp_parts
    )
    gate_sums = (Reduction(grads[0], grads[1], True), Reduction(grads[2], grads[3], False))
    up_sums = (Reduction(grads[4], grads[5], True), Reduction(grads[6], grads[7], False))
    mlp_out, d_normed_two = mlp_outputs(hidden, d_gate, d_up, w_down_all, mlp_parts)
    d_normed_two = list(d_normed_two)
    if paired:
        for part in gate_sums + up_sums:
            part.over_core()
        d_normed_two[0] = after(d_normed_two[0], gate_sums[0].out, gate_sums[1].out)
    back = []
    for batch in batches:
        back.append(
            attn_backward(
                batch,
                upstream,
                middle[batch],
                d_normed_two[batch],
                inputs,
                query_rot[batch],
                key_both[batch],
                value_both[batch],
                probs[batch],
                tables,
                gains,
                places,
                weights,
            )
        )
        if paired and batch == 0:
            for part in gate_sums:
                part.over_second()
            for part in up_sums:
                part.out = after(part.out, gate_sums[0].out, gate_sums[1].out)
            d_normed_two[-1] = after(d_normed_two[-1], up_sums[0].out, up_sums[1].out)
    token_rows, wires_in, wires_out, gain_parts = zip(*back)
    if paired:
        for part in up_sums:
            part.over_second()
        for part in gate_sums:
            part.over_first()
        wires_in = after(wires_in, up_sums[0].out, up_sums[1].out)
    one_kept, one_sent, two_kept, two_sent = attn_grads(
        normed, mixed, wires_in, wires_out, gain_parts
    )
    output_rows = jnp.concatenate(
        [(middle[batch] + mlp_out[batch]).astype(bf16) for batch in batches], axis=0
    )
    output = jnp.dot(output_rows, spread[:D].T, preferred_element_type=f32).astype(bf16)
    token_grad = jnp.dot(
        jnp.concatenate(token_rows, axis=0), spread[:D].T, preferred_element_type=f32
    ).astype(bf16)
    if paired:
        one = Reduction(one_kept, one_sent, True)
        two = Reduction(two_kept, two_sent, False)
        one.over_core()
        two.over_core()
        gate_sum = over_z(*gate_sums)
        for part in up_sums:
            part.over_first()
        one.over_second()
        two.over_second()
        up_sum = over_z(*up_sums)
        one.over_first()
        two.over_first()
        attn_sum = over_z(one, two)
        gain_sums = (attn_sum[USED, :USED], attn_sum[USED + 1, :USED])
        attn_sum = attn_sum[:USED]
        grads = [
            attn_sum[:, 0:240],
            attn_sum[:, 240:320],
            attn_sum[:, 320:400],
            attn_sum[:, 400:640],
            gate_sum[:USED],
            up_sum[:USED],
            down_of(jnp.concatenate([gate_sum[SLOT:], up_sum[SLOT:]], axis=0)),
        ]
    else:
        attn_blocks = jnp.concatenate(
            [join_parts(one_kept, one_sent, True), join_parts(two_kept, two_sent, False)], axis=2
        )
        gain_sums = tuple(
            lax.psum(
                lax.psum_scatter(
                    attn_blocks[:, 0, USED + which, :USED].astype(f32).reshape(D),
                    "fsdp",
                    scatter_dimension=0,
                    tiled=True,
                ),
                "rep",
            )
            for which in range(2)
        )
        attn_blocks = attn_blocks[:, :, :USED]
        gate_blocks, up_blocks = [
            jnp.concatenate(
                [join_parts(*sums[0].parts(), True), join_parts(*sums[1].parts(), False)], axis=2
            )
            for sums in (gate_sums, up_sums)
        ]
        down_blocks = jnp.concatenate([gate_blocks[:, :, SLOT:], up_blocks[:, :, SLOT:]], axis=2)
        grads = [
            owned(attn_blocks[..., 0:240]),
            owned(attn_blocks[..., 240:320]),
            owned(attn_blocks[..., 320:400]),
            owned(attn_blocks[..., 400:640]),
            owned(gate_blocks[:, :, :USED]),
            owned(up_blocks[:, :, :USED]),
            owned(jax.vmap(jax.vmap(down_of))(down_blocks)),
        ]
    return (
        output,
        token_grad,
        gain_sums[0],
        grads[0],
        grads[1],
        grads[2],
        grads[3],
        gain_sums[1],
        grads[4],
        grads[5],
        grads[6],
    )


def solution(mesh):
    placed = (
        P(("fsdp", "rep"), None),
        P(("fsdp", "rep"), None),
        P("fsdp"),
        P("fsdp", "rep"),
        P("fsdp", "rep"),
        P("fsdp", "rep"),
        P("fsdp", "rep"),
        P("fsdp"),
        P("fsdp", "rep"),
        P("fsdp", "rep"),
        P("fsdp", "rep"),
        P(("fsdp", "rep"), None),
    )
    return jax.shard_map(
        per_device,
        mesh=mesh,
        in_specs=placed,
        out_specs=(
            P(("fsdp", "rep"), None),
            P(("fsdp", "rep"), None),
            P("fsdp"),
            P("fsdp", "rep"),
            P("fsdp", "rep"),
            P("fsdp", "rep"),
            P("fsdp", "rep"),
            P("fsdp"),
            P("fsdp", "rep"),
            P("fsdp", "rep"),
            P("fsdp", "rep"),
        ),
        check_vma=False,
    )
```

```python
import jax
import jax.numpy as jnp
from jax import lax
from jax.experimental import pallas as pl
from jax.experimental.pallas import tpu as pltpu
from jax.sharding import PartitionSpec as P

D = 960
FF = 2560
HEADS = 15
KV_HEADS = 5
HEAD = 64
MB_TOK = 384
SEGS = 3
GROUP = 3
QW = 960
KVW = 320

SLOTS = 8
REPS = 4
USED = 120
SLOT = 128
WIDE = SLOTS * SLOT
PACK = 640
HALF_PACK = 320
ROWS_A = 64
ROWS_M = 96
REST = SLOT - ROWS_M
VMEM_BYTES = 60 * 1024 * 1024

norm_epsilon = 1e-05
rope_base = 100000.0
masked_value = -1e30

f32 = jnp.float32
bf16 = jnp.bfloat16


def layout(length_row):
    starts = jnp.cumsum(length_row) - length_row
    places = jnp.arange(MB_TOK, dtype=jnp.int32)
    inside = (
        (places[:, None] >= starts[None, :]) & (places[:, None] < (starts + length_row)[None, :])
    ).astype(jnp.int32)
    segment = jnp.sum(inside * jnp.arange(SEGS, dtype=jnp.int32)[None, :], axis=1)
    position = places - jnp.sum(inside * starts[None, :], axis=1)
    return (segment, position)


def rope_tables(position):
    half_width = HEAD // 2
    exponent = jnp.arange(half_width, dtype=f32) * (2.0 / HEAD)
    inverse = jnp.power(rope_base, -exponent)
    angles = position.astype(f32)[:, None] * inverse
    cosines, sines = (jnp.cos(angles), jnp.sin(angles))
    return (
        jnp.concatenate([cosines] * 4, axis=1),
        jnp.concatenate([-sines, sines, -sines, sines], axis=1),
    )


def slot_of(eighth):
    return (eighth & 1) * 4 + (eighth >> 1)


def eighth_of(slot):
    return (slot & 3) * 2 + (slot >> 2)


def feature_lanes(eighth_here):
    lanes = jnp.arange(WIDE, dtype=jnp.int32)
    eighth = eighth_of(lanes // SLOT) ^ eighth_here
    return jnp.where(lanes % SLOT < USED, eighth * USED + lanes % SLOT, -1)


def spreading(eighth_here):
    features = jnp.arange(D, dtype=jnp.int32)
    return (features[:, None] == feature_lanes(eighth_here)[None, :]).astype(bf16)


def dot_nn(left, right):
    return lax.dot_general(left, right, (((1,), (0,)), ((), ())), preferred_element_type=f32)


def dot_nt(left, right):
    return lax.dot_general(left, right, (((1,), (1,)), ((), ())), preferred_element_type=f32)


def dot_tn(left, right):
    return lax.dot_general(left, right, (((0,), (0,)), ((), ())), preferred_element_type=f32)


def lane_index(shape):
    return lax.broadcasted_iota(jnp.int32, shape, len(shape) - 1)


def swapped(values):
    first = (lane_index(values.shape) & 63) < 32
    return jnp.where(first, pltpu.roll(values, 96, 1), pltpu.roll(values, 32, 1))


def turned(values, cosines, sines):
    return values * cosines + swapped(values) * sines


def both_halves(values, odd):
    low = lane_index(values.shape) < 64
    moved = pltpu.roll(values, 64, 1)
    return jnp.where(low, moved, values) if odd else jnp.where(low, values, moved)


def only_half(values, odd):
    low = lane_index(values.shape) < 64
    return jnp.where(low != bool(odd), values, jnp.zeros_like(values))


def laid(pieces, rows, tiles):
    lane = lane_index((rows, 128))
    made = [jnp.zeros((rows, 128), f32)] * tiles
    for source, start, target, width in pieces:
        shifted = {}
        done = 0
        while done < width:
            from_tile, from_lane = divmod(start + done, 128)
            to_tile, to_lane = divmod(target + done, 128)
            now = min(width - done, 128 - from_lane, 128 - to_lane)
            if from_tile not in shifted:
                values = source[from_tile]
                turn = (to_lane - from_lane) % 128
                shifted[from_tile] = pltpu.roll(values, turn, 1) if turn else values
            inside = (lane >= to_lane) & (lane < to_lane + now)
            made[to_tile] = jnp.where(inside, shifted[from_tile], made[to_tile])
            done += now
    return made


def tiles_of(values):
    return [values[:, t : t + 128] for t in range(0, values.shape[1], 128)]


def joined(tiles):
    return jnp.concatenate(tiles, axis=1)


def gain_row(attn_ref, which):
    rows = [attn_ref[0, s, 112:128, 0:SLOT].astype(f32)[8 + which : 9 + which] for s in range(SLOTS)]
    return jnp.concatenate(rows, axis=1)


def views(parts):
    one, two, one_across, two_across, near, far = parts
    return (
        [one, near.at[0:SLOTS], one_across, far.at[0:SLOTS]],
        [two, near.at[SLOTS : 2 * SLOTS], two_across, far.at[SLOTS : 2 * SLOTS]],
    )


def attn_fetches(parts, attn_all, sems):
    copies = []
    firsts, seconds = views(parts)
    for quarter, source in enumerate(firsts):
        copies.append((source, attn_all.at[quarter, :, 0:ROWS_A, :]))
    for place, source in enumerate(seconds):
        side, core = (place >> 1, place & 1)
        for y in range(2):
            copies.append(
                (
                    source.at[y * 4 : y * 4 + 4],
                    attn_all.at[y * 2 + core, side * 4 : side * 4 + 4, ROWS_A : 2 * ROWS_A, :],
                )
            )
    return [
        pltpu.make_async_copy(source, target, sems.at[n])
        for n, (source, target) in enumerate(copies)
    ]


def block_columns(attn_all, quarter, low, high):
    return attn_all[quarter, :, :, low:high].reshape(WIDE, high - low)


def probs_at(part):
    return (0, 128, 384)[part]


def attn_forward_kernel(
    here,
    inputs,
    cosines,
    sines,
    segment_rows,
    segment_columns,
    *refs,
):
    parts = refs[:6]
    (
        normed_out,
        query_out,
        key_out,
        value_out,
        probs_out,
        mixed_out,
        middle_out,
        normed_two_out,
        attn_all,
        wire,
        heads_out,
        mixed_slots,
        out_slots,
        bias,
        sems,
    ) = refs[6:]
    eighth_here, quarter_here = (here[0], here[1])
    fetches = attn_fetches(parts, attn_all, sems)
    for copy in fetches:
        copy.start()
    values = inputs[...].astype(f32)
    scale = lax.rsqrt(jnp.sum(values * values, axis=1, keepdims=True) * (1.0 / D) + norm_epsilon)
    for copy in fetches:
        copy.wait()
    normed = (values * scale * gain_row(attn_all, 0)).astype(bf16)
    normed_out[...] = normed
    cosine, sine = (cosines[...], sines[...])
    for quarter in range(REPS):
        wire[quarter] = dot_nn(normed, block_columns(attn_all, quarter, 0, 512))
    sources = [
        [wire[r ^ quarter_here, :, t * 128 : t * 128 + 128] for t in range(4)] for r in range(REPS)
    ]
    query_tiles = laid([(sources[r], 0, 240 * r, 240) for r in range(REPS)], MB_TOK, 8)
    for c in range(8):
        query_out[:, c * 128 : c * 128 + 128] = turned(query_tiles[c], cosine, sine).astype(bf16)
    key_tiles = laid([(sources[r], 240, 80 * r, 80) for r in range(REPS)], MB_TOK, 3)
    value_tiles = laid([(sources[r], 320, 80 * r, 80) for r in range(REPS)], MB_TOK, 3)
    for c in range(3):
        key_part = turned(key_tiles[c], cosine, sine)
        for odd in range(2 if c < 2 else 1):
            at = slice((2 * c + odd) * 128, (2 * c + odd) * 128 + 128)
            key_out[:, at] = both_halves(key_part, odd).astype(bf16)
            value_out[:, at] = both_halves(value_tiles[c], odd).astype(bf16)

    query_place = lax.broadcasted_iota(jnp.int32, (MB_TOK, MB_TOK), 0)
    key_place = lax.broadcasted_iota(jnp.int32, (MB_TOK, MB_TOK), 1)
    seen = (segment_rows[...] == segment_columns[0]) & (key_place <= query_place)
    bias[...] = jnp.where(seen, 0.0, masked_value)
    for j in range(KV_HEADS):
        at = slice(j * 128, j * 128 + 128)
        for part in range(3):
            keys = 128 * (part + 1)
            rows = slice(part * 128, part * 128 + 128)
            queries = jnp.concatenate(
                [
                    only_half(query_out[rows, (h // 2) * 128 : (h // 2) * 128 + 128], h % 2)
                    for h in range(3 * j, 3 * j + 3)
                ],
                axis=0,
            )
            scores = dot_nt(queries, key_out[0:keys, at]) * HEAD**-0.5
            hidden_part = bias[rows, 0:keys]
            scores = scores + jnp.concatenate([hidden_part] * GROUP, axis=0)
            peak = jnp.max(scores, axis=1, keepdims=True)
            weights = jnp.exp(scores - peak)
            total = jnp.sum(weights, axis=1, keepdims=True)
            probs = (weights * (1.0 / total)).astype(bf16)
            probs_out[j, :, probs_at(part) : probs_at(part) + keys] = probs
            gathered = dot_nn(probs, value_out[0:keys, at])
            for g in range(GROUP):
                heads_out[3 * j + g, rows, :] = gathered[g * 128 : g * 128 + 128]
    low = lane_index((MB_TOK, 128)) < 64
    head_tiles = [
        jnp.where(
            low,
            heads_out[2 * c],
            heads_out[2 * c + 1] if 2 * c + 1 < HEADS else jnp.zeros((MB_TOK, 128), f32),
        )
        for c in range(8)
    ]
    for eighth in range(SLOTS):
        (slot_tile,) = laid([(head_tiles, USED * eighth, 0, USED)], MB_TOK, 1)
        mixed_slots[slot_of(eighth ^ eighth_here)] = slot_tile.astype(bf16)
    mixed = joined([mixed_slots[s] for s in range(SLOTS)])
    mixed_out[...] = mixed
    for quarter in range(REPS):
        part = tiles_of(dot_nn(mixed, block_columns(attn_all, quarter, 384, 640)))
        for which in range(2):
            eighth = (quarter ^ quarter_here) * 2 + which
            (slot_tile,) = laid([(part, 16 + USED * which, 0, USED)], MB_TOK, 1)
            out_slots[slot_of(eighth ^ eighth_here)] = slot_tile
    middle = values + joined([out_slots[s] for s in range(SLOTS)])
    middle_out[...] = middle
    scale_two = lax.rsqrt(
        jnp.sum(middle * middle, axis=1, keepdims=True) * (1.0 / D) + norm_epsilon
    )
    normed_two_out[...] = (middle * scale_two * gain_row(attn_all, 1)).astype(bf16)


def whole_block(shape):
    return pl.BlockSpec(
        shape, lambda *ids: (0,) * len(shape), pipeline_mode=pl.Buffered(buffer_count=1)
    )


def anywhere():
    return pl.BlockSpec(memory_space=pl.ANY)


def batch_block(batch, columns):
    return pl.BlockSpec((MB_TOK, columns), lambda i: (batch, 0))


def attn_scratch():
    return [
        pltpu.VMEM((REPS, SLOTS, SLOT, PACK), bf16),
        pltpu.VMEM((REPS, MB_TOK, 512), f32),
        pltpu.VMEM((HEADS, MB_TOK, 128), f32),
    ]


def in_scalars():
    return pl.BlockSpec(memory_space=pltpu.SMEM)


def attn_forward(batch, here, inputs, parts, tables, segments):
    count = inputs.shape[0] // MB_TOK
    outs = [
        ((MB_TOK, WIDE), bf16),
        ((MB_TOK, WIDE), bf16),
        ((MB_TOK, PACK), bf16),
        ((MB_TOK, PACK), bf16),
        ((KV_HEADS, MB_TOK, 768), bf16),
        ((MB_TOK, WIDE), bf16),
        ((MB_TOK, WIDE), f32),
        ((MB_TOK, WIDE), bf16),
    ]
    return pl.pallas_call(
        attn_forward_kernel,
        grid=(1,),
        in_specs=[
            in_scalars(),
            batch_block(batch, WIDE),
            batch_block(batch, 128),
            batch_block(batch, 128),
            batch_block(batch, 1),
            pl.BlockSpec((1, 1, MB_TOK), lambda i: (batch, 0, 0)),
        ]
        + [anywhere()] * 6,
        out_specs=[whole_block(out[0]) for out in outs],
        out_shape=[jax.ShapeDtypeStruct(*out) for out in outs],
        scratch_shapes=attn_scratch()
        + [
            pltpu.VMEM((SLOTS, MB_TOK, SLOT), bf16),
            pltpu.VMEM((SLOTS, MB_TOK, SLOT), f32),
            pltpu.VMEM((MB_TOK, MB_TOK), f32),
            pltpu.SemaphoreType.DMA((12,)),
        ],
        compiler_params=pltpu.CompilerParams(vmem_limit_bytes=VMEM_BYTES),
        cost_estimate=pl.CostEstimate(
            flops=8_000_000_000, bytes_accessed=16_000_000, transcendentals=2_000_000
        ),
        name="attn_forward",
    )(
        here,
        inputs,
        *tables,
        segments.reshape(-1, 1),
        segments.reshape(count, 1, MB_TOK),
        *parts,
    )


def left_right(left, right):
    first = lane_index(left.shape) < HALF_PACK
    left, right = (left.astype(f32), right.astype(f32))
    return (
        jnp.where(first, left, pltpu.roll(right, HALF_PACK, 1)).astype(bf16),
        jnp.where(first, pltpu.roll(left, HALF_PACK, 1), right).astype(bf16),
    )


def pair_fetches(parts, at, w_gate, w_up, sems):
    found = []
    for group, target in enumerate((w_gate, w_up)):
        firsts, seconds = views(parts[6 * group : 6 * group + 6])
        for core in range(2):
            lanes = slice(core * PACK, core * PACK + PACK)
            found.append((firsts[at * 2 + core], target.at[:, 0:ROWS_M, lanes]))
            for side in range(2):
                found.append(
                    (
                        seconds[side * 2 + core].at[at * 4 : at * 4 + 4, 0:REST, :],
                        target.at[side * 4 : side * 4 + 4, ROWS_M:SLOT, lanes],
                    )
                )
    return [
        pltpu.make_async_copy(source, target, sems.at[n])
        for n, (source, target) in enumerate(found)
    ]


def mlp_kernel(here, *refs, count):
    normed = refs[:count]
    cotangent, cotangent_turned = refs[count : count + 2]
    parts = refs[count + 2 : count + 14]
    hidden, d_gate, d_up, down_out, kept, sent = refs[count + 14 : count + 20]
    (
        w_gate,
        w_up,
        down_raw,
        normed_turned,
        grad_gate,
        grad_up,
        grad_down,
        down_made,
        sem_pair,
        sem_down,
        sem_out,
    ) = refs[count + 20 :]
    step = pl.program_id(0)
    eighth_here, quarter_here = (here[0], here[1])
    side_here = eighth_here & 1

    def plane_of(at, core):
        return ((2 * at + core) ^ quarter_here) ^ (eighth_here >> 1)

    def fetches(at):
        found = []
        for core in range(2):
            for side in range(2):
                for quarter in range(REPS):
                    y, inner = (quarter >> 1, quarter & 1)
                    for group in range(2):
                        seconds = views(parts[6 * group : 6 * group + 6])[1]
                        found.append(
                            (
                                seconds[side * 2 + inner].at[
                                    y * 4 + plane_of(at, core), REST:ROWS_M
                                ],
                                down_raw.at[
                                    core, side, quarter, group * ROWS_A : group * ROWS_A + ROWS_A
                                ],
                            )
                        )
        return pair_fetches(parts, at, w_gate, w_up, sem_pair) + [
            pltpu.make_async_copy(source, target, sem_down.at[n])
            for n, (source, target) in enumerate(found)
        ]

    def results(at):
        found = []
        for group, source in enumerate((grad_gate, grad_up)):
            firsts = (kept.at[2 * group], sent.at[2 * group])
            seconds = (kept.at[2 * group + 1], sent.at[2 * group + 1])
            for core in range(2):
                found.append((source.at[core, :, 0:ROWS_M], firsts[core].at[at]))
                for side in range(2):
                    found.append(
                        (
                            source.at[core, side * 4 : side * 4 + 4, ROWS_M:SLOT],
                            seconds[core].at[side, at * 4 : at * 4 + 4, 0:REST],
                        )
                    )
                    for quarter in range(REPS):
                        y, inner = (quarter >> 1, quarter & 1)
                        found.append(
                            (
                                down_made.at[
                                    core, side, quarter, group * ROWS_A : group * ROWS_A + ROWS_A
                                ],
                                seconds[inner].at[
                                    side, y * 4 + plane_of(at, core), REST:ROWS_M
                                ],
                            )
                        )
        return [
            pltpu.make_async_copy(source, target, sem_out.at[n])
            for n, (source, target) in enumerate(found)
        ]

    def rows_of(quarter, which):
        eighth = (quarter ^ quarter_here) * 2 + which
        return pl.multiple_of(slot_of(eighth ^ eighth_here) * SLOT, SLOT)

    @pl.when(step == 0)
    def _():
        for copy in fetches(0):
            copy.start()
        for batch in range(count):
            normed_turned[:, batch * MB_TOK : batch * MB_TOK + MB_TOK] = normed[batch][...].T
        for copy in fetches(0):
            copy.wait()

    @pl.when(step == 1)
    def _():
        for copy in fetches(1):
            copy.wait()

    for core in range(2):
        lanes = slice(core * PACK, core * PACK + PACK)
        for quarter in range(REPS):
            lefts, rights = left_right(
                down_raw[core, side_here, quarter], down_raw[core, 1 - side_here, quarter]
            )
            down_out[0, pl.ds(rows_of(quarter, 0), SLOT), lanes] = lefts
            down_out[0, pl.ds(rows_of(quarter, 1), SLOT), lanes] = rights

    gate_weights = w_gate[...].reshape(WIDE, 2 * PACK)
    up_weights = w_up[...].reshape(WIDE, 2 * PACK)
    for batch in range(count):
        rows = slice(batch * MB_TOK, batch * MB_TOK + MB_TOK)
        gate = dot_nn(normed[batch][...], gate_weights)
        up = dot_nn(normed[batch][...], up_weights)
        d_hidden = dot_nn(cotangent[rows, :], down_out[0])
        sigmoid = 1.0 / (1.0 + jnp.exp(-gate))
        silu = gate * sigmoid
        hidden[0, rows, :] = (silu * up).astype(bf16)
        d_gate[0, rows, :] = (d_hidden * up * sigmoid * (1.0 + gate * (1.0 - sigmoid))).astype(bf16)
        d_up[0, rows, :] = (d_hidden * silu).astype(bf16)

    @pl.when(step == 0)
    def _():
        for copy in fetches(1):
            copy.start()

    @pl.when(step == 1)
    def _():
        for copy in results(0):
            copy.wait()

    for half in range(2):
        rows = slice(half * 512, half * 512 + 512)
        four = slice(half * 4, half * 4 + 4)
        gate_part = dot_nn(normed_turned[rows, :], d_gate[0]).astype(bf16)
        up_part = dot_nn(normed_turned[rows, :], d_up[0]).astype(bf16)
        for core in range(2):
            lanes = slice(core * PACK, core * PACK + PACK)
            grad_gate[core, four] = gate_part[:, lanes].reshape(4, SLOT, PACK)
            grad_up[core, four] = up_part[:, lanes].reshape(4, SLOT, PACK)
        grad_down[rows, :] = dot_nn(cotangent_turned[rows, :], hidden[0])
    for core in range(2):
        lanes = slice(core * PACK, core * PACK + PACK)
        for quarter in range(REPS):
            lefts, rights = left_right(
                grad_down[pl.ds(rows_of(quarter, 0), SLOT), lanes],
                grad_down[pl.ds(rows_of(quarter, 1), SLOT), lanes],
            )
            down_made[core, side_here, quarter] = lefts
            down_made[core, 1 - side_here, quarter] = rights
    for at in range(2):

        @pl.when(step == at)
        def _():
            for copy in results(at):
                copy.start()

    @pl.when(step == 1)
    def _():
        for copy in results(1):
            copy.wait()


def chunk_block(rows, columns):
    return pl.BlockSpec((1, rows, columns), lambda i: (i, 0, 0))


def mlp(here, normed, cotangent, cotangent_turned, parts):
    count = len(normed)
    tokens = cotangent.shape[0]
    rows = jax.ShapeDtypeStruct((2, tokens, 2 * PACK), bf16)
    part = jax.ShapeDtypeStruct((4, 2, SLOTS, ROWS_M, PACK), bf16)
    return pl.pallas_call(
        lambda *refs: mlp_kernel(*refs, count=count),
        grid=(2,),
        in_specs=[pl.BlockSpec(memory_space=pltpu.SMEM)]
        + [whole_block((MB_TOK, WIDE))] * count
        + [whole_block((tokens, WIDE)), whole_block((WIDE, tokens))]
        + [anywhere()] * 12,
        out_specs=[chunk_block(tokens, 2 * PACK)] * 3
        + [chunk_block(WIDE, 2 * PACK)]
        + [anywhere()] * 2,
        out_shape=[rows, rows, rows, jax.ShapeDtypeStruct((2, WIDE, 2 * PACK), bf16), part, part],
        scratch_shapes=[
            pltpu.VMEM((SLOTS, SLOT, 2 * PACK), bf16),
            pltpu.VMEM((SLOTS, SLOT, 2 * PACK), bf16),
            pltpu.VMEM((2, 2, REPS, SLOT, PACK), bf16),
            pltpu.VMEM((WIDE, tokens), bf16),
            pltpu.VMEM((2, SLOTS, SLOT, PACK), bf16),
            pltpu.VMEM((2, SLOTS, SLOT, PACK), bf16),
            pltpu.VMEM((WIDE, 2 * PACK), f32),
            pltpu.VMEM((2, 2, REPS, SLOT, PACK), bf16),
            pltpu.SemaphoreType.DMA((12,)),
            pltpu.SemaphoreType.DMA((32,)),
            pltpu.SemaphoreType.DMA((44,)),
        ],
        compiler_params=pltpu.CompilerParams(vmem_limit_bytes=VMEM_BYTES),
        cost_estimate=pl.CostEstimate(
            flops=30_000_000_000, bytes_accessed=50_000_000, transcendentals=2_000_000
        ),
        name="mlp",
    )(here, *normed, cotangent, cotangent_turned, *parts)


def mlp_outputs_kernel(hidden, d_gate, d_up, w_down, *refs, count):
    parts = refs[:12]
    outs, d_normed = (refs[12 : 12 + count], refs[12 + count : 12 + 2 * count])
    w_gate, w_up, sem_pair = refs[12 + 2 * count :]
    step = pl.program_id(0)

    def fetches(at):
        return pair_fetches(parts, at, w_gate.at[at], w_up.at[at], sem_pair.at[at])

    @pl.when(step == 0)
    def _():
        for at in range(2):
            for copy in fetches(at):
                copy.start()

    for at in range(2):

        @pl.when(step == at)
        def _():
            for copy in fetches(at):
                copy.wait()
            gate_weights = w_gate[at].reshape(WIDE, 2 * PACK)
            up_weights = w_up[at].reshape(WIDE, 2 * PACK)
            for batch in range(count):
                rows = slice(batch * MB_TOK, batch * MB_TOK + MB_TOK)
                out_part = dot_nt(hidden[0, rows, :], w_down[0])
                normed_part = dot_nt(d_gate[0, rows, :], gate_weights) + dot_nt(
                    d_up[0, rows, :], up_weights
                )
                if at == 0:
                    outs[batch][...] = out_part
                    d_normed[batch][...] = normed_part
                else:
                    outs[batch][...] += out_part
                    d_normed[batch][...] += normed_part


def mlp_outputs(hidden, d_gate, d_up, w_down, parts):
    tokens = hidden.shape[1]
    count = tokens // MB_TOK
    outs = pl.pallas_call(
        lambda *refs: mlp_outputs_kernel(*refs, count=count),
        grid=(2,),
        in_specs=[chunk_block(tokens, 2 * PACK)] * 3
        + [chunk_block(WIDE, 2 * PACK)]
        + [anywhere()] * 12,
        out_specs=[whole_block((MB_TOK, WIDE))] * (2 * count),
        out_shape=[jax.ShapeDtypeStruct((MB_TOK, WIDE), f32)] * (2 * count),
        scratch_shapes=[
            pltpu.VMEM((2, SLOTS, SLOT, 2 * PACK), bf16),
            pltpu.VMEM((2, SLOTS, SLOT, 2 * PACK), bf16),
            pltpu.SemaphoreType.DMA((2, 12)),
        ],
        compiler_params=pltpu.CompilerParams(vmem_limit_bytes=VMEM_BYTES),
        cost_estimate=pl.CostEstimate(
            flops=15_000_000_000, bytes_accessed=35_000_000, transcendentals=0
        ),
        name="mlp_outputs",
    )(hidden, d_gate, d_up, w_down, *parts)
    return (outs[:count], outs[count:])


def attn_backward_kernel(
    here,
    cotangent,
    middle,
    d_normed_two,
    inputs,
    query_rot,
    key_both,
    value_both,
    probs_in,
    cosines,
    sines,
    *refs,
):
    parts = refs[:6]
    (
        token_grad,
        wire_in,
        wire_out,
        gain_sums,
        attn_all,
        slots,
        head_parts,
        key_parts,
        value_parts,
        d_mixed_heads,
        sems,
    ) = refs[6:]
    eighth_here, quarter_here = (here[0], here[1])
    fetches = attn_fetches(parts, attn_all, sems)
    for copy in fetches:
        copy.start()
    mid = middle[...]
    upstream = d_normed_two[...]
    scale_two = lax.rsqrt(jnp.sum(mid * mid, axis=1, keepdims=True) * (1.0 / D) + norm_epsilon)
    term_two = jnp.sum(upstream * mid * scale_two, axis=0, keepdims=True)
    for copy in fetches:
        copy.wait()
    gain_one, gain_two = (gain_row(attn_all, 0), gain_row(attn_all, 1))
    weighted = upstream * gain_two
    inner = jnp.sum(weighted * mid, axis=1, keepdims=True) * (1.0 / D)
    d_middle = (
        cotangent[...].astype(f32)
        + scale_two * weighted
        - mid * scale_two * scale_two * scale_two * inner
    )
    for s in range(SLOTS):
        slots[s] = d_middle[:, s * SLOT : s * SLOT + SLOT]

    def slot_at(eighth):
        return slots[slot_of(eighth ^ eighth_here)]

    for quarter in range(REPS):
        first = (quarter ^ quarter_here) * 2
        tiles = laid(
            [([slot_at(first)], 0, 16, USED), ([slot_at(first + 1)], 0, 16 + USED, USED)], MB_TOK, 2
        )
        wire_out[:, quarter * 256 : quarter * 256 + 256] = joined(tiles).astype(bf16)
    output_columns = joined([block_columns(attn_all, q, 384, 640) for q in range(REPS)])
    d_mixed = dot_nt(wire_out[...], output_columns)
    for s in range(SLOTS):
        slots[s] = d_mixed[:, s * SLOT : s * SLOT + SLOT]
    tiles = laid([([slot_at(e)], 0, USED * e, USED) for e in range(SLOTS)], MB_TOK, 8)
    for c in range(8):
        d_mixed_heads[:, c * 128 : c * 128 + 128] = tiles[c].astype(bf16)
    for j in range(KV_HEADS):
        at = slice(j * 128, j * 128 + 128)
        for part in (2, 1, 0):
            keys = 128 * (part + 1)
            rows = slice(part * 128, part * 128 + 128)

            def three(ref):
                return jnp.concatenate(
                    [
                        only_half(ref[rows, (h // 2) * 128 : (h // 2) * 128 + 128], h % 2)
                        for h in range(3 * j, 3 * j + 3)
                    ],
                    axis=0,
                )

            queries = three(query_rot)
            d_mix = three(d_mixed_heads)
            probs = probs_in[j, :, probs_at(part) : probs_at(part) + keys]
            probs_f = probs.astype(f32)
            d_probs = dot_nt(d_mix, value_both[0:keys, at])
            product = probs_f * d_probs
            d_scores = product - probs_f * jnp.sum(product, axis=1, keepdims=True)
            d_scores = d_scores.astype(bf16)
            d_query = dot_nn(d_scores, key_both[0:keys, at])
            for g in range(GROUP):
                head_parts[3 * j + g, rows, :] = d_query[g * 128 : g * 128 + 128]
            d_key = dot_tn(d_scores, queries)
            d_value = dot_tn(probs, d_mix)
            if part == 2:
                key_parts[j] = d_key
                value_parts[j] = d_value
            else:
                key_parts[j, 0:keys, :] += d_key
                value_parts[j, 0:keys, :] += d_value

    low = lane_index((MB_TOK, 128)) < 64
    cosine, sine = (cosines[...], sines[...])
    empty = jnp.zeros((MB_TOK, 128), f32)

    def paired_heads(parts_of, count, c):
        return jnp.where(low, parts_of(2 * c), parts_of(2 * c + 1) if 2 * c + 1 < count else empty)

    def summed(ref):
        return lambda j: ref[j] + pltpu.roll(ref[j], 64, 1)

    query_tiles = [
        turned(paired_heads(lambda h: head_parts[h], HEADS, c) * HEAD**-0.5, cosine, -sine)
        for c in range(8)
    ]
    key_tiles = [
        turned(paired_heads(summed(key_parts), KV_HEADS, c) * HEAD**-0.5, cosine, -sine)
        for c in range(3)
    ]
    value_tiles = [paired_heads(summed(value_parts), KV_HEADS, c) for c in range(3)]
    for r in range(REPS):
        tiles = laid(
            [
                (query_tiles, 240 * r, 0, 240),
                (key_tiles, 80 * r, 240, 80),
                (value_tiles, 80 * r, 320, 80),
            ],
            MB_TOK,
            4,
        )
        wire_in[r ^ quarter_here] = joined(tiles).astype(bf16)
    d_normed = sum(
        dot_nt(wire_in[quarter], block_columns(attn_all, quarter, 0, 512))
        for quarter in range(REPS)
    )
    values = inputs[...].astype(f32)
    scale = lax.rsqrt(jnp.sum(values * values, axis=1, keepdims=True) * (1.0 / D) + norm_epsilon)
    weighted = d_normed * gain_one
    inner = jnp.sum(weighted * values, axis=1, keepdims=True) * (1.0 / D)
    term_one = jnp.sum(d_normed * values * scale, axis=0, keepdims=True)
    total = d_middle + scale * weighted - values * scale * scale * scale * inner
    token_grad[...] = total.astype(bf16)
    gain_sums[0:1, :] = term_one
    gain_sums[1:2, :] = term_two


def attn_grads_kernel(*refs, count):
    normed, mixed, wires_in, wires_out, gain_parts = [
        refs[n * count : n * count + count] for n in range(5)
    ]
    arrays = refs[5 * count : 5 * count + 2]
    gain_sums = sum(part[0:8, :] for part in gain_parts)

    def stacked(parts, *at):
        return jnp.concatenate([part[at] for part in parts], axis=0)

    normed_turned = stacked(normed, ...).T
    mixed_turned = stacked(mixed, ...).T
    wire_out = stacked(wires_out, ...)
    row = lax.broadcasted_iota(jnp.int32, (SLOTS, 16, SLOT), 1)
    gain_rows = jnp.zeros((SLOTS, 16, SLOT), f32)
    for which in range(2):
        spots = [
            gain_sums[which : which + 1, s * SLOT : s * SLOT + SLOT].reshape(1, 1, SLOT)
            for s in range(SLOTS)
        ]
        gain_rows = jnp.where(row == 8 + which, jnp.concatenate(spots, axis=0), gain_rows)
    for quarter in range(REPS):
        first = dot_nn(normed_turned, stacked(wires_in, quarter))
        second = dot_nn(mixed_turned, wire_out[:, quarter * 256 : quarter * 256 + 256])
        block = jnp.concatenate(
            [first[:, 0:384], first[:, 384:512] + second[:, 0:128], second[:, 128:256]], axis=1
        ).reshape(SLOTS, SLOT, PACK)
        y, core = (quarter >> 1, quarter & 1)
        low_rows = block[:, 0:ROWS_A, :].astype(bf16)
        high_rows = block[:, ROWS_A:SLOT, :].astype(bf16)
        target = arrays[core]
        target[0, y, :, :, :] = low_rows
        tail = (block[:, 112:SLOT, 0:SLOT] + gain_rows).astype(bf16)
        for side in range(2):
            slots = slice(side * 4, side * 4 + 4)
            target[1, side, y * 4 : y * 4 + 4, :, :] = high_rows[slots]
            target[1, side, y * 4 : y * 4 + 4, 48:64, 0:SLOT] = tail[slots]


def attn_backward(
    batch,
    here,
    cotangent,
    middle,
    d_normed_two,
    inputs,
    query_rot,
    key_both,
    value_both,
    probs,
    tables,
    parts,
):
    one = [middle, d_normed_two]
    own = [query_rot, key_both, value_both, probs]
    outs = [
        ((MB_TOK, WIDE), bf16),
        ((REPS, MB_TOK, 512), bf16),
        ((MB_TOK, REPS * 256), bf16),
        ((8, WIDE), f32),
    ]
    return pl.pallas_call(
        attn_backward_kernel,
        grid=(1,),
        in_specs=[in_scalars(), batch_block(batch, WIDE)]
        + [whole_block(array.shape) for array in one]
        + [batch_block(batch, WIDE)]
        + [whole_block(array.shape) for array in own]
        + [batch_block(batch, 128)] * 2
        + [anywhere()] * 6,
        out_specs=[whole_block(out[0]) for out in outs],
        out_shape=[jax.ShapeDtypeStruct(*out) for out in outs],
        scratch_shapes=[
            pltpu.VMEM((REPS, SLOTS, SLOT, PACK), bf16),
            pltpu.VMEM((SLOTS, MB_TOK, SLOT), f32),
            pltpu.VMEM((HEADS, MB_TOK, 128), f32),
            pltpu.VMEM((KV_HEADS, MB_TOK, 128), f32),
            pltpu.VMEM((KV_HEADS, MB_TOK, 128), f32),
            pltpu.VMEM((MB_TOK, WIDE), bf16),
            pltpu.SemaphoreType.DMA((12,)),
        ],
        compiler_params=pltpu.CompilerParams(vmem_limit_bytes=VMEM_BYTES),
        cost_estimate=pl.CostEstimate(
            flops=12_000_000_000, bytes_accessed=20_000_000, transcendentals=0
        ),
        name="attn_backward",
    )(here, cotangent, *one, inputs, *own, *tables, *parts)


def attn_grads(normed, mixed, wires_in, wires_out, gain_parts):
    count = len(normed)
    half = jax.ShapeDtypeStruct((2, 2, SLOTS, ROWS_A, PACK), bf16)
    arrays = (*normed, *mixed, *wires_in, *wires_out, *gain_parts)
    return pl.pallas_call(
        lambda *refs: attn_grads_kernel(*refs, count=count),
        grid=(1,),
        in_specs=[whole_block(array.shape) for array in arrays],
        out_specs=[whole_block(half.shape)] * 2,
        out_shape=[half] * 2,
        compiler_params=pltpu.CompilerParams(vmem_limit_bytes=VMEM_BYTES),
        cost_estimate=pl.CostEstimate(
            flops=8_000_000_000, bytes_accessed=14_000_000, transcendentals=0
        ),
        name="attn_grads",
    )(*arrays)


X_SIDE = ("fsdp", 1)
Y_SIDE = ("rep", 2)
CORE = ("rep", 1)


def swap_with(values, step):
    axis, mask = step
    count = lax.axis_size(axis)
    return lax.ppermute(values, axis, [(i, i ^ mask) for i in range(count)])


def after(values, *done):
    return lax.optimization_barrier((values, done))[0]


def sent_along_z(block):
    return [swap_with(block, ("fsdp", 2 * k)) for k in range(1, 4)]


def along_z(block, came):
    return jnp.stack([block] + list(came))


def sides_of(side_first):
    return (X_SIDE, Y_SIDE) if side_first else (Y_SIDE, X_SIDE)


def sent_along_first(four, side_first):
    return swap_with(four, sides_of(side_first)[0])


def along_first(four, side_first):
    return jnp.concatenate([four, sent_along_first(four, side_first)])


def along_second(eight, side_first):
    return swap_with(eight, sides_of(side_first)[1])


def over_core(one, two):
    return swap_with(jnp.concatenate([one, two]), CORE)


def added(left, right):
    return (left.astype(f32) + right.astype(f32)).astype(bf16)


class Reduction:
    def __init__(self, kept, came, which, side_first):
        self.kept = kept
        self.came = came
        self.which = which
        self.first, self.second = sides_of(side_first)
        self.out = added(kept[which, 1], came[which, 1])

    def sent_second(self):
        return swap_with(self.out, self.second)

    def over_second(self, came):
        kept, before = after((self.kept, self.came), came)
        eight = added(kept[self.which, 0], before[self.which, 0])
        self.out = added(eight[4:8], came[4:8])
        self.four = added(eight[0:4], came[0:4])

    def sent_first(self):
        return swap_with(self.out, self.first)

    def over_first(self, came):
        self.blocks = [added(self.four[k], came[k]) for k in range(4)]


def z_stage(one, two):
    blocks = [jnp.concatenate([one.blocks[k], two.blocks[k]], axis=0) for k in range(4)]
    return (blocks[0], [swap_with(blocks[k], ("fsdp", 2 * k)) for k in range(1, 4)])


def z_sum(kept, came):
    return sum((block.astype(f32) for block in came), kept.astype(f32))


def split_parts(blocks, side_first):
    rows, columns = blocks.shape[2:]
    grid = blocks.reshape(4, 2, 2, 2, rows, columns)
    parts = []
    for second in range(2):
        for core in range(2):
            if side_first:
                part = grid[:, :, second, core].transpose(1, 0, 2, 3)
            else:
                part = grid[:, second, :, core].transpose(1, 0, 2, 3)
            parts.append(part.reshape(SLOTS, rows, columns))
    return parts


def six_parts(first_blocks, second_blocks):
    one, two = (split_parts(first_blocks, True), split_parts(second_blocks, False))
    near, far = (jnp.concatenate([one[1], two[1]]), jnp.concatenate([one[3], two[3]]))
    return (one[0], two[0], one[2], two[2], near, far)


def join_parts(kept, sent, side_first):
    rows, columns = kept.shape[2:]
    grid = jnp.stack([kept, sent]).reshape(2, 2, 2, 4, rows, columns)
    grid = grid.transpose(3, 2, 1, 0, 4, 5) if side_first else grid.transpose(3, 1, 2, 0, 4, 5)
    return grid.reshape(SLOTS, REPS, rows, columns)


def attn_block(w_query, w_key, w_value, w_output, attn_gain, mlp_gain):
    matrices = jnp.concatenate([w_query, w_key, w_value, w_output], axis=1)
    gains = jnp.stack([attn_gain, mlp_gain])
    gains = jnp.pad(gains, ((0, SLOT - USED - 2), (0, PACK - USED)))
    return jnp.concatenate([matrices, gains], axis=0)


def down_block(w_down):
    halves = w_down.T.reshape(2, USED, HALF_PACK)
    halves = jnp.concatenate([halves[0], halves[1]], axis=1)
    return jnp.pad(halves, ((0, SLOT - USED), (0, 0)))


def mlp_blocks(w_gate, w_up, w_down):
    taller = ((0, SLOT - USED), (0, 0))
    down = down_block(w_down)
    return (
        jnp.concatenate([jnp.pad(w_gate, taller), down[:ROWS_A]], axis=0),
        jnp.concatenate([jnp.pad(w_up, taller), down[ROWS_A:]], axis=0),
    )


def down_of(block):
    halves = jnp.stack([block[:USED, :HALF_PACK], block[:USED, HALF_PACK:]])
    return halves.reshape(2 * USED, HALF_PACK).T


def whole(shard):
    return lax.all_gather(lax.all_gather(shard, "rep", axis=1, tiled=True), "fsdp", axis=0, tiled=True)


def cut(matrix, eighth, quarter):
    rows, columns = (matrix.shape[0] // SLOTS, matrix.shape[1] // REPS)
    return matrix[
        eighth * rows : eighth * rows + rows, quarter * columns : quarter * columns + columns
    ]


def every_block(make):
    return jnp.stack(
        [jnp.stack([make(e, q) for q in range(REPS)]) for e in range(SLOTS)]
    )


def owned(blocks):
    eighths, quarters, rows, columns = blocks.shape
    matrix = blocks.transpose(0, 2, 1, 3).reshape(eighths * rows, quarters * columns)
    part = lax.psum_scatter(matrix, "fsdp", scatter_dimension=0, tiled=True)
    return lax.psum_scatter(part, "rep", scatter_dimension=1, tiled=True).astype(f32)


def per_device(
    tokens,
    lengths,
    attn_gain,
    w_query,
    w_key,
    w_value,
    w_output,
    mlp_gain,
    w_gate,
    w_up,
    w_down,
    cotangent,
):
    paired = lax.axis_size("fsdp") == SLOTS and lax.axis_size("rep") == REPS
    if paired:
        eighth_here = lax.axis_index("fsdp").astype(jnp.int32)
        quarter_here = lax.axis_index("rep").astype(jnp.int32)
    else:
        eighth_here = jnp.int32(0)
        quarter_here = jnp.int32(0)
    here = jnp.stack([eighth_here, quarter_here])
    spread = spreading(eighth_here)
    segments, positions = jax.vmap(layout)(lengths)
    tables = rope_tables(positions.reshape(-1))
    inputs = jnp.dot(tokens, spread, preferred_element_type=f32).astype(bf16)
    upstream = jnp.dot(cotangent, spread, preferred_element_type=f32).astype(bf16)
    upstream_turned = upstream.T
    batches = range(tokens.shape[0] // MB_TOK)
    forward_inputs = [inputs for _ in batches]

    if paired:
        attn_pack = attn_block(w_query, w_key, w_value, w_output, attn_gain, mlp_gain)
        gate_pack, up_pack = mlp_blocks(w_gate, w_up, w_down)
        attn_four = along_z(attn_pack, sent_along_z(attn_pack))
        gate_pack = after(gate_pack, attn_four)
        gate_came = sent_along_z(gate_pack)
        one, two = (attn_four[:, :ROWS_A], attn_four[:, ROWS_A:])
        came = (sent_along_first(one, True), sent_along_first(two, False))
        gate_came, came, up_pack = lax.optimization_barrier((gate_came, came, up_pack))
        one, two = (jnp.concatenate([one, came[0]]), jnp.concatenate([two, came[1]]))
        gate_four = along_z(gate_pack, gate_came)
        gate_one, gate_two = (gate_four[:, :ROWS_M], gate_four[:, ROWS_M:])
        up_came = sent_along_z(up_pack)
        across = (along_second(one, True), along_second(two, False))
        came = (sent_along_first(gate_one, True), sent_along_first(gate_two, False))
        up_came, across, came = lax.optimization_barrier((up_came, across, came))
        attn_near = over_core(one, two)
        attn_far = over_core(*across)
        attn_parts = (one, two, *across, attn_near, attn_far)
        gate_one, gate_two = (
            jnp.concatenate([gate_one, came[0]]),
            jnp.concatenate([gate_two, came[1]]),
        )
        up_four = along_z(up_pack, up_came)
        up_one, up_two = (up_four[:, :ROWS_M], up_four[:, ROWS_M:])
        up_came = (sent_along_first(up_one, True), sent_along_first(up_two, False))
        forward_inputs[0] = after(inputs, gate_one, gate_two, up_four, upstream_turned)
        gate_across = (along_second(gate_one, True), along_second(gate_two, False))
    else:
        gain_one, gain_two = (
            lax.all_gather(attn_gain, "fsdp", axis=0, tiled=True).reshape(SLOTS, USED),
            lax.all_gather(mlp_gain, "fsdp", axis=0, tiled=True).reshape(SLOTS, USED),
        )
        mats = [whole(w) for w in (w_query, w_key, w_value, w_output, w_gate, w_up, w_down)]
        attn_blocks = every_block(
            lambda e, q: attn_block(*[cut(m, e, q) for m in mats[:4]], gain_one[e], gain_two[e])
        )
        attn_parts = six_parts(attn_blocks[:, :, :ROWS_A], attn_blocks[:, :, ROWS_A:])
        mlp_each = [
            [
                mlp_blocks(cut(mats[4], e, q), cut(mats[5], e, q), cut(mats[6], e, q))
                for q in range(REPS)
            ]
            for e in range(SLOTS)
        ]
        mlp_parts = []
        for group in range(2):
            blocks = every_block(lambda e, q: mlp_each[e][q][group])
            mlp_parts += six_parts(blocks[:, :, :ROWS_M], blocks[:, :, ROWS_M:])

    made = []
    for batch in batches:
        made.append(attn_forward(batch, here, forward_inputs[batch], attn_parts, tables, segments))
        if paired and batch == 0:
            up_came = after(up_came, made[0][-1])
            up_one = jnp.concatenate([up_one, up_came[0]])
            up_two = jnp.concatenate([up_two, up_came[1]])
            forward_inputs[-1] = after(inputs, up_one, up_two)
            up_across = (along_second(up_one, True), along_second(up_two, False))
    normed, query_rot, key_both, value_both, probs, mixed, middle, normed_two = zip(*made)
    if paired:
        gate_one, gate_two = after((gate_one, gate_two), normed_two[0])
        gate_near = over_core(gate_one, gate_two)
        gate_across, up_one, up_two = after((gate_across, up_one, up_two), normed_two[-1])
        gate_far = over_core(*gate_across)
        up_near = over_core(up_one, up_two)
        up_far = over_core(*up_across)
        mlp_parts = (
            *(gate_one, gate_two, *gate_across, gate_near, gate_far),
            *(up_one, up_two, *up_across, up_near, up_far),
        )
    hidden, d_gate, d_up, w_down_all, kept, sent = mlp(
        here, normed_two, upstream, upstream_turned, mlp_parts
    )
    mlp_out, d_normed_two = mlp_outputs(hidden, d_gate, d_up, w_down_all, mlp_parts)
    d_normed_two = list(d_normed_two)
    if paired:
        came = swap_with(sent, CORE)
        gate_sums = [Reduction(kept, came, which, which == 0) for which in range(2)]
        up_sums = [Reduction(kept, came, 2 + which, which == 0) for which in range(2)]
        d_normed_two[0] = after(d_normed_two[0], gate_sums[0].out, gate_sums[1].out)
    back = []
    for batch in batches:
        back.append(
            attn_backward(
                batch,
                here,
                upstream,
                middle[batch],
                d_normed_two[batch],
                inputs,
                query_rot[batch],
                key_both[batch],
                value_both[batch],
                probs[batch],
                tables,
                attn_parts,
            )
        )
        if paired and batch == 0:
            for part in gate_sums:
                part.over_second(part.sent_second())
            for part in up_sums:
                part.out = after(part.out, gate_sums[0].out, gate_sums[1].out)
            d_normed_two[-1] = after(d_normed_two[-1], up_sums[0].out, up_sums[1].out)
    token_rows, wires_in, wires_out, gain_parts = zip(*back)
    if paired:
        for part in up_sums:
            part.over_second(part.sent_second())
        for part in gate_sums:
            part.over_first(part.sent_first())
        wires_in = after(
            wires_in, up_sums[0].out, up_sums[1].out, gate_sums[0].blocks, gate_sums[1].blocks
        )
    attn_kept, attn_sent = attn_grads(
        normed, mixed, wires_in, wires_out, gain_parts
    )
    middle, mlp_out, token_rows = after((middle, mlp_out, token_rows), attn_kept)
    output_rows = jnp.concatenate(
        [(middle[batch] + mlp_out[batch]).astype(bf16) for batch in batches], axis=0
    )
    output = jnp.dot(output_rows, spread.T, preferred_element_type=f32).astype(bf16)
    token_grad = jnp.dot(
        jnp.concatenate(token_rows, axis=0), spread.T, preferred_element_type=f32
    ).astype(bf16)
    if paired:
        up_came = [part.sent_first() for part in up_sums]
        gate_kept, gate_came = z_stage(*gate_sums)
        up_came, gate_came, attn_sent = lax.optimization_barrier((up_came, gate_came, attn_sent))
        came = swap_with(attn_sent, CORE)
        for part, part_came in zip(up_sums, up_came):
            part.over_first(part_came)
        one, two = [Reduction(attn_kept, came, which, which == 0) for which in range(2)]
        up_kept, up_came = z_stage(*up_sums)
        across = (one.sent_second(), two.sent_second())
        up_came, across = lax.optimization_barrier((up_came, across))
        one.over_second(across[0])
        two.over_second(across[1])
        one.over_first(one.sent_first())
        two.over_first(two.sent_first())
        gate_sum = z_sum(gate_kept, gate_came)
        up_sum = z_sum(up_kept, up_came)
        attn_sum = z_sum(*z_stage(one, two))
        gain_sums = (attn_sum[USED, :USED], attn_sum[USED + 1, :USED])
        attn_sum = attn_sum[:USED]
        grads = [
            attn_sum[:, 0:240],
            attn_sum[:, 240:320],
            attn_sum[:, 320:400],
            attn_sum[:, 400:640],
            gate_sum[:USED],
            up_sum[:USED],
            down_of(jnp.concatenate([gate_sum[SLOT:], up_sum[SLOT:]], axis=0)),
        ]
    else:
        attn_blocks = jnp.concatenate(
            [join_parts(attn_kept[k], attn_sent[k], k == 0) for k in range(2)], axis=2
        )
        gain_sums = tuple(
            lax.psum(
                lax.psum_scatter(
                    attn_blocks[:, 0, USED + which, :USED].astype(f32).reshape(D),
                    "fsdp",
                    scatter_dimension=0,
                    tiled=True,
                ),
                "rep",
            )
            for which in range(2)
        )
        attn_blocks = attn_blocks[:, :, :USED]
        gate_blocks, up_blocks = [
            jnp.concatenate(
                [join_parts(kept[k], sent[k], k % 2 == 0) for k in (which, which + 1)], axis=2
            )
            for which in (0, 2)
        ]
        down_blocks = jnp.concatenate([gate_blocks[:, :, SLOT:], up_blocks[:, :, SLOT:]], axis=2)
        grads = [
            owned(attn_blocks[..., 0:240]),
            owned(attn_blocks[..., 240:320]),
            owned(attn_blocks[..., 320:400]),
            owned(attn_blocks[..., 400:640]),
            owned(gate_blocks[:, :, :USED]),
            owned(up_blocks[:, :, :USED]),
            owned(jax.vmap(jax.vmap(down_of))(down_blocks)),
        ]
    return (
        output,
        token_grad,
        gain_sums[0],
        grads[0],
        grads[1],
        grads[2],
        grads[3],
        gain_sums[1],
        grads[4],
        grads[5],
        grads[6],
    )


def solution(mesh):
    placed = (
        P(("fsdp", "rep"), None),
        P(("fsdp", "rep"), None),
        P("fsdp"),
        P("fsdp", "rep"),
        P("fsdp", "rep"),
        P("fsdp", "rep"),
        P("fsdp", "rep"),
        P("fsdp"),
        P("fsdp", "rep"),
        P("fsdp", "rep"),
        P("fsdp", "rep"),
        P(("fsdp", "rep"), None),
    )
    return jax.shard_map(
        per_device,
        mesh=mesh,
        in_specs=placed,
        out_specs=(
            P(("fsdp", "rep"), None),
            P(("fsdp", "rep"), None),
            P("fsdp"),
            P("fsdp", "rep"),
            P("fsdp", "rep"),
            P("fsdp", "rep"),
            P("fsdp", "rep"),
            P("fsdp"),
            P("fsdp", "rep"),
            P("fsdp", "rep"),
            P("fsdp", "rep"),
        ),
        check_vma=False,
    )
```

```python
import jax
import jax.numpy as jnp
from jax import lax
from jax.experimental import pallas as pl
from jax.experimental.pallas import tpu as pltpu
from jax.sharding import PartitionSpec as P

D = 960
FF = 2560
HEADS = 15
KV_HEADS = 5
HEAD = 64
MB_TOK = 384
SEGS = 3
GROUP = 3
QW = 960
KVW = 320

SLOTS = 8
REPS = 4
USED = 120
SLOT = 128
WIDE = SLOTS * SLOT
PACK = 640
HALF_PACK = 320
ROWS_A = 64
ROWS_M = 96
REST = SLOT - ROWS_M
ROWS_W = 192
VMEM_BYTES = 60 * 1024 * 1024

norm_epsilon = 1e-05
rope_base = 100000.0
masked_value = -1e30

f32 = jnp.float32
bf16 = jnp.bfloat16


def layout(length_row):
    starts = jnp.cumsum(length_row) - length_row
    places = jnp.arange(MB_TOK, dtype=jnp.int32)
    inside = (
        (places[:, None] >= starts[None, :]) & (places[:, None] < (starts + length_row)[None, :])
    ).astype(jnp.int32)
    segment = jnp.sum(inside * jnp.arange(SEGS, dtype=jnp.int32)[None, :], axis=1)
    position = places - jnp.sum(inside * starts[None, :], axis=1)
    return (segment, position)


def rope_tables(position):
    half_width = HEAD // 2
    exponent = jnp.arange(half_width, dtype=f32) * (2.0 / HEAD)
    inverse = jnp.power(rope_base, -exponent)
    angles = position.astype(f32)[:, None] * inverse
    cosines, sines = (jnp.cos(angles), jnp.sin(angles))
    return (
        jnp.concatenate([cosines] * 4, axis=1),
        jnp.concatenate([-sines, sines, -sines, sines], axis=1),
    )


def slot_of(eighth):
    return (eighth & 1) * 4 + (eighth >> 1)


def eighth_of(slot):
    return (slot & 3) * 2 + (slot >> 2)


def feature_lanes(eighth_here):
    lanes = jnp.arange(WIDE, dtype=jnp.int32)
    eighth = eighth_of(lanes // SLOT) ^ eighth_here
    return jnp.where(lanes % SLOT < USED, eighth * USED + lanes % SLOT, -1)


def spreading(eighth_here):
    features = jnp.arange(D, dtype=jnp.int32)
    return (features[:, None] == feature_lanes(eighth_here)[None, :]).astype(bf16)


def dot_nn(left, right):
    return lax.dot_general(left, right, (((1,), (0,)), ((), ())), preferred_element_type=f32)


def dot_nt(left, right):
    return lax.dot_general(left, right, (((1,), (1,)), ((), ())), preferred_element_type=f32)


def dot_tn(left, right):
    return lax.dot_general(left, right, (((0,), (0,)), ((), ())), preferred_element_type=f32)


def lane_index(shape):
    return lax.broadcasted_iota(jnp.int32, shape, len(shape) - 1)


def swapped(values):
    first = (lane_index(values.shape) & 63) < 32
    return jnp.where(first, pltpu.roll(values, 96, 1), pltpu.roll(values, 32, 1))


def turned(values, cosines, sines):
    return values * cosines + swapped(values) * sines


def both_halves(values, odd):
    low = lane_index(values.shape) < 64
    moved = pltpu.roll(values, 64, 1)
    return jnp.where(low, moved, values) if odd else jnp.where(low, values, moved)


def only_half(values, odd):
    low = lane_index(values.shape) < 64
    return jnp.where(low != bool(odd), values, jnp.zeros_like(values))


def laid(pieces, rows, tiles):
    lane = lane_index((rows, 128))
    made = [jnp.zeros((rows, 128), f32)] * tiles
    for source, start, target, width in pieces:
        shifted = {}
        done = 0
        while done < width:
            from_tile, from_lane = divmod(start + done, 128)
            to_tile, to_lane = divmod(target + done, 128)
            now = min(width - done, 128 - from_lane, 128 - to_lane)
            if from_tile not in shifted:
                values = source[from_tile]
                turn = (to_lane - from_lane) % 128
                shifted[from_tile] = pltpu.roll(values, turn, 1) if turn else values
            inside = (lane >= to_lane) & (lane < to_lane + now)
            made[to_tile] = jnp.where(inside, shifted[from_tile], made[to_tile])
            done += now
    return made


def tiles_of(values):
    return [values[:, t : t + 128] for t in range(0, values.shape[1], 128)]


def joined(tiles):
    return jnp.concatenate(tiles, axis=1)


def gain_row(attn_ref, which):
    rows = [attn_ref[0, s, 112:128, 0:SLOT].astype(f32)[8 + which : 9 + which] for s in range(SLOTS)]
    return jnp.concatenate(rows, axis=1)


def views(parts):
    return (parts[:4], parts[4:])


def attn_fetches(parts, attn_all, sems):
    copies = []
    firsts, seconds = views(parts)
    for quarter, source in enumerate(firsts):
        copies.append((source, attn_all.at[quarter, :, 0:ROWS_A, :]))
    for place, source in enumerate(seconds):
        side, core = (place >> 1, place & 1)
        for y in range(2):
            copies.append(
                (
                    source.at[y * 4 : y * 4 + 4],
                    attn_all.at[y * 2 + core, side * 4 : side * 4 + 4, ROWS_A : 2 * ROWS_A, :],
                )
            )
    return [
        pltpu.make_async_copy(source, target, sems.at[n])
        for n, (source, target) in enumerate(copies)
    ]


def block_columns(attn_all, quarter, low, high):
    return attn_all[quarter, :, :, low:high].reshape(WIDE, high - low)


def probs_at(part):
    return (0, 128, 384)[part]


def attn_forward_kernel(
    here,
    inputs,
    cosines,
    sines,
    segment_rows,
    segment_columns,
    *refs,
):
    parts = refs[:8]
    (
        normed_out,
        query_out,
        key_out,
        value_out,
        probs_out,
        mixed_out,
        middle_out,
        normed_two_out,
        attn_all,
        wire,
        heads_out,
        mixed_slots,
        out_slots,
        bias,
        sems,
    ) = refs[8:]
    eighth_here, quarter_here = (here[0], here[1])
    fetches = attn_fetches(parts, attn_all, sems)
    for copy in fetches:
        copy.start()
    values = inputs[...].astype(f32)
    scale = lax.rsqrt(jnp.sum(values * values, axis=1, keepdims=True) * (1.0 / D) + norm_epsilon)
    for copy in fetches:
        copy.wait()
    normed = (values * scale * gain_row(attn_all, 0)).astype(bf16)
    normed_out[...] = normed
    cosine, sine = (cosines[...], sines[...])
    for quarter in range(REPS):
        wire[quarter] = dot_nn(normed, block_columns(attn_all, quarter, 0, 512))
    sources = [
        [wire[r ^ quarter_here, :, t * 128 : t * 128 + 128] for t in range(4)] for r in range(REPS)
    ]
    query_tiles = laid([(sources[r], 0, 240 * r, 240) for r in range(REPS)], MB_TOK, 8)
    for c in range(8):
        query_out[:, c * 128 : c * 128 + 128] = turned(query_tiles[c], cosine, sine).astype(bf16)
    key_tiles = laid([(sources[r], 240, 80 * r, 80) for r in range(REPS)], MB_TOK, 3)
    value_tiles = laid([(sources[r], 320, 80 * r, 80) for r in range(REPS)], MB_TOK, 3)
    for c in range(3):
        key_part = turned(key_tiles[c], cosine, sine)
        for odd in range(2 if c < 2 else 1):
            at = slice((2 * c + odd) * 128, (2 * c + odd) * 128 + 128)
            key_out[:, at] = both_halves(key_part, odd).astype(bf16)
            value_out[:, at] = both_halves(value_tiles[c], odd).astype(bf16)

    query_place = lax.broadcasted_iota(jnp.int32, (MB_TOK, MB_TOK), 0)
    key_place = lax.broadcasted_iota(jnp.int32, (MB_TOK, MB_TOK), 1)
    seen = (segment_rows[...] == segment_columns[0]) & (key_place <= query_place)
    bias[...] = jnp.where(seen, 0.0, masked_value)
    for j in range(KV_HEADS):
        at = slice(j * 128, j * 128 + 128)
        for part in range(3):
            keys = 128 * (part + 1)
            rows = slice(part * 128, part * 128 + 128)
            queries = jnp.concatenate(
                [
                    only_half(query_out[rows, (h // 2) * 128 : (h // 2) * 128 + 128], h % 2)
                    for h in range(3 * j, 3 * j + 3)
                ],
                axis=0,
            )
            scores = dot_nt(queries, key_out[0:keys, at]) * HEAD**-0.5
            hidden_part = bias[rows, 0:keys]
            scores = scores + jnp.concatenate([hidden_part] * GROUP, axis=0)
            peak = jnp.max(scores, axis=1, keepdims=True)
            weights = jnp.exp(scores - peak)
            total = jnp.sum(weights, axis=1, keepdims=True)
            probs = (weights * (1.0 / total)).astype(bf16)
            probs_out[j, :, probs_at(part) : probs_at(part) + keys] = probs
            gathered = dot_nn(probs, value_out[0:keys, at])
            for g in range(GROUP):
                heads_out[3 * j + g, rows, :] = gathered[g * 128 : g * 128 + 128]
    low = lane_index((MB_TOK, 128)) < 64
    head_tiles = [
        jnp.where(
            low,
            heads_out[2 * c],
            heads_out[2 * c + 1] if 2 * c + 1 < HEADS else jnp.zeros((MB_TOK, 128), f32),
        )
        for c in range(8)
    ]
    for eighth in range(SLOTS):
        (slot_tile,) = laid([(head_tiles, USED * eighth, 0, USED)], MB_TOK, 1)
        mixed_slots[slot_of(eighth ^ eighth_here)] = slot_tile.astype(bf16)
    mixed = joined([mixed_slots[s] for s in range(SLOTS)])
    mixed_out[...] = mixed
    for quarter in range(REPS):
        part = tiles_of(dot_nn(mixed, block_columns(attn_all, quarter, 384, 640)))
        for which in range(2):
            eighth = (quarter ^ quarter_here) * 2 + which
            (slot_tile,) = laid([(part, 16 + USED * which, 0, USED)], MB_TOK, 1)
            out_slots[slot_of(eighth ^ eighth_here)] = slot_tile
    middle = values + joined([out_slots[s] for s in range(SLOTS)])
    middle_out[...] = middle
    scale_two = lax.rsqrt(
        jnp.sum(middle * middle, axis=1, keepdims=True) * (1.0 / D) + norm_epsilon
    )
    normed_two_out[...] = (middle * scale_two * gain_row(attn_all, 1)).astype(bf16)


def whole_block(shape):
    return pl.BlockSpec(
        shape, lambda *ids: (0,) * len(shape), pipeline_mode=pl.Buffered(buffer_count=1)
    )


def anywhere():
    return pl.BlockSpec(memory_space=pl.ANY)


def batch_block(batch, columns):
    return pl.BlockSpec((MB_TOK, columns), lambda i: (batch, 0))


def attn_scratch():
    return [
        pltpu.VMEM((REPS, SLOTS, SLOT, PACK), bf16),
        pltpu.VMEM((REPS, MB_TOK, 512), f32),
        pltpu.VMEM((HEADS, MB_TOK, 128), f32),
    ]


def in_scalars():
    return pl.BlockSpec(memory_space=pltpu.SMEM)


def attn_forward(batch, here, inputs, parts, tables, segments):
    count = inputs.shape[0] // MB_TOK
    outs = [
        ((MB_TOK, WIDE), bf16),
        ((MB_TOK, WIDE), bf16),
        ((MB_TOK, PACK), bf16),
        ((MB_TOK, PACK), bf16),
        ((KV_HEADS, MB_TOK, 768), bf16),
        ((MB_TOK, WIDE), bf16),
        ((MB_TOK, WIDE), f32),
        ((MB_TOK, WIDE), bf16),
    ]
    return pl.pallas_call(
        attn_forward_kernel,
        grid=(1,),
        in_specs=[
            in_scalars(),
            batch_block(batch, WIDE),
            batch_block(batch, 128),
            batch_block(batch, 128),
            batch_block(batch, 1),
            pl.BlockSpec((1, 1, MB_TOK), lambda i: (batch, 0, 0)),
        ]
        + [anywhere()] * 8,
        out_specs=[whole_block(out[0]) for out in outs],
        out_shape=[jax.ShapeDtypeStruct(*out) for out in outs],
        scratch_shapes=attn_scratch()
        + [
            pltpu.VMEM((SLOTS, MB_TOK, SLOT), bf16),
            pltpu.VMEM((SLOTS, MB_TOK, SLOT), f32),
            pltpu.VMEM((MB_TOK, MB_TOK), f32),
            pltpu.SemaphoreType.DMA((12,)),
        ],
        compiler_params=pltpu.CompilerParams(vmem_limit_bytes=VMEM_BYTES),
        cost_estimate=pl.CostEstimate(
            flops=8_000_000_000, bytes_accessed=16_000_000, transcendentals=2_000_000
        ),
        name="attn_forward",
    )(
        here,
        inputs,
        *tables,
        segments.reshape(-1, 1),
        segments.reshape(count, 1, MB_TOK),
        *parts,
    )


def left_right(left, right):
    first = lane_index(left.shape) < HALF_PACK
    left, right = (left.astype(f32), right.astype(f32))
    return (
        jnp.where(first, left, pltpu.roll(right, HALF_PACK, 1)).astype(bf16),
        jnp.where(first, pltpu.roll(left, HALF_PACK, 1), right).astype(bf16),
    )


def pair_fetches(parts, at, w_gate, w_up, sems):
    found = []
    firsts, seconds = views(parts)
    for core in range(2):
        lanes = slice(core * PACK, core * PACK + PACK)
        source = firsts[at * 2 + core]
        found.append((source.at[:, 0:SLOT, :], w_gate.at[:, :, lanes]))
        found.append((source.at[:, SLOT:ROWS_W, :], w_up.at[:, 0:64, lanes]))
        for side in range(2):
            found.append(
                (
                    seconds[side * 2 + core].at[at * 4 : at * 4 + 4, 0:64, :],
                    w_up.at[side * 4 : side * 4 + 4, 64:SLOT, lanes],
                )
            )
    return [
        pltpu.make_async_copy(source, target, sems.at[n])
        for n, (source, target) in enumerate(found)
    ]


def mlp_kernel(here, *refs, count):
    normed = refs[:count]
    cotangent = refs[count]
    parts = refs[count + 1 : count + 9]
    hidden, d_gate, d_up, down_out, kept, sent = refs[count + 9 : count + 15]
    (
        w_gate,
        w_up,
        down_raw,
        normed_turned,
        cotangent_turned,
        grad_gate,
        grad_up,
        grad_down,
        down_made,
        sem_pair,
        sem_down,
        sem_out,
    ) = refs[count + 15 :]
    step = pl.program_id(0)
    eighth_here, quarter_here = (here[0], here[1])
    side_here = eighth_here & 1

    def plane_of(at, core):
        return ((2 * at + core) ^ quarter_here) ^ (eighth_here >> 1)

    def fetches(at):
        found = []
        for core in range(2):
            for side in range(2):
                for quarter in range(REPS):
                    y, inner = (quarter >> 1, quarter & 1)
                    found.append(
                        (
                            views(parts)[1][side * 2 + inner].at[
                                y * 4 + plane_of(at, core), 64:ROWS_W
                            ],
                            down_raw.at[core, side, quarter],
                        )
                    )
        return pair_fetches(parts, at, w_gate, w_up, sem_pair) + [
            pltpu.make_async_copy(source, target, sem_down.at[n])
            for n, (source, target) in enumerate(found)
        ]

    def results(at):
        found = []
        for group, source in enumerate((grad_gate, grad_up)):
            firsts = (kept.at[2 * group], sent.at[2 * group])
            seconds = (kept.at[2 * group + 1], sent.at[2 * group + 1])
            for core in range(2):
                found.append((source.at[core, :, 0:ROWS_M], firsts[core].at[at]))
                for side in range(2):
                    found.append(
                        (
                            source.at[core, side * 4 : side * 4 + 4, ROWS_M:SLOT],
                            seconds[core].at[side, at * 4 : at * 4 + 4, 0:REST],
                        )
                    )
                    for quarter in range(REPS):
                        y, inner = (quarter >> 1, quarter & 1)
                        found.append(
                            (
                                down_made.at[
                                    core, side, quarter, group * ROWS_A : group * ROWS_A + ROWS_A
                                ],
                                seconds[inner].at[
                                    side, y * 4 + plane_of(at, core), REST:ROWS_M
                                ],
                            )
                        )
        return [
            pltpu.make_async_copy(source, target, sem_out.at[n])
            for n, (source, target) in enumerate(found)
        ]

    def rows_of(quarter, which):
        eighth = (quarter ^ quarter_here) * 2 + which
        return pl.multiple_of(slot_of(eighth ^ eighth_here) * SLOT, SLOT)

    @pl.when(step == 0)
    def _():
        for copy in fetches(0):
            copy.start()
        for batch in range(count):
            rows = slice(batch * MB_TOK, batch * MB_TOK + MB_TOK)
            normed_turned[:, rows] = normed[batch][...].T
            cotangent_turned[:, rows] = cotangent[rows, :].T
        for copy in fetches(0):
            copy.wait()

    @pl.when(step == 1)
    def _():
        for copy in fetches(1):
            copy.wait()

    for core in range(2):
        lanes = slice(core * PACK, core * PACK + PACK)
        for quarter in range(REPS):
            lefts, rights = left_right(
                down_raw[core, side_here, quarter], down_raw[core, 1 - side_here, quarter]
            )
            down_out[0, pl.ds(rows_of(quarter, 0), SLOT), lanes] = lefts
            down_out[0, pl.ds(rows_of(quarter, 1), SLOT), lanes] = rights

    gate_weights = w_gate[...].reshape(WIDE, 2 * PACK)
    up_weights = w_up[...].reshape(WIDE, 2 * PACK)
    for batch in range(count):
        rows = slice(batch * MB_TOK, batch * MB_TOK + MB_TOK)
        gate = dot_nn(normed[batch][...], gate_weights)
        up = dot_nn(normed[batch][...], up_weights)
        d_hidden = dot_nn(cotangent[rows, :], down_out[0])
        sigmoid = 1.0 / (1.0 + jnp.exp(-gate))
        silu = gate * sigmoid
        hidden[0, rows, :] = (silu * up).astype(bf16)
        d_gate[0, rows, :] = (d_hidden * up * sigmoid * (1.0 + gate * (1.0 - sigmoid))).astype(bf16)
        d_up[0, rows, :] = (d_hidden * silu).astype(bf16)

    @pl.when(step == 0)
    def _():
        for copy in fetches(1):
            copy.start()

    @pl.when(step == 1)
    def _():
        for copy in results(0):
            copy.wait()

    for half in range(2):
        rows = slice(half * 512, half * 512 + 512)
        four = slice(half * 4, half * 4 + 4)
        gate_part = dot_nn(normed_turned[rows, :], d_gate[0]).astype(bf16)
        up_part = dot_nn(normed_turned[rows, :], d_up[0]).astype(bf16)
        for core in range(2):
            lanes = slice(core * PACK, core * PACK + PACK)
            grad_gate[core, four] = gate_part[:, lanes].reshape(4, SLOT, PACK)
            grad_up[core, four] = up_part[:, lanes].reshape(4, SLOT, PACK)
        grad_down[rows, :] = dot_nn(cotangent_turned[rows, :], hidden[0])
    for core in range(2):
        lanes = slice(core * PACK, core * PACK + PACK)
        for quarter in range(REPS):
            lefts, rights = left_right(
                grad_down[pl.ds(rows_of(quarter, 0), SLOT), lanes],
                grad_down[pl.ds(rows_of(quarter, 1), SLOT), lanes],
            )
            down_made[core, side_here, quarter] = lefts
            down_made[core, 1 - side_here, quarter] = rights
    for at in range(2):

        @pl.when(step == at)
        def _():
            for copy in results(at):
                copy.start()

    @pl.when(step == 1)
    def _():
        for copy in results(1):
            copy.wait()


def chunk_block(rows, columns):
    return pl.BlockSpec((1, rows, columns), lambda i: (i, 0, 0))


def mlp(here, normed, cotangent, parts):
    count = len(normed)
    tokens = cotangent.shape[0]
    rows = jax.ShapeDtypeStruct((2, tokens, 2 * PACK), bf16)
    part = jax.ShapeDtypeStruct((4, 2, SLOTS, ROWS_M, PACK), bf16)
    return pl.pallas_call(
        lambda *refs: mlp_kernel(*refs, count=count),
        grid=(2,),
        in_specs=[pl.BlockSpec(memory_space=pltpu.SMEM)]
        + [whole_block((MB_TOK, WIDE))] * count
        + [whole_block((tokens, WIDE))]
        + [anywhere()] * 8,
        out_specs=[chunk_block(tokens, 2 * PACK)] * 3
        + [chunk_block(WIDE, 2 * PACK)]
        + [anywhere()] * 2,
        out_shape=[rows, rows, rows, jax.ShapeDtypeStruct((2, WIDE, 2 * PACK), bf16), part, part],
        scratch_shapes=[
            pltpu.VMEM((SLOTS, SLOT, 2 * PACK), bf16),
            pltpu.VMEM((SLOTS, SLOT, 2 * PACK), bf16),
            pltpu.VMEM((2, 2, REPS, SLOT, PACK), bf16),
            pltpu.VMEM((WIDE, tokens), bf16),
            pltpu.VMEM((WIDE, tokens), bf16),
            pltpu.VMEM((2, SLOTS, SLOT, PACK), bf16),
            pltpu.VMEM((2, SLOTS, SLOT, PACK), bf16),
            pltpu.VMEM((WIDE, 2 * PACK), f32),
            pltpu.VMEM((2, 2, REPS, SLOT, PACK), bf16),
            pltpu.SemaphoreType.DMA((8,)),
            pltpu.SemaphoreType.DMA((16,)),
            pltpu.SemaphoreType.DMA((44,)),
        ],
        compiler_params=pltpu.CompilerParams(vmem_limit_bytes=VMEM_BYTES),
        cost_estimate=pl.CostEstimate(
            flops=30_000_000_000, bytes_accessed=50_000_000, transcendentals=2_000_000
        ),
        name="mlp",
    )(here, *normed, cotangent, *parts)


def mlp_outputs_kernel(hidden, d_gate, d_up, w_down, *refs, count):
    parts = refs[:8]
    outs, d_normed = (refs[8 : 8 + count], refs[8 + count : 8 + 2 * count])
    w_gate, w_up, sem_pair = refs[8 + 2 * count :]
    step = pl.program_id(0)

    def fetches(at):
        return pair_fetches(parts, at, w_gate.at[at], w_up.at[at], sem_pair.at[at])

    @pl.when(step == 0)
    def _():
        for at in range(2):
            for copy in fetches(at):
                copy.start()

    for at in range(2):

        @pl.when(step == at)
        def _():
            for copy in fetches(at):
                copy.wait()
            gate_weights = w_gate[at].reshape(WIDE, 2 * PACK)
            up_weights = w_up[at].reshape(WIDE, 2 * PACK)
            for batch in range(count):
                rows = slice(batch * MB_TOK, batch * MB_TOK + MB_TOK)
                out_part = dot_nt(hidden[0, rows, :], w_down[0])
                normed_part = dot_nt(d_gate[0, rows, :], gate_weights) + dot_nt(
                    d_up[0, rows, :], up_weights
                )
                if at == 0:
                    outs[batch][...] = out_part
                    d_normed[batch][...] = normed_part
                else:
                    outs[batch][...] += out_part
                    d_normed[batch][...] += normed_part


def mlp_outputs(hidden, d_gate, d_up, w_down, parts):
    tokens = hidden.shape[1]
    count = tokens // MB_TOK
    outs = pl.pallas_call(
        lambda *refs: mlp_outputs_kernel(*refs, count=count),
        grid=(2,),
        in_specs=[chunk_block(tokens, 2 * PACK)] * 3
        + [chunk_block(WIDE, 2 * PACK)]
        + [anywhere()] * 8,
        out_specs=[whole_block((MB_TOK, WIDE))] * (2 * count),
        out_shape=[jax.ShapeDtypeStruct((MB_TOK, WIDE), f32)] * (2 * count),
        scratch_shapes=[
            pltpu.VMEM((2, SLOTS, SLOT, 2 * PACK), bf16),
            pltpu.VMEM((2, SLOTS, SLOT, 2 * PACK), bf16),
            pltpu.SemaphoreType.DMA((2, 8)),
        ],
        compiler_params=pltpu.CompilerParams(vmem_limit_bytes=VMEM_BYTES),
        cost_estimate=pl.CostEstimate(
            flops=15_000_000_000, bytes_accessed=35_000_000, transcendentals=0
        ),
        name="mlp_outputs",
    )(hidden, d_gate, d_up, w_down, *parts)
    return (outs[:count], outs[count:])


def attn_backward_kernel(
    here,
    cotangent,
    middle,
    d_normed_two,
    inputs,
    query_rot,
    key_both,
    value_both,
    probs_in,
    cosines,
    sines,
    *refs,
):
    parts = refs[:8]
    (
        token_grad,
        wire_in,
        wire_out,
        gain_sums,
        attn_all,
        slots,
        head_parts,
        key_parts,
        value_parts,
        d_mixed_heads,
        sems,
    ) = refs[8:]
    eighth_here, quarter_here = (here[0], here[1])
    fetches = attn_fetches(parts, attn_all, sems)
    for copy in fetches:
        copy.start()
    mid = middle[...]
    upstream = d_normed_two[...]
    scale_two = lax.rsqrt(jnp.sum(mid * mid, axis=1, keepdims=True) * (1.0 / D) + norm_epsilon)
    term_two = jnp.sum(upstream * mid * scale_two, axis=0, keepdims=True)
    for copy in fetches:
        copy.wait()
    gain_one, gain_two = (gain_row(attn_all, 0), gain_row(attn_all, 1))
    weighted = upstream * gain_two
    inner = jnp.sum(weighted * mid, axis=1, keepdims=True) * (1.0 / D)
    d_middle = (
        cotangent[...].astype(f32)
        + scale_two * weighted
        - mid * scale_two * scale_two * scale_two * inner
    )
    for s in range(SLOTS):
        slots[s] = d_middle[:, s * SLOT : s * SLOT + SLOT]

    def slot_at(eighth):
        return slots[slot_of(eighth ^ eighth_here)]

    for quarter in range(REPS):
        first = (quarter ^ quarter_here) * 2
        tiles = laid(
            [([slot_at(first)], 0, 16, USED), ([slot_at(first + 1)], 0, 16 + USED, USED)], MB_TOK, 2
        )
        wire_out[:, quarter * 256 : quarter * 256 + 256] = joined(tiles).astype(bf16)
    output_columns = joined([block_columns(attn_all, q, 384, 640) for q in range(REPS)])
    d_mixed = dot_nt(wire_out[...], output_columns)
    for s in range(SLOTS):
        slots[s] = d_mixed[:, s * SLOT : s * SLOT + SLOT]
    tiles = laid([([slot_at(e)], 0, USED * e, USED) for e in range(SLOTS)], MB_TOK, 8)
    for c in range(8):
        d_mixed_heads[:, c * 128 : c * 128 + 128] = tiles[c].astype(bf16)
    for j in range(KV_HEADS):
        at = slice(j * 128, j * 128 + 128)
        for part in (2, 1, 0):
            keys = 128 * (part + 1)
            rows = slice(part * 128, part * 128 + 128)

            def three(ref):
                return jnp.concatenate(
                    [
                        only_half(ref[rows, (h // 2) * 128 : (h // 2) * 128 + 128], h % 2)
                        for h in range(3 * j, 3 * j + 3)
                    ],
                    axis=0,
                )

            queries = three(query_rot)
            d_mix = three(d_mixed_heads)
            probs = probs_in[j, :, probs_at(part) : probs_at(part) + keys]
            probs_f = probs.astype(f32)
            d_probs = dot_nt(d_mix, value_both[0:keys, at])
            product = probs_f * d_probs
            d_scores = product - probs_f * jnp.sum(product, axis=1, keepdims=True)
            d_scores = d_scores.astype(bf16)
            d_query = dot_nn(d_scores, key_both[0:keys, at])
            for g in range(GROUP):
                head_parts[3 * j + g, rows, :] = d_query[g * 128 : g * 128 + 128]
            d_key = dot_tn(d_scores, queries)
            d_value = dot_tn(probs, d_mix)
            if part == 2:
                key_parts[j] = d_key
                value_parts[j] = d_value
            else:
                key_parts[j, 0:keys, :] += d_key
                value_parts[j, 0:keys, :] += d_value

    low = lane_index((MB_TOK, 128)) < 64
    cosine, sine = (cosines[...], sines[...])
    empty = jnp.zeros((MB_TOK, 128), f32)

    def paired_heads(parts_of, count, c):
        return jnp.where(low, parts_of(2 * c), parts_of(2 * c + 1) if 2 * c + 1 < count else empty)

    def summed(ref):
        return lambda j: ref[j] + pltpu.roll(ref[j], 64, 1)

    query_tiles = [
        turned(paired_heads(lambda h: head_parts[h], HEADS, c) * HEAD**-0.5, cosine, -sine)
        for c in range(8)
    ]
    key_tiles = [
        turned(paired_heads(summed(key_parts), KV_HEADS, c) * HEAD**-0.5, cosine, -sine)
        for c in range(3)
    ]
    value_tiles = [paired_heads(summed(value_parts), KV_HEADS, c) for c in range(3)]
    for r in range(REPS):
        tiles = laid(
            [
                (query_tiles, 240 * r, 0, 240),
                (key_tiles, 80 * r, 240, 80),
                (value_tiles, 80 * r, 320, 80),
            ],
            MB_TOK,
            4,
        )
        wire_in[r ^ quarter_here] = joined(tiles).astype(bf16)
    d_normed = sum(
        dot_nt(wire_in[quarter], block_columns(attn_all, quarter, 0, 512))
        for quarter in range(REPS)
    )
    values = inputs[...].astype(f32)
    scale = lax.rsqrt(jnp.sum(values * values, axis=1, keepdims=True) * (1.0 / D) + norm_epsilon)
    weighted = d_normed * gain_one
    inner = jnp.sum(weighted * values, axis=1, keepdims=True) * (1.0 / D)
    term_one = jnp.sum(d_normed * values * scale, axis=0, keepdims=True)
    total = d_middle + scale * weighted - values * scale * scale * scale * inner
    token_grad[...] = total.astype(bf16)
    gain_sums[0:1, :] = term_one
    gain_sums[1:2, :] = term_two


def attn_grads_kernel(*refs, count):
    normed, mixed, wires_in, wires_out, gain_parts = [
        refs[n * count : n * count + count] for n in range(5)
    ]
    arrays = refs[5 * count : 5 * count + 2]
    gain_sums = sum(part[0:8, :] for part in gain_parts)

    def stacked(parts, *at):
        return jnp.concatenate([part[at] for part in parts], axis=0)

    normed_turned = stacked(normed, ...).T
    mixed_turned = stacked(mixed, ...).T
    wire_out = stacked(wires_out, ...)
    row = lax.broadcasted_iota(jnp.int32, (SLOTS, 16, SLOT), 1)
    gain_rows = jnp.zeros((SLOTS, 16, SLOT), f32)
    for which in range(2):
        spots = [
            gain_sums[which : which + 1, s * SLOT : s * SLOT + SLOT].reshape(1, 1, SLOT)
            for s in range(SLOTS)
        ]
        gain_rows = jnp.where(row == 8 + which, jnp.concatenate(spots, axis=0), gain_rows)
    for quarter in range(REPS):
        first = dot_nn(normed_turned, stacked(wires_in, quarter))
        second = dot_nn(mixed_turned, wire_out[:, quarter * 256 : quarter * 256 + 256])
        block = jnp.concatenate(
            [first[:, 0:384], first[:, 384:512] + second[:, 0:128], second[:, 128:256]], axis=1
        ).reshape(SLOTS, SLOT, PACK)
        y, core = (quarter >> 1, quarter & 1)
        low_rows = block[:, 0:ROWS_A, :].astype(bf16)
        high_rows = block[:, ROWS_A:SLOT, :].astype(bf16)
        target = arrays[core]
        target[0, y, :, :, :] = low_rows
        tail = (block[:, 112:SLOT, 0:SLOT] + gain_rows).astype(bf16)
        for side in range(2):
            slots = slice(side * 4, side * 4 + 4)
            target[1, side, y * 4 : y * 4 + 4, :, :] = high_rows[slots]
            target[1, side, y * 4 : y * 4 + 4, 48:64, 0:SLOT] = tail[slots]


def attn_backward(
    batch,
    here,
    cotangent,
    middle,
    d_normed_two,
    inputs,
    query_rot,
    key_both,
    value_both,
    probs,
    tables,
    parts,
):
    one = [middle, d_normed_two]
    own = [query_rot, key_both, value_both, probs]
    outs = [
        ((MB_TOK, WIDE), bf16),
        ((REPS, MB_TOK, 512), bf16),
        ((MB_TOK, REPS * 256), bf16),
        ((8, WIDE), f32),
    ]
    return pl.pallas_call(
        attn_backward_kernel,
        grid=(1,),
        in_specs=[in_scalars(), batch_block(batch, WIDE)]
        + [whole_block(array.shape) for array in one]
        + [batch_block(batch, WIDE)]
        + [whole_block(array.shape) for array in own]
        + [batch_block(batch, 128)] * 2
        + [anywhere()] * 8,
        out_specs=[whole_block(out[0]) for out in outs],
        out_shape=[jax.ShapeDtypeStruct(*out) for out in outs],
        scratch_shapes=[
            pltpu.VMEM((REPS, SLOTS, SLOT, PACK), bf16),
            pltpu.VMEM((SLOTS, MB_TOK, SLOT), f32),
            pltpu.VMEM((HEADS, MB_TOK, 128), f32),
            pltpu.VMEM((KV_HEADS, MB_TOK, 128), f32),
            pltpu.VMEM((KV_HEADS, MB_TOK, 128), f32),
            pltpu.VMEM((MB_TOK, WIDE), bf16),
            pltpu.SemaphoreType.DMA((12,)),
        ],
        compiler_params=pltpu.CompilerParams(vmem_limit_bytes=VMEM_BYTES),
        cost_estimate=pl.CostEstimate(
            flops=12_000_000_000, bytes_accessed=20_000_000, transcendentals=0
        ),
        name="attn_backward",
    )(here, cotangent, *one, inputs, *own, *tables, *parts)


def attn_grads(normed, mixed, wires_in, wires_out, gain_parts):
    count = len(normed)
    half = jax.ShapeDtypeStruct((2, 2, SLOTS, ROWS_A, PACK), bf16)
    arrays = (*normed, *mixed, *wires_in, *wires_out, *gain_parts)
    return pl.pallas_call(
        lambda *refs: attn_grads_kernel(*refs, count=count),
        grid=(1,),
        in_specs=[whole_block(array.shape) for array in arrays],
        out_specs=[whole_block(half.shape)] * 2,
        out_shape=[half] * 2,
        compiler_params=pltpu.CompilerParams(vmem_limit_bytes=VMEM_BYTES),
        cost_estimate=pl.CostEstimate(
            flops=8_000_000_000, bytes_accessed=14_000_000, transcendentals=0
        ),
        name="attn_grads",
    )(*arrays)


X_SIDE = ("fsdp", 1)
Y_SIDE = ("rep", 2)
CORE = ("rep", 1)


def swap_with(values, step):
    axis, mask = step
    count = lax.axis_size(axis)
    return lax.ppermute(values, axis, [(i, i ^ mask) for i in range(count)])


def after(values, *done):
    return lax.optimization_barrier((values, done))[0]


def sent_along_z(block):
    return [swap_with(block, ("fsdp", 2 * k)) for k in range(1, 4)]


def along_z(block, came):
    return jnp.stack([block] + list(came))


def sides_of(side_first):
    return (X_SIDE, Y_SIDE) if side_first else (Y_SIDE, X_SIDE)


def sent_along_first(four, side_first):
    return swap_with(four, sides_of(side_first)[0])


def along_first(four, side_first):
    return jnp.concatenate([four, sent_along_first(four, side_first)])


def along_second(eight, side_first):
    return swap_with(eight, sides_of(side_first)[1])


def along_core(eight, across):
    return (eight, swap_with(eight, CORE), across, swap_with(across, CORE))


def added(left, right):
    return (left.astype(f32) + right.astype(f32)).astype(bf16)


class Reduction:
    def __init__(self, kept, came, which, side_first):
        self.kept = kept
        self.came = came
        self.which = which
        self.first, self.second = sides_of(side_first)
        self.out = added(kept[which, 1], came[which, 1])

    def sent_second(self):
        return swap_with(self.out, self.second)

    def over_second(self, came):
        kept, before = after((self.kept, self.came), came)
        eight = added(kept[self.which, 0], before[self.which, 0])
        self.out = added(eight[4:8], came[4:8])
        self.four = added(eight[0:4], came[0:4])

    def sent_first(self):
        return swap_with(self.out, self.first)

    def over_first(self, came):
        self.blocks = [added(self.four[k], came[k]) for k in range(4)]


def z_stage(one, two):
    blocks = [jnp.concatenate([one.blocks[k], two.blocks[k]], axis=0) for k in range(4)]
    return (blocks[0], [swap_with(blocks[k], ("fsdp", 2 * k)) for k in range(1, 4)])


def z_sum(kept, came):
    return sum((block.astype(f32) for block in came), kept.astype(f32))


def split_parts(blocks, side_first):
    rows, columns = blocks.shape[2:]
    grid = blocks.reshape(4, 2, 2, 2, rows, columns)
    parts = []
    for second in range(2):
        for core in range(2):
            if side_first:
                part = grid[:, :, second, core].transpose(1, 0, 2, 3)
            else:
                part = grid[:, second, :, core].transpose(1, 0, 2, 3)
            parts.append(part.reshape(SLOTS, rows, columns))
    return parts


def eight_parts(first_blocks, second_blocks):
    return (*split_parts(first_blocks, True), *split_parts(second_blocks, False))


def join_parts(kept, sent, side_first):
    rows, columns = kept.shape[2:]
    grid = jnp.stack([kept, sent]).reshape(2, 2, 2, 4, rows, columns)
    grid = grid.transpose(3, 2, 1, 0, 4, 5) if side_first else grid.transpose(3, 1, 2, 0, 4, 5)
    return grid.reshape(SLOTS, REPS, rows, columns)


def attn_block(w_query, w_key, w_value, w_output, attn_gain, mlp_gain):
    matrices = jnp.concatenate([w_query, w_key, w_value, w_output], axis=1)
    gains = jnp.stack([attn_gain, mlp_gain])
    gains = jnp.pad(gains, ((0, SLOT - USED - 2), (0, PACK - USED)))
    return jnp.concatenate([matrices, gains], axis=0)


def down_block(w_down):
    halves = w_down.T.reshape(2, USED, HALF_PACK)
    halves = jnp.concatenate([halves[0], halves[1]], axis=1)
    return jnp.pad(halves, ((0, SLOT - USED), (0, 0)))


def mlp_block(w_gate, w_up, w_down):
    taller = ((0, SLOT - USED), (0, 0))
    return jnp.concatenate([jnp.pad(w_gate, taller), jnp.pad(w_up, taller), down_block(w_down)])


def down_of(block):
    halves = jnp.stack([block[:USED, :HALF_PACK], block[:USED, HALF_PACK:]])
    return halves.reshape(2 * USED, HALF_PACK).T


def whole(shard):
    return lax.all_gather(lax.all_gather(shard, "rep", axis=1, tiled=True), "fsdp", axis=0, tiled=True)


def cut(matrix, eighth, quarter):
    rows, columns = (matrix.shape[0] // SLOTS, matrix.shape[1] // REPS)
    return matrix[
        eighth * rows : eighth * rows + rows, quarter * columns : quarter * columns + columns
    ]


def every_block(make):
    return jnp.stack(
        [jnp.stack([make(e, q) for q in range(REPS)]) for e in range(SLOTS)]
    )


def owned(blocks):
    eighths, quarters, rows, columns = blocks.shape
    matrix = blocks.transpose(0, 2, 1, 3).reshape(eighths * rows, quarters * columns)
    part = lax.psum_scatter(matrix, "fsdp", scatter_dimension=0, tiled=True)
    return lax.psum_scatter(part, "rep", scatter_dimension=1, tiled=True).astype(f32)


def per_device(
    tokens,
    lengths,
    attn_gain,
    w_query,
    w_key,
    w_value,
    w_output,
    mlp_gain,
    w_gate,
    w_up,
    w_down,
    cotangent,
):
    paired = lax.axis_size("fsdp") == SLOTS and lax.axis_size("rep") == REPS
    if paired:
        eighth_here = lax.axis_index("fsdp").astype(jnp.int32)
        quarter_here = lax.axis_index("rep").astype(jnp.int32)
    else:
        eighth_here = jnp.int32(0)
        quarter_here = jnp.int32(0)
    here = jnp.stack([eighth_here, quarter_here])
    spread = spreading(eighth_here)
    segments, positions = jax.vmap(layout)(lengths)
    tables = rope_tables(positions.reshape(-1))
    inputs = jnp.dot(tokens, spread, preferred_element_type=f32).astype(bf16)
    upstream = jnp.dot(cotangent, spread, preferred_element_type=f32).astype(bf16)
    batches = range(tokens.shape[0] // MB_TOK)
    forward_inputs = [inputs for _ in batches]

    if paired:
        attn_pack = attn_block(w_query, w_key, w_value, w_output, attn_gain, mlp_gain)
        pack = mlp_block(w_gate, w_up, w_down)
        attn_four = along_z(attn_pack, sent_along_z(attn_pack))
        three, four, attn_four = lax.optimization_barrier((pack[:ROWS_W], pack[ROWS_W:], attn_four))
        three_came = sent_along_z(three)
        one, two = (attn_four[:, :ROWS_A], attn_four[:, ROWS_A:])
        came = (sent_along_first(one, True), sent_along_first(two, False))
        three_came, came, four = lax.optimization_barrier((three_came, came, four))
        one, two = (jnp.concatenate([one, came[0]]), jnp.concatenate([two, came[1]]))
        four_came = sent_along_z(four)
        across = (along_second(one, True), along_second(two, False))
        four_came, across = lax.optimization_barrier((four_came, across))
        three, four = (along_z(three, three_came), along_z(four, four_came))
        attn_parts = (*along_core(one, across[0]), *along_core(two, across[1]))
        three, four = (along_first(three, True), along_first(four, False))
        across = (along_second(three, True), along_second(four, False))
        forward_inputs[0] = after(inputs, three, four, upstream)
    else:
        gain_one, gain_two = (
            lax.all_gather(attn_gain, "fsdp", axis=0, tiled=True).reshape(SLOTS, USED),
            lax.all_gather(mlp_gain, "fsdp", axis=0, tiled=True).reshape(SLOTS, USED),
        )
        mats = [whole(w) for w in (w_query, w_key, w_value, w_output, w_gate, w_up, w_down)]
        attn_blocks = every_block(
            lambda e, q: attn_block(*[cut(m, e, q) for m in mats[:4]], gain_one[e], gain_two[e])
        )
        attn_parts = eight_parts(attn_blocks[:, :, :ROWS_A], attn_blocks[:, :, ROWS_A:])
        mlp_blocks = every_block(
            lambda e, q: mlp_block(cut(mats[4], e, q), cut(mats[5], e, q), cut(mats[6], e, q))
        )
        mlp_parts = eight_parts(mlp_blocks[:, :, :ROWS_W], mlp_blocks[:, :, ROWS_W:])

    made = [
        attn_forward(batch, here, forward_inputs[batch], attn_parts, tables, segments)
        for batch in batches
    ]
    normed, query_rot, key_both, value_both, probs, mixed, middle, normed_two = zip(*made)
    if paired:
        three, four = after((three, four), normed_two[0])
        across = after(across, normed_two[-1])
        mlp_parts = (*along_core(three, across[0]), *along_core(four, across[1]))
    hidden, d_gate, d_up, w_down_all, kept, sent = mlp(
        here, normed_two, upstream, mlp_parts
    )
    mlp_out, d_normed_two = mlp_outputs(hidden, d_gate, d_up, w_down_all, mlp_parts)
    d_normed_two = list(d_normed_two)
    if paired:
        came = swap_with(sent, CORE)
        gate_sums = [Reduction(kept, came, which, which == 0) for which in range(2)]
        up_sums = [Reduction(kept, came, 2 + which, which == 0) for which in range(2)]
        d_normed_two[0] = after(d_normed_two[0], gate_sums[0].out, gate_sums[1].out)
    back = []
    for batch in batches:
        back.append(
            attn_backward(
                batch,
                here,
                upstream,
                middle[batch],
                d_normed_two[batch],
                inputs,
                query_rot[batch],
                key_both[batch],
                value_both[batch],
                probs[batch],
                tables,
                attn_parts,
            )
        )
        if paired and batch == 0:
            for part in gate_sums:
                part.over_second(part.sent_second())
            for part in up_sums:
                part.out = after(part.out, gate_sums[0].out, gate_sums[1].out)
            d_normed_two[-1] = after(d_normed_two[-1], up_sums[0].out, up_sums[1].out)
    token_rows, wires_in, wires_out, gain_parts = zip(*back)
    if paired:
        for part in up_sums:
            part.over_second(part.sent_second())
        for part in gate_sums:
            part.over_first(part.sent_first())
        wires_in = after(
            wires_in, up_sums[0].out, up_sums[1].out, gate_sums[0].blocks, gate_sums[1].blocks
        )
    attn_kept, attn_sent = attn_grads(
        normed, mixed, wires_in, wires_out, gain_parts
    )
    if paired:
        up_came = [part.sent_first() for part in up_sums]
        gate_kept, gate_came = z_stage(*gate_sums)
        up_came, gate_came, attn_sent = lax.optimization_barrier((up_came, gate_came, attn_sent))
        came = swap_with(attn_sent, CORE)
        for part, part_came in zip(up_sums, up_came):
            part.over_first(part_came)
        one, two = [Reduction(attn_kept, came, which, which == 0) for which in range(2)]
        up_kept, up_came = z_stage(*up_sums)
        across = (one.sent_second(), two.sent_second())
        up_came, across = lax.optimization_barrier((up_came, across))
        tail = across
        one.over_second(across[0])
        two.over_second(across[1])
        one.over_first(one.sent_first())
        two.over_first(two.sent_first())
        gate_sum = z_sum(gate_kept, gate_came)
        up_sum = z_sum(up_kept, up_came)
        attn_sum = z_sum(*z_stage(one, two))
        gain_sums = (attn_sum[USED, :USED], attn_sum[USED + 1, :USED])
        attn_sum = attn_sum[:USED]
        grads = [
            attn_sum[:, 0:240],
            attn_sum[:, 240:320],
            attn_sum[:, 320:400],
            attn_sum[:, 400:640],
            gate_sum[:USED],
            up_sum[:USED],
            down_of(jnp.concatenate([gate_sum[SLOT:], up_sum[SLOT:]], axis=0)),
        ]
    else:
        tail = (attn_kept,)
        attn_blocks = jnp.concatenate(
            [join_parts(attn_kept[k], attn_sent[k], k == 0) for k in range(2)], axis=2
        )
        gain_sums = tuple(
            lax.psum(
                lax.psum_scatter(
                    attn_blocks[:, 0, USED + which, :USED].astype(f32).reshape(D),
                    "fsdp",
                    scatter_dimension=0,
                    tiled=True,
                ),
                "rep",
            )
            for which in range(2)
        )
        attn_blocks = attn_blocks[:, :, :USED]
        gate_blocks, up_blocks = [
            jnp.concatenate(
                [join_parts(kept[k], sent[k], k % 2 == 0) for k in (which, which + 1)], axis=2
            )
            for which in (0, 2)
        ]
        down_blocks = jnp.concatenate([gate_blocks[:, :, SLOT:], up_blocks[:, :, SLOT:]], axis=2)
        grads = [
            owned(attn_blocks[..., 0:240]),
            owned(attn_blocks[..., 240:320]),
            owned(attn_blocks[..., 320:400]),
            owned(attn_blocks[..., 400:640]),
            owned(gate_blocks[:, :, :USED]),
            owned(up_blocks[:, :, :USED]),
            owned(jax.vmap(jax.vmap(down_of))(down_blocks)),
        ]
    middle, mlp_out, token_rows = after((middle, mlp_out, token_rows), *tail)
    output_rows = jnp.concatenate(
        [(middle[batch] + mlp_out[batch]).astype(bf16) for batch in batches], axis=0
    )
    output = jnp.dot(output_rows, spread.T, preferred_element_type=f32).astype(bf16)
    token_grad = jnp.dot(
        jnp.concatenate(token_rows, axis=0), spread.T, preferred_element_type=f32
    ).astype(bf16)
    return (
        output,
        token_grad,
        gain_sums[0],
        grads[0],
        grads[1],
        grads[2],
        grads[3],
        gain_sums[1],
        grads[4],
        grads[5],
        grads[6],
    )


def solution(mesh):
    placed = (
        P(("fsdp", "rep"), None),
        P(("fsdp", "rep"), None),
        P("fsdp"),
        P("fsdp", "rep"),
        P("fsdp", "rep"),
        P("fsdp", "rep"),
        P("fsdp", "rep"),
        P("fsdp"),
        P("fsdp", "rep"),
        P("fsdp", "rep"),
        P("fsdp", "rep"),
        P(("fsdp", "rep"), None),
    )
    return jax.shard_map(
        per_device,
        mesh=mesh,
        in_specs=placed,
        out_specs=(
            P(("fsdp", "rep"), None),
            P(("fsdp", "rep"), None),
            P("fsdp"),
            P("fsdp", "rep"),
            P("fsdp", "rep"),
            P("fsdp", "rep"),
            P("fsdp", "rep"),
            P("fsdp"),
            P("fsdp", "rep"),
            P("fsdp", "rep"),
            P("fsdp", "rep"),
        ),
        check_vma=False,
    )
```

```python
import jax
import jax.numpy as jnp
from jax import lax
from jax.experimental import pallas as pl
from jax.experimental.pallas import tpu as pltpu
from jax.sharding import PartitionSpec as P

D = 960
FF = 2560
HEADS = 15
KV_HEADS = 5
HEAD = 64
MB_TOK = 384
SEGS = 3
GROUP = 3
QW = 960
KVW = 320

SLOTS = 8
REPS = 4
USED = 120
SLOT = 128
WIDE = SLOTS * SLOT
PACK = 640
HALF_PACK = 320
ROWS_A = 64
ROWS_M = 96
REST = SLOT - ROWS_M
ROWS_W = 192
VMEM_BYTES = 60 * 1024 * 1024

norm_epsilon = 1e-05
rope_base = 100000.0
masked_value = -1e30

f32 = jnp.float32
bf16 = jnp.bfloat16


def layout(length_row):
    starts = jnp.cumsum(length_row) - length_row
    places = jnp.arange(MB_TOK, dtype=jnp.int32)
    inside = (
        (places[:, None] >= starts[None, :]) & (places[:, None] < (starts + length_row)[None, :])
    ).astype(jnp.int32)
    segment = jnp.sum(inside * jnp.arange(SEGS, dtype=jnp.int32)[None, :], axis=1)
    position = places - jnp.sum(inside * starts[None, :], axis=1)
    return (segment, position)


def rope_tables(position):
    half_width = HEAD // 2
    exponent = jnp.arange(half_width, dtype=f32) * (2.0 / HEAD)
    inverse = jnp.power(rope_base, -exponent)
    angles = position.astype(f32)[:, None] * inverse
    cosines, sines = (jnp.cos(angles), jnp.sin(angles))
    return (
        jnp.concatenate([cosines] * 4, axis=1),
        jnp.concatenate([-sines, sines, -sines, sines], axis=1),
    )


def slot_of(eighth):
    return (eighth & 1) * 4 + (eighth >> 1)


def eighth_of(slot):
    return (slot & 3) * 2 + (slot >> 2)


def feature_lanes(eighth_here):
    lanes = jnp.arange(WIDE, dtype=jnp.int32)
    eighth = eighth_of(lanes // SLOT) ^ eighth_here
    return jnp.where(lanes % SLOT < USED, eighth * USED + lanes % SLOT, -1)


def spreading(eighth_here):
    features = jnp.arange(D, dtype=jnp.int32)
    return (features[:, None] == feature_lanes(eighth_here)[None, :]).astype(bf16)


def dot_nn(left, right):
    return lax.dot_general(left, right, (((1,), (0,)), ((), ())), preferred_element_type=f32)


def dot_nt(left, right):
    return lax.dot_general(left, right, (((1,), (1,)), ((), ())), preferred_element_type=f32)


def dot_tn(left, right):
    return lax.dot_general(left, right, (((0,), (0,)), ((), ())), preferred_element_type=f32)


def lane_index(shape):
    return lax.broadcasted_iota(jnp.int32, shape, len(shape) - 1)


def swapped(values):
    first = (lane_index(values.shape) & 63) < 32
    return jnp.where(first, pltpu.roll(values, 96, 1), pltpu.roll(values, 32, 1))


def turned(values, cosines, sines):
    return values * cosines + swapped(values) * sines


def both_halves(values, odd):
    low = lane_index(values.shape) < 64
    moved = pltpu.roll(values, 64, 1)
    return jnp.where(low, moved, values) if odd else jnp.where(low, values, moved)


def only_half(values, odd):
    low = lane_index(values.shape) < 64
    return jnp.where(low != bool(odd), values, jnp.zeros_like(values))


def laid(pieces, rows, tiles):
    lane = lane_index((rows, 128))
    made = [jnp.zeros((rows, 128), f32)] * tiles
    for source, start, target, width in pieces:
        shifted = {}
        done = 0
        while done < width:
            from_tile, from_lane = divmod(start + done, 128)
            to_tile, to_lane = divmod(target + done, 128)
            now = min(width - done, 128 - from_lane, 128 - to_lane)
            if from_tile not in shifted:
                values = source[from_tile]
                turn = (to_lane - from_lane) % 128
                shifted[from_tile] = pltpu.roll(values, turn, 1) if turn else values
            inside = (lane >= to_lane) & (lane < to_lane + now)
            made[to_tile] = jnp.where(inside, shifted[from_tile], made[to_tile])
            done += now
    return made


def tiles_of(values):
    return [values[:, t : t + 128] for t in range(0, values.shape[1], 128)]


def joined(tiles):
    return jnp.concatenate(tiles, axis=1)


def gain_row(attn_ref, which):
    rows = [attn_ref[0, s, 112:128, 0:SLOT].astype(f32)[8 + which : 9 + which] for s in range(SLOTS)]
    return jnp.concatenate(rows, axis=1)


def views(parts):
    return (parts[:4], parts[4:])


def attn_fetches(parts, attn_all, sems):
    copies = []
    firsts, seconds = views(parts)
    for quarter, source in enumerate(firsts):
        copies.append((source, attn_all.at[quarter, :, 0:ROWS_A, :]))
    for place, source in enumerate(seconds):
        side, core = (place >> 1, place & 1)
        for y in range(2):
            copies.append(
                (
                    source.at[y * 4 : y * 4 + 4],
                    attn_all.at[y * 2 + core, side * 4 : side * 4 + 4, ROWS_A : 2 * ROWS_A, :],
                )
            )
    return [
        pltpu.make_async_copy(source, target, sems.at[n])
        for n, (source, target) in enumerate(copies)
    ]


def block_columns(attn_all, quarter, low, high):
    return attn_all[quarter, :, :, low:high].reshape(WIDE, high - low)


def probs_at(part):
    return (0, 128, 384)[part]


def attn_forward_kernel(
    here,
    inputs,
    cosines,
    sines,
    segment_rows,
    segment_columns,
    *refs,
):
    parts = refs[:8]
    (
        normed_out,
        query_out,
        key_out,
        value_out,
        probs_out,
        mixed_out,
        middle_out,
        normed_two_out,
        attn_all,
        wire,
        heads_out,
        mixed_slots,
        out_slots,
        bias,
        sems,
    ) = refs[8:]
    eighth_here, quarter_here = (here[0], here[1])
    fetches = attn_fetches(parts, attn_all, sems)
    for copy in fetches:
        copy.start()
    values = inputs[...].astype(f32)
    scale = lax.rsqrt(jnp.sum(values * values, axis=1, keepdims=True) * (1.0 / D) + norm_epsilon)
    for copy in fetches:
        copy.wait()
    normed = (values * scale * gain_row(attn_all, 0)).astype(bf16)
    normed_out[...] = normed
    cosine, sine = (cosines[...], sines[...])
    for quarter in range(REPS):
        wire[quarter] = dot_nn(normed, block_columns(attn_all, quarter, 0, 512))
    sources = [
        [wire[r ^ quarter_here, :, t * 128 : t * 128 + 128] for t in range(4)] for r in range(REPS)
    ]
    query_tiles = laid([(sources[r], 0, 240 * r, 240) for r in range(REPS)], MB_TOK, 8)
    for c in range(8):
        query_out[:, c * 128 : c * 128 + 128] = turned(query_tiles[c], cosine, sine).astype(bf16)
    key_tiles = laid([(sources[r], 240, 80 * r, 80) for r in range(REPS)], MB_TOK, 3)
    value_tiles = laid([(sources[r], 320, 80 * r, 80) for r in range(REPS)], MB_TOK, 3)
    for c in range(3):
        key_part = turned(key_tiles[c], cosine, sine)
        for odd in range(2 if c < 2 else 1):
            at = slice((2 * c + odd) * 128, (2 * c + odd) * 128 + 128)
            key_out[:, at] = both_halves(key_part, odd).astype(bf16)
            value_out[:, at] = both_halves(value_tiles[c], odd).astype(bf16)

    query_place = lax.broadcasted_iota(jnp.int32, (MB_TOK, MB_TOK), 0)
    key_place = lax.broadcasted_iota(jnp.int32, (MB_TOK, MB_TOK), 1)
    seen = (segment_rows[...] == segment_columns[0]) & (key_place <= query_place)
    bias[...] = jnp.where(seen, 0.0, masked_value)
    for j in range(KV_HEADS):
        at = slice(j * 128, j * 128 + 128)
        for part in range(3):
            keys = 128 * (part + 1)
            rows = slice(part * 128, part * 128 + 128)
            queries = jnp.concatenate(
                [
                    only_half(query_out[rows, (h // 2) * 128 : (h // 2) * 128 + 128], h % 2)
                    for h in range(3 * j, 3 * j + 3)
                ],
                axis=0,
            )
            scores = dot_nt(queries, key_out[0:keys, at]) * HEAD**-0.5
            hidden_part = bias[rows, 0:keys]
            scores = scores + jnp.concatenate([hidden_part] * GROUP, axis=0)
            peak = jnp.max(scores, axis=1, keepdims=True)
            weights = jnp.exp(scores - peak)
            total = jnp.sum(weights, axis=1, keepdims=True)
            probs = (weights * (1.0 / total)).astype(bf16)
            probs_out[j, :, probs_at(part) : probs_at(part) + keys] = probs
            gathered = dot_nn(probs, value_out[0:keys, at])
            for g in range(GROUP):
                heads_out[3 * j + g, rows, :] = gathered[g * 128 : g * 128 + 128]
    low = lane_index((MB_TOK, 128)) < 64
    head_tiles = [
        jnp.where(
            low,
            heads_out[2 * c],
            heads_out[2 * c + 1] if 2 * c + 1 < HEADS else jnp.zeros((MB_TOK, 128), f32),
        )
        for c in range(8)
    ]
    for eighth in range(SLOTS):
        (slot_tile,) = laid([(head_tiles, USED * eighth, 0, USED)], MB_TOK, 1)
        mixed_slots[slot_of(eighth ^ eighth_here)] = slot_tile.astype(bf16)
    mixed = joined([mixed_slots[s] for s in range(SLOTS)])
    mixed_out[...] = mixed
    for quarter in range(REPS):
        part = tiles_of(dot_nn(mixed, block_columns(attn_all, quarter, 384, 640)))
        for which in range(2):
            eighth = (quarter ^ quarter_here) * 2 + which
            (slot_tile,) = laid([(part, 16 + USED * which, 0, USED)], MB_TOK, 1)
            out_slots[slot_of(eighth ^ eighth_here)] = slot_tile
    middle = values + joined([out_slots[s] for s in range(SLOTS)])
    middle_out[...] = middle
    scale_two = lax.rsqrt(
        jnp.sum(middle * middle, axis=1, keepdims=True) * (1.0 / D) + norm_epsilon
    )
    normed_two_out[...] = (middle * scale_two * gain_row(attn_all, 1)).astype(bf16)


def whole_block(shape):
    return pl.BlockSpec(
        shape, lambda *ids: (0,) * len(shape), pipeline_mode=pl.Buffered(buffer_count=1)
    )


def anywhere():
    return pl.BlockSpec(memory_space=pl.ANY)


def batch_block(batch, columns):
    return pl.BlockSpec((MB_TOK, columns), lambda i: (batch, 0))


def attn_scratch():
    return [
        pltpu.VMEM((REPS, SLOTS, SLOT, PACK), bf16),
        pltpu.VMEM((REPS, MB_TOK, 512), f32),
        pltpu.VMEM((HEADS, MB_TOK, 128), f32),
    ]


def in_scalars():
    return pl.BlockSpec(memory_space=pltpu.SMEM)


def attn_forward(batch, here, inputs, parts, tables, segments):
    count = inputs.shape[0] // MB_TOK
    outs = [
        ((MB_TOK, WIDE), bf16),
        ((MB_TOK, WIDE), bf16),
        ((MB_TOK, PACK), bf16),
        ((MB_TOK, PACK), bf16),
        ((KV_HEADS, MB_TOK, 768), bf16),
        ((MB_TOK, WIDE), bf16),
        ((MB_TOK, WIDE), f32),
        ((MB_TOK, WIDE), bf16),
    ]
    return pl.pallas_call(
        attn_forward_kernel,
        grid=(1,),
        in_specs=[
            in_scalars(),
            batch_block(batch, WIDE),
            batch_block(batch, 128),
            batch_block(batch, 128),
            batch_block(batch, 1),
            pl.BlockSpec((1, 1, MB_TOK), lambda i: (batch, 0, 0)),
        ]
        + [anywhere()] * 8,
        out_specs=[whole_block(out[0]) for out in outs],
        out_shape=[jax.ShapeDtypeStruct(*out) for out in outs],
        scratch_shapes=attn_scratch()
        + [
            pltpu.VMEM((SLOTS, MB_TOK, SLOT), bf16),
            pltpu.VMEM((SLOTS, MB_TOK, SLOT), f32),
            pltpu.VMEM((MB_TOK, MB_TOK), f32),
            pltpu.SemaphoreType.DMA((12,)),
        ],
        compiler_params=pltpu.CompilerParams(vmem_limit_bytes=VMEM_BYTES),
        cost_estimate=pl.CostEstimate(
            flops=8_000_000_000, bytes_accessed=16_000_000, transcendentals=2_000_000
        ),
        name="attn_forward",
    )(
        here,
        inputs,
        *tables,
        segments.reshape(-1, 1),
        segments.reshape(count, 1, MB_TOK),
        *parts,
    )


def left_right(left, right):
    first = lane_index(left.shape) < HALF_PACK
    left, right = (left.astype(f32), right.astype(f32))
    return (
        jnp.where(first, left, pltpu.roll(right, HALF_PACK, 1)).astype(bf16),
        jnp.where(first, pltpu.roll(left, HALF_PACK, 1), right).astype(bf16),
    )


def pair_fetches(parts, at, w_gate, w_up, sems):
    found = []
    firsts, seconds = views(parts)
    for core in range(2):
        lanes = slice(core * PACK, core * PACK + PACK)
        source = firsts[at * 2 + core]
        found.append((source.at[:, 0:SLOT, :], w_gate.at[:, :, lanes]))
        found.append((source.at[:, SLOT:ROWS_W, :], w_up.at[:, 0:64, lanes]))
        for side in range(2):
            found.append(
                (
                    seconds[side * 2 + core].at[at * 4 : at * 4 + 4, 0:64, :],
                    w_up.at[side * 4 : side * 4 + 4, 64:SLOT, lanes],
                )
            )
    return [
        pltpu.make_async_copy(source, target, sems.at[n])
        for n, (source, target) in enumerate(found)
    ]


def mlp_kernel(here, *refs, count):
    normed = refs[:count]
    cotangent = refs[count]
    parts = refs[count + 1 : count + 9]
    hidden, d_gate, d_up, down_out, kept, sent = refs[count + 9 : count + 15]
    (
        w_gate,
        w_up,
        down_raw,
        normed_turned,
        cotangent_turned,
        grad_gate,
        grad_up,
        grad_down,
        down_made,
        sem_pair,
        sem_down,
        sem_out,
    ) = refs[count + 15 :]
    step = pl.program_id(0)
    eighth_here, quarter_here = (here[0], here[1])
    side_here = eighth_here & 1

    def plane_of(at, core):
        return ((2 * at + core) ^ quarter_here) ^ (eighth_here >> 1)

    def fetches(at):
        found = []
        for core in range(2):
            for side in range(2):
                for quarter in range(REPS):
                    y, inner = (quarter >> 1, quarter & 1)
                    found.append(
                        (
                            views(parts)[1][side * 2 + inner].at[
                                y * 4 + plane_of(at, core), 64:ROWS_W
                            ],
                            down_raw.at[core, side, quarter],
                        )
                    )
        return pair_fetches(parts, at, w_gate, w_up, sem_pair) + [
            pltpu.make_async_copy(source, target, sem_down.at[n])
            for n, (source, target) in enumerate(found)
        ]

    def results(at):
        found = []
        for group, source in enumerate((grad_gate, grad_up)):
            firsts = (kept.at[2 * group], sent.at[2 * group])
            seconds = (kept.at[2 * group + 1], sent.at[2 * group + 1])
            for core in range(2):
                found.append((source.at[core, :, 0:ROWS_M], firsts[core].at[at]))
                for side in range(2):
                    found.append(
                        (
                            source.at[core, side * 4 : side * 4 + 4, ROWS_M:SLOT],
                            seconds[core].at[side, at * 4 : at * 4 + 4, 0:REST],
                        )
                    )
                    for quarter in range(REPS):
                        y, inner = (quarter >> 1, quarter & 1)
                        found.append(
                            (
                                down_made.at[
                                    core, side, quarter, group * ROWS_A : group * ROWS_A + ROWS_A
                                ],
                                seconds[inner].at[
                                    side, y * 4 + plane_of(at, core), REST:ROWS_M
                                ],
                            )
                        )
        return [
            pltpu.make_async_copy(source, target, sem_out.at[n])
            for n, (source, target) in enumerate(found)
        ]

    def rows_of(quarter, which):
        eighth = (quarter ^ quarter_here) * 2 + which
        return pl.multiple_of(slot_of(eighth ^ eighth_here) * SLOT, SLOT)

    @pl.when(step == 0)
    def _():
        for copy in fetches(0):
            copy.start()
        for batch in range(count):
            rows = slice(batch * MB_TOK, batch * MB_TOK + MB_TOK)
            normed_turned[:, rows] = normed[batch][...].T
            cotangent_turned[:, rows] = cotangent[rows, :].T
        for copy in fetches(0):
            copy.wait()

    @pl.when(step == 1)
    def _():
        for copy in fetches(1):
            copy.wait()

    for core in range(2):
        lanes = slice(core * PACK, core * PACK + PACK)
        for quarter in range(REPS):
            lefts, rights = left_right(
                down_raw[core, side_here, quarter], down_raw[core, 1 - side_here, quarter]
            )
            down_out[0, pl.ds(rows_of(quarter, 0), SLOT), lanes] = lefts
            down_out[0, pl.ds(rows_of(quarter, 1), SLOT), lanes] = rights

    gate_weights = w_gate[...].reshape(WIDE, 2 * PACK)
    up_weights = w_up[...].reshape(WIDE, 2 * PACK)
    for batch in range(count):
        rows = slice(batch * MB_TOK, batch * MB_TOK + MB_TOK)
        gate = dot_nn(normed[batch][...], gate_weights)
        up = dot_nn(normed[batch][...], up_weights)
        d_hidden = dot_nn(cotangent[rows, :], down_out[0])
        sigmoid = 1.0 / (1.0 + jnp.exp(-gate))
        silu = gate * sigmoid
        hidden[0, rows, :] = (silu * up).astype(bf16)
        d_gate[0, rows, :] = (d_hidden * up * sigmoid * (1.0 + gate * (1.0 - sigmoid))).astype(bf16)
        d_up[0, rows, :] = (d_hidden * silu).astype(bf16)

    @pl.when(step == 0)
    def _():
        for copy in fetches(1):
            copy.start()

    @pl.when(step == 1)
    def _():
        for copy in results(0):
            copy.wait()

    for half in range(2):
        rows = slice(half * 512, half * 512 + 512)
        four = slice(half * 4, half * 4 + 4)
        gate_part = dot_nn(normed_turned[rows, :], d_gate[0]).astype(bf16)
        up_part = dot_nn(normed_turned[rows, :], d_up[0]).astype(bf16)
        for core in range(2):
            lanes = slice(core * PACK, core * PACK + PACK)
            grad_gate[core, four] = gate_part[:, lanes].reshape(4, SLOT, PACK)
            grad_up[core, four] = up_part[:, lanes].reshape(4, SLOT, PACK)
        grad_down[rows, :] = dot_nn(cotangent_turned[rows, :], hidden[0])
    for core in range(2):
        lanes = slice(core * PACK, core * PACK + PACK)
        for quarter in range(REPS):
            lefts, rights = left_right(
                grad_down[pl.ds(rows_of(quarter, 0), SLOT), lanes],
                grad_down[pl.ds(rows_of(quarter, 1), SLOT), lanes],
            )
            down_made[core, side_here, quarter] = lefts
            down_made[core, 1 - side_here, quarter] = rights
    for at in range(2):

        @pl.when(step == at)
        def _():
            for copy in results(at):
                copy.start()

    @pl.when(step == 1)
    def _():
        for copy in results(1):
            copy.wait()


def chunk_block(rows, columns):
    return pl.BlockSpec((1, rows, columns), lambda i: (i, 0, 0))


def mlp(here, normed, cotangent, parts):
    count = len(normed)
    tokens = cotangent.shape[0]
    rows = jax.ShapeDtypeStruct((2, tokens, 2 * PACK), bf16)
    part = jax.ShapeDtypeStruct((4, 2, SLOTS, ROWS_M, PACK), bf16)
    return pl.pallas_call(
        lambda *refs: mlp_kernel(*refs, count=count),
        grid=(2,),
        in_specs=[pl.BlockSpec(memory_space=pltpu.SMEM)]
        + [whole_block((MB_TOK, WIDE))] * count
        + [whole_block((tokens, WIDE))]
        + [anywhere()] * 8,
        out_specs=[chunk_block(tokens, 2 * PACK)] * 3
        + [chunk_block(WIDE, 2 * PACK)]
        + [anywhere()] * 2,
        out_shape=[rows, rows, rows, jax.ShapeDtypeStruct((2, WIDE, 2 * PACK), bf16), part, part],
        scratch_shapes=[
            pltpu.VMEM((SLOTS, SLOT, 2 * PACK), bf16),
            pltpu.VMEM((SLOTS, SLOT, 2 * PACK), bf16),
            pltpu.VMEM((2, 2, REPS, SLOT, PACK), bf16),
            pltpu.VMEM((WIDE, tokens), bf16),
            pltpu.VMEM((WIDE, tokens), bf16),
            pltpu.VMEM((2, SLOTS, SLOT, PACK), bf16),
            pltpu.VMEM((2, SLOTS, SLOT, PACK), bf16),
            pltpu.VMEM((WIDE, 2 * PACK), f32),
            pltpu.VMEM((2, 2, REPS, SLOT, PACK), bf16),
            pltpu.SemaphoreType.DMA((8,)),
            pltpu.SemaphoreType.DMA((16,)),
            pltpu.SemaphoreType.DMA((44,)),
        ],
        compiler_params=pltpu.CompilerParams(vmem_limit_bytes=VMEM_BYTES),
        cost_estimate=pl.CostEstimate(
            flops=30_000_000_000, bytes_accessed=50_000_000, transcendentals=2_000_000
        ),
        name="mlp",
    )(here, *normed, cotangent, *parts)


def mlp_outputs_kernel(hidden, d_gate, d_up, w_down, *refs, count):
    parts = refs[:8]
    outs, d_normed = (refs[8 : 8 + count], refs[8 + count : 8 + 2 * count])
    w_gate, w_up, sem_pair = refs[8 + 2 * count :]
    step = pl.program_id(0)

    def fetches(at):
        return pair_fetches(parts, at, w_gate.at[at], w_up.at[at], sem_pair.at[at])

    @pl.when(step == 0)
    def _():
        for at in range(2):
            for copy in fetches(at):
                copy.start()

    for at in range(2):

        @pl.when(step == at)
        def _():
            for copy in fetches(at):
                copy.wait()
            gate_weights = w_gate[at].reshape(WIDE, 2 * PACK)
            up_weights = w_up[at].reshape(WIDE, 2 * PACK)
            for batch in range(count):
                rows = slice(batch * MB_TOK, batch * MB_TOK + MB_TOK)
                out_part = dot_nt(hidden[0, rows, :], w_down[0])
                normed_part = dot_nt(d_gate[0, rows, :], gate_weights) + dot_nt(
                    d_up[0, rows, :], up_weights
                )
                if at == 0:
                    outs[batch][...] = out_part
                    d_normed[batch][...] = normed_part
                else:
                    outs[batch][...] += out_part
                    d_normed[batch][...] += normed_part


def mlp_outputs(hidden, d_gate, d_up, w_down, parts):
    tokens = hidden.shape[1]
    count = tokens // MB_TOK
    outs = pl.pallas_call(
        lambda *refs: mlp_outputs_kernel(*refs, count=count),
        grid=(2,),
        in_specs=[chunk_block(tokens, 2 * PACK)] * 3
        + [chunk_block(WIDE, 2 * PACK)]
        + [anywhere()] * 8,
        out_specs=[whole_block((MB_TOK, WIDE))] * (2 * count),
        out_shape=[jax.ShapeDtypeStruct((MB_TOK, WIDE), f32)] * (2 * count),
        scratch_shapes=[
            pltpu.VMEM((2, SLOTS, SLOT, 2 * PACK), bf16),
            pltpu.VMEM((2, SLOTS, SLOT, 2 * PACK), bf16),
            pltpu.SemaphoreType.DMA((2, 8)),
        ],
        compiler_params=pltpu.CompilerParams(vmem_limit_bytes=VMEM_BYTES),
        cost_estimate=pl.CostEstimate(
            flops=15_000_000_000, bytes_accessed=35_000_000, transcendentals=0
        ),
        name="mlp_outputs",
    )(hidden, d_gate, d_up, w_down, *parts)
    return (outs[:count], outs[count:])


def attn_backward_kernel(
    here,
    cotangent,
    middle,
    d_normed_two,
    inputs,
    query_rot,
    key_both,
    value_both,
    probs_in,
    cosines,
    sines,
    *refs,
):
    parts = refs[:8]
    (
        token_grad,
        wire_in,
        wire_out,
        gain_sums,
        attn_all,
        slots,
        head_parts,
        key_parts,
        value_parts,
        d_mixed_heads,
        sems,
    ) = refs[8:]
    eighth_here, quarter_here = (here[0], here[1])
    fetches = attn_fetches(parts, attn_all, sems)
    for copy in fetches:
        copy.start()
    mid = middle[...]
    upstream = d_normed_two[...]
    scale_two = lax.rsqrt(jnp.sum(mid * mid, axis=1, keepdims=True) * (1.0 / D) + norm_epsilon)
    term_two = jnp.sum(upstream * mid * scale_two, axis=0, keepdims=True)
    for copy in fetches:
        copy.wait()
    gain_one, gain_two = (gain_row(attn_all, 0), gain_row(attn_all, 1))
    weighted = upstream * gain_two
    inner = jnp.sum(weighted * mid, axis=1, keepdims=True) * (1.0 / D)
    d_middle = (
        cotangent[...].astype(f32)
        + scale_two * weighted
        - mid * scale_two * scale_two * scale_two * inner
    )
    for s in range(SLOTS):
        slots[s] = d_middle[:, s * SLOT : s * SLOT + SLOT]

    def slot_at(eighth):
        return slots[slot_of(eighth ^ eighth_here)]

    for quarter in range(REPS):
        first = (quarter ^ quarter_here) * 2
        tiles = laid(
            [([slot_at(first)], 0, 16, USED), ([slot_at(first + 1)], 0, 16 + USED, USED)], MB_TOK, 2
        )
        wire_out[:, quarter * 256 : quarter * 256 + 256] = joined(tiles).astype(bf16)
    output_columns = joined([block_columns(attn_all, q, 384, 640) for q in range(REPS)])
    d_mixed = dot_nt(wire_out[...], output_columns)
    for s in range(SLOTS):
        slots[s] = d_mixed[:, s * SLOT : s * SLOT + SLOT]
    tiles = laid([([slot_at(e)], 0, USED * e, USED) for e in range(SLOTS)], MB_TOK, 8)
    for c in range(8):
        d_mixed_heads[:, c * 128 : c * 128 + 128] = tiles[c].astype(bf16)
    for j in range(KV_HEADS):
        at = slice(j * 128, j * 128 + 128)
        for part in (2, 1, 0):
            keys = 128 * (part + 1)
            rows = slice(part * 128, part * 128 + 128)

            def three(ref):
                return jnp.concatenate(
                    [
                        only_half(ref[rows, (h // 2) * 128 : (h // 2) * 128 + 128], h % 2)
                        for h in range(3 * j, 3 * j + 3)
                    ],
                    axis=0,
                )

            queries = three(query_rot)
            d_mix = three(d_mixed_heads)
            probs = probs_in[j, :, probs_at(part) : probs_at(part) + keys]
            probs_f = probs.astype(f32)
            d_probs = dot_nt(d_mix, value_both[0:keys, at])
            product = probs_f * d_probs
            d_scores = product - probs_f * jnp.sum(product, axis=1, keepdims=True)
            d_scores = d_scores.astype(bf16)
            d_query = dot_nn(d_scores, key_both[0:keys, at])
            for g in range(GROUP):
                head_parts[3 * j + g, rows, :] = d_query[g * 128 : g * 128 + 128]
            d_key = dot_tn(d_scores, queries)
            d_value = dot_tn(probs, d_mix)
            if part == 2:
                key_parts[j] = d_key
                value_parts[j] = d_value
            else:
                key_parts[j, 0:keys, :] += d_key
                value_parts[j, 0:keys, :] += d_value

    low = lane_index((MB_TOK, 128)) < 64
    cosine, sine = (cosines[...], sines[...])
    empty = jnp.zeros((MB_TOK, 128), f32)

    def paired_heads(parts_of, count, c):
        return jnp.where(low, parts_of(2 * c), parts_of(2 * c + 1) if 2 * c + 1 < count else empty)

    def summed(ref):
        return lambda j: ref[j] + pltpu.roll(ref[j], 64, 1)

    query_tiles = [
        turned(paired_heads(lambda h: head_parts[h], HEADS, c) * HEAD**-0.5, cosine, -sine)
        for c in range(8)
    ]
    key_tiles = [
        turned(paired_heads(summed(key_parts), KV_HEADS, c) * HEAD**-0.5, cosine, -sine)
        for c in range(3)
    ]
    value_tiles = [paired_heads(summed(value_parts), KV_HEADS, c) for c in range(3)]
    for r in range(REPS):
        tiles = laid(
            [
                (query_tiles, 240 * r, 0, 240),
                (key_tiles, 80 * r, 240, 80),
                (value_tiles, 80 * r, 320, 80),
            ],
            MB_TOK,
            4,
        )
        wire_in[r ^ quarter_here] = joined(tiles).astype(bf16)
    d_normed = sum(
        dot_nt(wire_in[quarter], block_columns(attn_all, quarter, 0, 512))
        for quarter in range(REPS)
    )
    values = inputs[...].astype(f32)
    scale = lax.rsqrt(jnp.sum(values * values, axis=1, keepdims=True) * (1.0 / D) + norm_epsilon)
    weighted = d_normed * gain_one
    inner = jnp.sum(weighted * values, axis=1, keepdims=True) * (1.0 / D)
    term_one = jnp.sum(d_normed * values * scale, axis=0, keepdims=True)
    total = d_middle + scale * weighted - values * scale * scale * scale * inner
    token_grad[...] = total.astype(bf16)
    gain_sums[0:1, :] = term_one
    gain_sums[1:2, :] = term_two


def attn_grads_kernel(*refs, count):
    normed, mixed, wires_in, wires_out, gain_parts = [
        refs[n * count : n * count + count] for n in range(5)
    ]
    arrays = refs[5 * count : 5 * count + 2]
    gain_sums = sum(part[0:8, :] for part in gain_parts)

    def stacked(parts, *at):
        return jnp.concatenate([part[at] for part in parts], axis=0)

    normed_turned = stacked(normed, ...).T
    mixed_turned = stacked(mixed, ...).T
    wire_out = stacked(wires_out, ...)
    row = lax.broadcasted_iota(jnp.int32, (SLOTS, 16, SLOT), 1)
    gain_rows = jnp.zeros((SLOTS, 16, SLOT), f32)
    for which in range(2):
        spots = [
            gain_sums[which : which + 1, s * SLOT : s * SLOT + SLOT].reshape(1, 1, SLOT)
            for s in range(SLOTS)
        ]
        gain_rows = jnp.where(row == 8 + which, jnp.concatenate(spots, axis=0), gain_rows)
    for quarter in range(REPS):
        first = dot_nn(normed_turned, stacked(wires_in, quarter))
        second = dot_nn(mixed_turned, wire_out[:, quarter * 256 : quarter * 256 + 256])
        block = jnp.concatenate(
            [first[:, 0:384], first[:, 384:512] + second[:, 0:128], second[:, 128:256]], axis=1
        ).reshape(SLOTS, SLOT, PACK)
        y, core = (quarter >> 1, quarter & 1)
        low_rows = block[:, 0:ROWS_A, :].astype(bf16)
        high_rows = block[:, ROWS_A:SLOT, :].astype(bf16)
        target = arrays[core]
        target[0, y, :, :, :] = low_rows
        tail = (block[:, 112:SLOT, 0:SLOT] + gain_rows).astype(bf16)
        for side in range(2):
            slots = slice(side * 4, side * 4 + 4)
            target[1, side, y * 4 : y * 4 + 4, :, :] = high_rows[slots]
            target[1, side, y * 4 : y * 4 + 4, 48:64, 0:SLOT] = tail[slots]


def attn_backward(
    batch,
    here,
    cotangent,
    middle,
    d_normed_two,
    inputs,
    query_rot,
    key_both,
    value_both,
    probs,
    tables,
    parts,
):
    one = [middle, d_normed_two]
    own = [query_rot, key_both, value_both, probs]
    outs = [
        ((MB_TOK, WIDE), bf16),
        ((REPS, MB_TOK, 512), bf16),
        ((MB_TOK, REPS * 256), bf16),
        ((8, WIDE), f32),
    ]
    return pl.pallas_call(
        attn_backward_kernel,
        grid=(1,),
        in_specs=[in_scalars(), batch_block(batch, WIDE)]
        + [whole_block(array.shape) for array in one]
        + [batch_block(batch, WIDE)]
        + [whole_block(array.shape) for array in own]
        + [batch_block(batch, 128)] * 2
        + [anywhere()] * 8,
        out_specs=[whole_block(out[0]) for out in outs],
        out_shape=[jax.ShapeDtypeStruct(*out) for out in outs],
        scratch_shapes=[
            pltpu.VMEM((REPS, SLOTS, SLOT, PACK), bf16),
            pltpu.VMEM((SLOTS, MB_TOK, SLOT), f32),
            pltpu.VMEM((HEADS, MB_TOK, 128), f32),
            pltpu.VMEM((KV_HEADS, MB_TOK, 128), f32),
            pltpu.VMEM((KV_HEADS, MB_TOK, 128), f32),
            pltpu.VMEM((MB_TOK, WIDE), bf16),
            pltpu.SemaphoreType.DMA((12,)),
        ],
        compiler_params=pltpu.CompilerParams(vmem_limit_bytes=VMEM_BYTES),
        cost_estimate=pl.CostEstimate(
            flops=12_000_000_000, bytes_accessed=20_000_000, transcendentals=0
        ),
        name="attn_backward",
    )(here, cotangent, *one, inputs, *own, *tables, *parts)


def attn_grads(normed, mixed, wires_in, wires_out, gain_parts):
    count = len(normed)
    half = jax.ShapeDtypeStruct((2, 2, SLOTS, ROWS_A, PACK), bf16)
    arrays = (*normed, *mixed, *wires_in, *wires_out, *gain_parts)
    return pl.pallas_call(
        lambda *refs: attn_grads_kernel(*refs, count=count),
        grid=(1,),
        in_specs=[whole_block(array.shape) for array in arrays],
        out_specs=[whole_block(half.shape)] * 2,
        out_shape=[half] * 2,
        compiler_params=pltpu.CompilerParams(vmem_limit_bytes=VMEM_BYTES),
        cost_estimate=pl.CostEstimate(
            flops=8_000_000_000, bytes_accessed=14_000_000, transcendentals=0
        ),
        name="attn_grads",
    )(*arrays)


X_SIDE = ("fsdp", 1)
Y_SIDE = ("rep", 2)
CORE = ("rep", 1)


def swap_with(values, step):
    axis, mask = step
    count = lax.axis_size(axis)
    return lax.ppermute(values, axis, [(i, i ^ mask) for i in range(count)])


def after(values, *done):
    return lax.optimization_barrier((values, done))[0]


def sent_along_z(block):
    return [swap_with(block, ("fsdp", 2 * k)) for k in range(1, 4)]


def along_z(block, came):
    return jnp.stack([block] + list(came))


def sides_of(side_first):
    return (X_SIDE, Y_SIDE) if side_first else (Y_SIDE, X_SIDE)


def sent_along_first(four, side_first):
    return swap_with(four, sides_of(side_first)[0])


def along_first(four, side_first):
    return jnp.concatenate([four, sent_along_first(four, side_first)])


def along_second(eight, side_first):
    return swap_with(eight, sides_of(side_first)[1])


def along_core(eight, across):
    return (eight, swap_with(eight, CORE), across, swap_with(across, CORE))


def added(left, right):
    return (left.astype(f32) + right.astype(f32)).astype(bf16)


class Reduction:
    def __init__(self, kept, came, which, side_first):
        self.kept = kept
        self.came = came
        self.which = which
        self.first, self.second = sides_of(side_first)
        self.out = added(kept[which, 1], came[which, 1])

    def sent_second(self):
        return swap_with(self.out, self.second)

    def over_second(self, came):
        kept, before = after((self.kept, self.came), came)
        self.terms = [kept[self.which, 0], before[self.which, 0], came]
        self.out = sum(term[4:8].astype(f32) for term in self.terms).astype(bf16)

    def sent_first(self):
        return swap_with(self.out, self.first)

    def over_first(self, came):
        terms, came = after((self.terms, came), came)
        self.blocks = [
            sum(term[k].astype(f32) for term in (*terms, came)).astype(bf16) for k in range(4)
        ]


def z_stage(one, two):
    blocks = [jnp.concatenate([one.blocks[k], two.blocks[k]], axis=0) for k in range(4)]
    return (blocks[0], [swap_with(blocks[k], ("fsdp", 2 * k)) for k in range(1, 4)])


def z_sum(kept, came):
    return sum((block.astype(f32) for block in came), kept.astype(f32))


def split_parts(blocks, side_first):
    rows, columns = blocks.shape[2:]
    grid = blocks.reshape(4, 2, 2, 2, rows, columns)
    parts = []
    for second in range(2):
        for core in range(2):
            if side_first:
                part = grid[:, :, second, core].transpose(1, 0, 2, 3)
            else:
                part = grid[:, second, :, core].transpose(1, 0, 2, 3)
            parts.append(part.reshape(SLOTS, rows, columns))
    return parts


def eight_parts(first_blocks, second_blocks):
    return (*split_parts(first_blocks, True), *split_parts(second_blocks, False))


def join_parts(kept, sent, side_first):
    rows, columns = kept.shape[2:]
    grid = jnp.stack([kept, sent]).reshape(2, 2, 2, 4, rows, columns)
    grid = grid.transpose(3, 2, 1, 0, 4, 5) if side_first else grid.transpose(3, 1, 2, 0, 4, 5)
    return grid.reshape(SLOTS, REPS, rows, columns)


def attn_block(w_query, w_key, w_value, w_output, attn_gain, mlp_gain):
    matrices = jnp.concatenate([w_query, w_key, w_value, w_output], axis=1)
    gains = jnp.stack([attn_gain, mlp_gain])
    gains = jnp.pad(gains, ((0, SLOT - USED - 2), (0, PACK - USED)))
    return jnp.concatenate([matrices, gains], axis=0)


def down_block(w_down):
    halves = w_down.T.reshape(2, USED, HALF_PACK)
    halves = jnp.concatenate([halves[0], halves[1]], axis=1)
    return jnp.pad(halves, ((0, SLOT - USED), (0, 0)))


def mlp_block(w_gate, w_up, w_down):
    taller = ((0, SLOT - USED), (0, 0))
    return jnp.concatenate([jnp.pad(w_gate, taller), jnp.pad(w_up, taller), down_block(w_down)])


def down_of(block):
    halves = jnp.stack([block[:USED, :HALF_PACK], block[:USED, HALF_PACK:]])
    return halves.reshape(2 * USED, HALF_PACK).T


def whole(shard):
    return lax.all_gather(lax.all_gather(shard, "rep", axis=1, tiled=True), "fsdp", axis=0, tiled=True)


def cut(matrix, eighth, quarter):
    rows, columns = (matrix.shape[0] // SLOTS, matrix.shape[1] // REPS)
    return matrix[
        eighth * rows : eighth * rows + rows, quarter * columns : quarter * columns + columns
    ]


def every_block(make):
    return jnp.stack(
        [jnp.stack([make(e, q) for q in range(REPS)]) for e in range(SLOTS)]
    )


def owned(blocks):
    eighths, quarters, rows, columns = blocks.shape
    matrix = blocks.transpose(0, 2, 1, 3).reshape(eighths * rows, quarters * columns)
    part = lax.psum_scatter(matrix, "fsdp", scatter_dimension=0, tiled=True)
    return lax.psum_scatter(part, "rep", scatter_dimension=1, tiled=True).astype(f32)


def per_device(
    tokens,
    lengths,
    attn_gain,
    w_query,
    w_key,
    w_value,
    w_output,
    mlp_gain,
    w_gate,
    w_up,
    w_down,
    cotangent,
):
    paired = lax.axis_size("fsdp") == SLOTS and lax.axis_size("rep") == REPS
    if paired:
        eighth_here = lax.axis_index("fsdp").astype(jnp.int32)
        quarter_here = lax.axis_index("rep").astype(jnp.int32)
    else:
        eighth_here = jnp.int32(0)
        quarter_here = jnp.int32(0)
    here = jnp.stack([eighth_here, quarter_here])
    spread = spreading(eighth_here)
    segments, positions = jax.vmap(layout)(lengths)
    tables = rope_tables(positions.reshape(-1))
    inputs = jnp.dot(tokens, spread, preferred_element_type=f32).astype(bf16)
    upstream = jnp.dot(cotangent, spread, preferred_element_type=f32).astype(bf16)
    batches = range(tokens.shape[0] // MB_TOK)
    forward_inputs = [inputs for _ in batches]

    if paired:
        attn_pack = attn_block(w_query, w_key, w_value, w_output, attn_gain, mlp_gain)
        pack = mlp_block(w_gate, w_up, w_down)
        attn_four = along_z(attn_pack, sent_along_z(attn_pack))
        three, four, attn_four = lax.optimization_barrier((pack[:ROWS_W], pack[ROWS_W:], attn_four))
        three_came = sent_along_z(three)
        one, two = (attn_four[:, :ROWS_A], attn_four[:, ROWS_A:])
        came = (sent_along_first(one, True), sent_along_first(two, False))
        three_came, came, four = lax.optimization_barrier((three_came, came, four))
        one, two = (jnp.concatenate([one, came[0]]), jnp.concatenate([two, came[1]]))
        four_came = sent_along_z(four)
        across = (along_second(one, True), along_second(two, False))
        four_came, across, inputs, upstream, tables, segments, here = lax.optimization_barrier(
            (four_came, across, inputs, upstream, tables, segments, here)
        )
        three, four = (along_z(three, three_came), along_z(four, four_came))
        attn_parts = (*along_core(one, across[0]), *along_core(two, across[1]))
        three, four = (along_first(three, True), along_first(four, False))
        across = (along_second(three, True), along_second(four, False))
        near = (swap_with(three, CORE), swap_with(four, CORE))
        forward_inputs[0] = after(inputs, three, four)
    else:
        gain_one, gain_two = (
            lax.all_gather(attn_gain, "fsdp", axis=0, tiled=True).reshape(SLOTS, USED),
            lax.all_gather(mlp_gain, "fsdp", axis=0, tiled=True).reshape(SLOTS, USED),
        )
        mats = [whole(w) for w in (w_query, w_key, w_value, w_output, w_gate, w_up, w_down)]
        attn_blocks = every_block(
            lambda e, q: attn_block(*[cut(m, e, q) for m in mats[:4]], gain_one[e], gain_two[e])
        )
        attn_parts = eight_parts(attn_blocks[:, :, :ROWS_A], attn_blocks[:, :, ROWS_A:])
        mlp_blocks = every_block(
            lambda e, q: mlp_block(cut(mats[4], e, q), cut(mats[5], e, q), cut(mats[6], e, q))
        )
        mlp_parts = eight_parts(mlp_blocks[:, :, :ROWS_W], mlp_blocks[:, :, ROWS_W:])

    made = []
    for batch in batches:
        made.append(attn_forward(batch, here, forward_inputs[batch], attn_parts, tables, segments))
        if paired and batch == 0:
            forward_inputs[-1] = after(inputs, near, made[0][-1])
    normed, query_rot, key_both, value_both, probs, mixed, middle, normed_two = zip(*made)
    if paired:
        across = after(across, normed_two[-1])
        far = (swap_with(across[0], CORE), swap_with(across[1], CORE))
        mlp_parts = (three, near[0], across[0], far[0], four, near[1], across[1], far[1])
    hidden, d_gate, d_up, w_down_all, kept, sent = mlp(
        here, normed_two, upstream, mlp_parts
    )
    mlp_out, d_normed_two = mlp_outputs(hidden, d_gate, d_up, w_down_all, mlp_parts)
    d_normed_two = list(d_normed_two)
    if paired:
        came = swap_with(sent, CORE)
        gate_sums = [Reduction(kept, came, which, which == 0) for which in range(2)]
        up_sums = [Reduction(kept, came, 2 + which, which == 0) for which in range(2)]
        d_normed_two[0] = after(d_normed_two[0], gate_sums[0].out, gate_sums[1].out)
    back = []
    for batch in batches:
        back.append(
            attn_backward(
                batch,
                here,
                upstream,
                middle[batch],
                d_normed_two[batch],
                inputs,
                query_rot[batch],
                key_both[batch],
                value_both[batch],
                probs[batch],
                tables,
                attn_parts,
            )
        )
        if paired and batch == 0:
            for part in gate_sums:
                part.over_second(part.sent_second())
            for part in up_sums:
                part.out = after(part.out, gate_sums[0].out, gate_sums[1].out)
            d_normed_two[-1] = after(d_normed_two[-1], up_sums[0].out, up_sums[1].out)
    token_rows, wires_in, wires_out, gain_parts = zip(*back)
    if paired:
        for part in up_sums:
            part.over_second(part.sent_second())
        for part in gate_sums:
            part.over_first(part.sent_first())
        wires_in = after(
            wires_in, up_sums[0].out, up_sums[1].out, gate_sums[0].blocks, gate_sums[1].blocks
        )
    attn_kept, attn_sent = attn_grads(
        normed, mixed, wires_in, wires_out, gain_parts
    )
    if paired:
        up_came = [part.sent_first() for part in up_sums]
        gate_kept, gate_came = z_stage(*gate_sums)
        up_came, gate_came, attn_sent = lax.optimization_barrier((up_came, gate_came, attn_sent))
        came = swap_with(attn_sent, CORE)
        for part, part_came in zip(up_sums, up_came):
            part.over_first(part_came)
        one, two = [Reduction(attn_kept, came, which, which == 0) for which in range(2)]
        up_kept, up_came = z_stage(*up_sums)
        across = (one.sent_second(), two.sent_second())
        up_first, up_second, up_last = up_came
        up_first, up_second, across = lax.optimization_barrier((up_first, up_second, across))
        one.over_second(across[0])
        two.over_second(across[1])
        came = (one.sent_first(), two.sent_first())
        came, up_last = lax.optimization_barrier((came, up_last))
        tail = came
        one.over_first(came[0])
        two.over_first(came[1])
        gate_sum = z_sum(gate_kept, gate_came)
        up_sum = z_sum(up_kept, (up_first, up_second, up_last))
        attn_sum = z_sum(*z_stage(one, two))
        gain_sums = (attn_sum[USED, :USED], attn_sum[USED + 1, :USED])
        attn_sum = attn_sum[:USED]
        grads = [
            attn_sum[:, 0:240],
            attn_sum[:, 240:320],
            attn_sum[:, 320:400],
            attn_sum[:, 400:640],
            gate_sum[:USED],
            up_sum[:USED],
            down_of(jnp.concatenate([gate_sum[SLOT:], up_sum[SLOT:]], axis=0)),
        ]
    else:
        tail = (attn_kept,)
        attn_blocks = jnp.concatenate(
            [join_parts(attn_kept[k], attn_sent[k], k == 0) for k in range(2)], axis=2
        )
        gain_sums = tuple(
            lax.psum(
                lax.psum_scatter(
                    attn_blocks[:, 0, USED + which, :USED].astype(f32).reshape(D),
                    "fsdp",
                    scatter_dimension=0,
                    tiled=True,
                ),
                "rep",
            )
            for which in range(2)
        )
        attn_blocks = attn_blocks[:, :, :USED]
        gate_blocks, up_blocks = [
            jnp.concatenate(
                [join_parts(kept[k], sent[k], k % 2 == 0) for k in (which, which + 1)], axis=2
            )
            for which in (0, 2)
        ]
        down_blocks = jnp.concatenate([gate_blocks[:, :, SLOT:], up_blocks[:, :, SLOT:]], axis=2)
        grads = [
            owned(attn_blocks[..., 0:240]),
            owned(attn_blocks[..., 240:320]),
            owned(attn_blocks[..., 320:400]),
            owned(attn_blocks[..., 400:640]),
            owned(gate_blocks[:, :, :USED]),
            owned(up_blocks[:, :, :USED]),
            owned(jax.vmap(jax.vmap(down_of))(down_blocks)),
        ]
    middle, mlp_out, token_rows = after((middle, mlp_out, token_rows), *tail)
    output_rows = jnp.concatenate(
        [(middle[batch] + mlp_out[batch]).astype(bf16) for batch in batches], axis=0
    )
    output = jnp.dot(output_rows, spread.T, preferred_element_type=f32).astype(bf16)
    token_grad = jnp.dot(
        jnp.concatenate(token_rows, axis=0), spread.T, preferred_element_type=f32
    ).astype(bf16)
    return (
        output,
        token_grad,
        gain_sums[0],
        grads[0],
        grads[1],
        grads[2],
        grads[3],
        gain_sums[1],
        grads[4],
        grads[5],
        grads[6],
    )


def solution(mesh):
    placed = (
        P(("fsdp", "rep"), None),
        P(("fsdp", "rep"), None),
        P("fsdp"),
        P("fsdp", "rep"),
        P("fsdp", "rep"),
        P("fsdp", "rep"),
        P("fsdp", "rep"),
        P("fsdp"),
        P("fsdp", "rep"),
        P("fsdp", "rep"),
        P("fsdp", "rep"),
        P(("fsdp", "rep"), None),
    )
    return jax.shard_map(
        per_device,
        mesh=mesh,
        in_specs=placed,
        out_specs=(
            P(("fsdp", "rep"), None),
            P(("fsdp", "rep"), None),
            P("fsdp"),
            P("fsdp", "rep"),
            P("fsdp", "rep"),
            P("fsdp", "rep"),
            P("fsdp", "rep"),
            P("fsdp"),
            P("fsdp", "rep"),
            P("fsdp", "rep"),
            P("fsdp", "rep"),
        ),
        check_vma=False,
    )
```

```python
import jax
import jax.numpy as jnp
from jax import lax
from jax.experimental import pallas as pl
from jax.experimental.pallas import tpu as pltpu
from jax.sharding import PartitionSpec as P

D = 960
FF = 2560
HEADS = 15
KV_HEADS = 5
HEAD = 64
MB_TOK = 384
SEGS = 3
GROUP = 3
QW = 960
KVW = 320

SLOTS = 8
REPS = 4
USED = 120
SLOT = 128
WIDE = SLOTS * SLOT
PACK = 640
HALF_PACK = 320
ROWS_A = 64
ROWS_M = 96
REST = SLOT - ROWS_M
ROWS_W = 192
VMEM_BYTES = 60 * 1024 * 1024

norm_epsilon = 1e-05
rope_base = 100000.0
masked_value = -1e30

f32 = jnp.float32
bf16 = jnp.bfloat16


def layout(length_row):
    starts = jnp.cumsum(length_row) - length_row
    places = jnp.arange(MB_TOK, dtype=jnp.int32)
    inside = (
        (places[:, None] >= starts[None, :]) & (places[:, None] < (starts + length_row)[None, :])
    ).astype(jnp.int32)
    segment = jnp.sum(inside * jnp.arange(SEGS, dtype=jnp.int32)[None, :], axis=1)
    position = places - jnp.sum(inside * starts[None, :], axis=1)
    return (segment, position)


def rope_tables(position):
    half_width = HEAD // 2
    exponent = jnp.arange(half_width, dtype=f32) * (2.0 / HEAD)
    inverse = jnp.power(rope_base, -exponent)
    angles = position.astype(f32)[:, None] * inverse
    cosines, sines = (jnp.cos(angles), jnp.sin(angles))
    return (
        jnp.concatenate([cosines] * 4, axis=1),
        jnp.concatenate([-sines, sines, -sines, sines], axis=1),
    )


def slot_of(eighth):
    return (eighth & 1) * 4 + (eighth >> 1)


def eighth_of(slot):
    return (slot & 3) * 2 + (slot >> 2)


def feature_lanes(eighth_here):
    lanes = jnp.arange(WIDE, dtype=jnp.int32)
    eighth = eighth_of(lanes // SLOT) ^ eighth_here
    return jnp.where(lanes % SLOT < USED, eighth * USED + lanes % SLOT, -1)


def spreading(eighth_here):
    features = jnp.arange(D, dtype=jnp.int32)
    return (features[:, None] == feature_lanes(eighth_here)[None, :]).astype(bf16)


def dot_nn(left, right):
    return lax.dot_general(left, right, (((1,), (0,)), ((), ())), preferred_element_type=f32)


def dot_nt(left, right):
    return lax.dot_general(left, right, (((1,), (1,)), ((), ())), preferred_element_type=f32)


def dot_tn(left, right):
    return lax.dot_general(left, right, (((0,), (0,)), ((), ())), preferred_element_type=f32)


def lane_index(shape):
    return lax.broadcasted_iota(jnp.int32, shape, len(shape) - 1)


def swapped(values):
    first = (lane_index(values.shape) & 63) < 32
    return jnp.where(first, pltpu.roll(values, 96, 1), pltpu.roll(values, 32, 1))


def turned(values, cosines, sines):
    return values * cosines + swapped(values) * sines


def both_halves(values, odd):
    low = lane_index(values.shape) < 64
    moved = pltpu.roll(values, 64, 1)
    return jnp.where(low, moved, values) if odd else jnp.where(low, values, moved)


def only_half(values, odd):
    low = lane_index(values.shape) < 64
    return jnp.where(low != bool(odd), values, jnp.zeros_like(values))


def laid(pieces, rows, tiles):
    lane = lane_index((rows, 128))
    made = [jnp.zeros((rows, 128), f32)] * tiles
    for source, start, target, width in pieces:
        shifted = {}
        done = 0
        while done < width:
            from_tile, from_lane = divmod(start + done, 128)
            to_tile, to_lane = divmod(target + done, 128)
            now = min(width - done, 128 - from_lane, 128 - to_lane)
            if from_tile not in shifted:
                values = source[from_tile]
                turn = (to_lane - from_lane) % 128
                shifted[from_tile] = pltpu.roll(values, turn, 1) if turn else values
            inside = (lane >= to_lane) & (lane < to_lane + now)
            made[to_tile] = jnp.where(inside, shifted[from_tile], made[to_tile])
            done += now
    return made


def tiles_of(values):
    return [values[:, t : t + 128] for t in range(0, values.shape[1], 128)]


def joined(tiles):
    return jnp.concatenate(tiles, axis=1)


def gain_row(attn_ref, which):
    rows = [attn_ref[0, s, 112:128, 0:SLOT].astype(f32)[8 + which : 9 + which] for s in range(SLOTS)]
    return jnp.concatenate(rows, axis=1)


def views(parts):
    return (parts[:4], parts[4:])


def attn_fetches(parts, attn_all, sems):
    copies = []
    firsts, seconds = views(parts)
    for quarter, source in enumerate(firsts):
        copies.append((source, attn_all.at[quarter, :, 0:ROWS_A, :]))
    for place, source in enumerate(seconds):
        side, core = (place >> 1, place & 1)
        for y in range(2):
            copies.append(
                (
                    source.at[y * 4 : y * 4 + 4],
                    attn_all.at[y * 2 + core, side * 4 : side * 4 + 4, ROWS_A : 2 * ROWS_A, :],
                )
            )
    return [
        pltpu.make_async_copy(source, target, sems.at[n])
        for n, (source, target) in enumerate(copies)
    ]


def block_columns(attn_all, quarter, low, high):
    return attn_all[quarter, :, :, low:high].reshape(WIDE, high - low)


def probs_at(part):
    return (0, 128, 384)[part]


def attn_forward_kernel(
    here,
    inputs,
    cosines,
    sines,
    segment_rows,
    segment_columns,
    *refs,
):
    parts = refs[:8]
    (
        normed_out,
        query_out,
        key_out,
        value_out,
        probs_out,
        mixed_out,
        middle_out,
        normed_two_out,
        attn_all,
        wire,
        heads_out,
        mixed_slots,
        out_slots,
        bias,
        sems,
    ) = refs[8:]
    eighth_here, quarter_here = (here[0], here[1])
    fetches = attn_fetches(parts, attn_all, sems)
    for copy in fetches:
        copy.start()
    values = inputs[...].astype(f32)
    scale = lax.rsqrt(jnp.sum(values * values, axis=1, keepdims=True) * (1.0 / D) + norm_epsilon)
    for copy in fetches:
        copy.wait()
    normed = (values * scale * gain_row(attn_all, 0)).astype(bf16)
    normed_out[...] = normed
    cosine, sine = (cosines[...], sines[...])
    for quarter in range(REPS):
        wire[quarter] = dot_nn(normed, block_columns(attn_all, quarter, 0, 512))
    sources = [
        [wire[r ^ quarter_here, :, t * 128 : t * 128 + 128] for t in range(4)] for r in range(REPS)
    ]
    query_tiles = laid([(sources[r], 0, 240 * r, 240) for r in range(REPS)], MB_TOK, 8)
    for c in range(8):
        query_out[:, c * 128 : c * 128 + 128] = turned(query_tiles[c], cosine, sine).astype(bf16)
    key_tiles = laid([(sources[r], 240, 80 * r, 80) for r in range(REPS)], MB_TOK, 3)
    value_tiles = laid([(sources[r], 320, 80 * r, 80) for r in range(REPS)], MB_TOK, 3)
    for c in range(3):
        key_part = turned(key_tiles[c], cosine, sine)
        for odd in range(2 if c < 2 else 1):
            at = slice((2 * c + odd) * 128, (2 * c + odd) * 128 + 128)
            key_out[:, at] = both_halves(key_part, odd).astype(bf16)
            value_out[:, at] = both_halves(value_tiles[c], odd).astype(bf16)

    query_place = lax.broadcasted_iota(jnp.int32, (MB_TOK, MB_TOK), 0)
    key_place = lax.broadcasted_iota(jnp.int32, (MB_TOK, MB_TOK), 1)
    seen = (segment_rows[...] == segment_columns[0]) & (key_place <= query_place)
    bias[...] = jnp.where(seen, 0.0, masked_value)
    for j in range(KV_HEADS):
        at = slice(j * 128, j * 128 + 128)
        for part in range(3):
            keys = 128 * (part + 1)
            rows = slice(part * 128, part * 128 + 128)
            queries = jnp.concatenate(
                [
                    only_half(query_out[rows, (h // 2) * 128 : (h // 2) * 128 + 128], h % 2)
                    for h in range(3 * j, 3 * j + 3)
                ],
                axis=0,
            )
            scores = dot_nt(queries, key_out[0:keys, at]) * HEAD**-0.5
            hidden_part = bias[rows, 0:keys]
            scores = scores + jnp.concatenate([hidden_part] * GROUP, axis=0)
            peak = jnp.max(scores, axis=1, keepdims=True)
            weights = jnp.exp(scores - peak)
            total = jnp.sum(weights, axis=1, keepdims=True)
            probs = (weights * (1.0 / total)).astype(bf16)
            probs_out[j, :, probs_at(part) : probs_at(part) + keys] = probs
            gathered = dot_nn(probs, value_out[0:keys, at])
            for g in range(GROUP):
                heads_out[3 * j + g, rows, :] = gathered[g * 128 : g * 128 + 128]
    low = lane_index((MB_TOK, 128)) < 64
    head_tiles = [
        jnp.where(
            low,
            heads_out[2 * c],
            heads_out[2 * c + 1] if 2 * c + 1 < HEADS else jnp.zeros((MB_TOK, 128), f32),
        )
        for c in range(8)
    ]
    for eighth in range(SLOTS):
        (slot_tile,) = laid([(head_tiles, USED * eighth, 0, USED)], MB_TOK, 1)
        mixed_slots[slot_of(eighth ^ eighth_here)] = slot_tile.astype(bf16)
    mixed = joined([mixed_slots[s] for s in range(SLOTS)])
    mixed_out[...] = mixed
    for quarter in range(REPS):
        part = tiles_of(dot_nn(mixed, block_columns(attn_all, quarter, 384, 640)))
        for which in range(2):
            eighth = (quarter ^ quarter_here) * 2 + which
            (slot_tile,) = laid([(part, 16 + USED * which, 0, USED)], MB_TOK, 1)
            out_slots[slot_of(eighth ^ eighth_here)] = slot_tile
    middle = values + joined([out_slots[s] for s in range(SLOTS)])
    middle_out[...] = middle
    scale_two = lax.rsqrt(
        jnp.sum(middle * middle, axis=1, keepdims=True) * (1.0 / D) + norm_epsilon
    )
    normed_two_out[...] = (middle * scale_two * gain_row(attn_all, 1)).astype(bf16)


def whole_block(shape):
    return pl.BlockSpec(
        shape, lambda *ids: (0,) * len(shape), pipeline_mode=pl.Buffered(buffer_count=1)
    )


def anywhere():
    return pl.BlockSpec(memory_space=pl.ANY)


def batch_block(batch, columns):
    return pl.BlockSpec((MB_TOK, columns), lambda i: (batch, 0))


def attn_scratch():
    return [
        pltpu.VMEM((REPS, SLOTS, SLOT, PACK), bf16),
        pltpu.VMEM((REPS, MB_TOK, 512), f32),
        pltpu.VMEM((HEADS, MB_TOK, 128), f32),
    ]


def in_scalars():
    return pl.BlockSpec(memory_space=pltpu.SMEM)


def attn_forward(batch, here, inputs, parts, tables, segments):
    outs = [
        ((MB_TOK, WIDE), bf16),
        ((MB_TOK, WIDE), bf16),
        ((MB_TOK, PACK), bf16),
        ((MB_TOK, PACK), bf16),
        ((KV_HEADS, MB_TOK, 768), bf16),
        ((MB_TOK, WIDE), bf16),
        ((MB_TOK, WIDE), f32),
        ((MB_TOK, WIDE), bf16),
    ]
    return pl.pallas_call(
        attn_forward_kernel,
        grid=(1,),
        in_specs=[
            in_scalars(),
            batch_block(batch, WIDE),
            batch_block(batch, 128),
            batch_block(batch, 128),
            batch_block(batch, 1),
            pl.BlockSpec((1, 1, MB_TOK), lambda i: (batch, 0, 0)),
        ]
        + [anywhere()] * 8,
        out_specs=[whole_block(out[0]) for out in outs],
        out_shape=[jax.ShapeDtypeStruct(*out) for out in outs],
        scratch_shapes=attn_scratch()
        + [
            pltpu.VMEM((SLOTS, MB_TOK, SLOT), bf16),
            pltpu.VMEM((SLOTS, MB_TOK, SLOT), f32),
            pltpu.VMEM((MB_TOK, MB_TOK), f32),
            pltpu.SemaphoreType.DMA((12,)),
        ],
        compiler_params=pltpu.CompilerParams(vmem_limit_bytes=VMEM_BYTES),
        cost_estimate=pl.CostEstimate(
            flops=8_000_000_000, bytes_accessed=16_000_000, transcendentals=2_000_000
        ),
        name="attn_forward",
    )(
        here,
        inputs,
        *tables,
        *segments,
        *parts,
    )


def left_right(left, right):
    first = lane_index(left.shape) < HALF_PACK
    left, right = (left.astype(f32), right.astype(f32))
    return (
        jnp.where(first, left, pltpu.roll(right, HALF_PACK, 1)).astype(bf16),
        jnp.where(first, pltpu.roll(left, HALF_PACK, 1), right).astype(bf16),
    )


def pair_fetches(parts, at, w_gate, w_up, sems):
    found = []
    firsts, seconds = views(parts)
    for core in range(2):
        lanes = slice(core * PACK, core * PACK + PACK)
        source = firsts[at * 2 + core]
        found.append((source.at[:, 0:SLOT, :], w_gate.at[:, :, lanes]))
        found.append((source.at[:, SLOT:ROWS_W, :], w_up.at[:, 0:64, lanes]))
        for side in range(2):
            found.append(
                (
                    seconds[side * 2 + core].at[at * 4 : at * 4 + 4, 0:64, :],
                    w_up.at[side * 4 : side * 4 + 4, 64:SLOT, lanes],
                )
            )
    return [
        pltpu.make_async_copy(source, target, sems.at[n])
        for n, (source, target) in enumerate(found)
    ]


def mlp_kernel(here, *refs, count):
    normed = refs[:count]
    cotangent = refs[count]
    parts = refs[count + 1 : count + 9]
    hidden, d_gate, d_up, down_out, kept, sent = refs[count + 9 : count + 15]
    (
        w_gate,
        w_up,
        down_raw,
        normed_turned,
        cotangent_turned,
        grad_gate,
        grad_up,
        grad_down,
        down_made,
        sem_pair,
        sem_down,
        sem_out,
    ) = refs[count + 15 :]
    step = pl.program_id(0)
    eighth_here, quarter_here = (here[0], here[1])
    side_here = eighth_here & 1

    def plane_of(at, core):
        return ((2 * at + core) ^ quarter_here) ^ (eighth_here >> 1)

    def fetches(at):
        found = []
        for core in range(2):
            for side in range(2):
                for quarter in range(REPS):
                    y, inner = (quarter >> 1, quarter & 1)
                    found.append(
                        (
                            views(parts)[1][side * 2 + inner].at[
                                y * 4 + plane_of(at, core), 64:ROWS_W
                            ],
                            down_raw.at[core, side, quarter],
                        )
                    )
        return pair_fetches(parts, at, w_gate, w_up, sem_pair) + [
            pltpu.make_async_copy(source, target, sem_down.at[n])
            for n, (source, target) in enumerate(found)
        ]

    def results(at):
        found = []
        for group, source in enumerate((grad_gate, grad_up)):
            firsts = (kept.at[2 * group], sent.at[2 * group])
            seconds = (kept.at[2 * group + 1], sent.at[2 * group + 1])
            for core in range(2):
                found.append((source.at[core, :, 0:ROWS_M], firsts[core].at[at]))
                for side in range(2):
                    found.append(
                        (
                            source.at[core, side * 4 : side * 4 + 4, ROWS_M:SLOT],
                            seconds[core].at[side, at * 4 : at * 4 + 4, 0:REST],
                        )
                    )
                    for quarter in range(REPS):
                        y, inner = (quarter >> 1, quarter & 1)
                        found.append(
                            (
                                down_made.at[
                                    core, side, quarter, group * ROWS_A : group * ROWS_A + ROWS_A
                                ],
                                seconds[inner].at[
                                    side, y * 4 + plane_of(at, core), REST:ROWS_M
                                ],
                            )
                        )
        return [
            pltpu.make_async_copy(source, target, sem_out.at[n])
            for n, (source, target) in enumerate(found)
        ]

    def rows_of(quarter, which):
        eighth = (quarter ^ quarter_here) * 2 + which
        return pl.multiple_of(slot_of(eighth ^ eighth_here) * SLOT, SLOT)

    @pl.when(step == 0)
    def _():
        for copy in fetches(0):
            copy.start()
        for batch in range(count):
            rows = slice(batch * MB_TOK, batch * MB_TOK + MB_TOK)
            normed_turned[:, rows] = normed[batch][...].T
            cotangent_turned[:, rows] = cotangent[rows, :].T
        for copy in fetches(0):
            copy.wait()

    @pl.when(step == 1)
    def _():
        for copy in fetches(1):
            copy.wait()

    for core in range(2):
        lanes = slice(core * PACK, core * PACK + PACK)
        for quarter in range(REPS):
            lefts, rights = left_right(
                down_raw[core, side_here, quarter], down_raw[core, 1 - side_here, quarter]
            )
            down_out[0, pl.ds(rows_of(quarter, 0), SLOT), lanes] = lefts
            down_out[0, pl.ds(rows_of(quarter, 1), SLOT), lanes] = rights

    gate_weights = w_gate[...].reshape(WIDE, 2 * PACK)
    up_weights = w_up[...].reshape(WIDE, 2 * PACK)
    for batch in range(count):
        rows = slice(batch * MB_TOK, batch * MB_TOK + MB_TOK)
        gate = dot_nn(normed[batch][...], gate_weights)
        up = dot_nn(normed[batch][...], up_weights)
        d_hidden = dot_nn(cotangent[rows, :], down_out[0])
        sigmoid = 1.0 / (1.0 + jnp.exp(-gate))
        silu = gate * sigmoid
        hidden[0, rows, :] = (silu * up).astype(bf16)
        d_gate[0, rows, :] = (d_hidden * up * sigmoid * (1.0 + gate * (1.0 - sigmoid))).astype(bf16)
        d_up[0, rows, :] = (d_hidden * silu).astype(bf16)

    @pl.when(step == 0)
    def _():
        for copy in fetches(1):
            copy.start()

    @pl.when(step == 1)
    def _():
        for copy in results(0):
            copy.wait()

    for half in range(2):
        rows = slice(half * 512, half * 512 + 512)
        four = slice(half * 4, half * 4 + 4)
        gate_part = dot_nn(normed_turned[rows, :], d_gate[0]).astype(bf16)
        up_part = dot_nn(normed_turned[rows, :], d_up[0]).astype(bf16)
        for core in range(2):
            lanes = slice(core * PACK, core * PACK + PACK)
            grad_gate[core, four] = gate_part[:, lanes].reshape(4, SLOT, PACK)
            grad_up[core, four] = up_part[:, lanes].reshape(4, SLOT, PACK)
        grad_down[rows, :] = dot_nn(cotangent_turned[rows, :], hidden[0])
    for core in range(2):
        lanes = slice(core * PACK, core * PACK + PACK)
        for quarter in range(REPS):
            lefts, rights = left_right(
                grad_down[pl.ds(rows_of(quarter, 0), SLOT), lanes],
                grad_down[pl.ds(rows_of(quarter, 1), SLOT), lanes],
            )
            down_made[core, side_here, quarter] = lefts
            down_made[core, 1 - side_here, quarter] = rights
    for at in range(2):

        @pl.when(step == at)
        def _():
            for copy in results(at):
                copy.start()

    @pl.when(step == 1)
    def _():
        for copy in results(1):
            copy.wait()


def chunk_block(rows, columns):
    return pl.BlockSpec((1, rows, columns), lambda i: (i, 0, 0))


def mlp(here, normed, cotangent, parts):
    count = len(normed)
    tokens = cotangent.shape[0]
    rows = jax.ShapeDtypeStruct((2, tokens, 2 * PACK), bf16)
    part = jax.ShapeDtypeStruct((4, 2, SLOTS, ROWS_M, PACK), bf16)
    return pl.pallas_call(
        lambda *refs: mlp_kernel(*refs, count=count),
        grid=(2,),
        in_specs=[pl.BlockSpec(memory_space=pltpu.SMEM)]
        + [whole_block((MB_TOK, WIDE))] * count
        + [whole_block((tokens, WIDE))]
        + [anywhere()] * 8,
        out_specs=[chunk_block(tokens, 2 * PACK)] * 3
        + [chunk_block(WIDE, 2 * PACK)]
        + [anywhere()] * 2,
        out_shape=[rows, rows, rows, jax.ShapeDtypeStruct((2, WIDE, 2 * PACK), bf16), part, part],
        scratch_shapes=[
            pltpu.VMEM((SLOTS, SLOT, 2 * PACK), bf16),
            pltpu.VMEM((SLOTS, SLOT, 2 * PACK), bf16),
            pltpu.VMEM((2, 2, REPS, SLOT, PACK), bf16),
            pltpu.VMEM((WIDE, tokens), bf16),
            pltpu.VMEM((WIDE, tokens), bf16),
            pltpu.VMEM((2, SLOTS, SLOT, PACK), bf16),
            pltpu.VMEM((2, SLOTS, SLOT, PACK), bf16),
            pltpu.VMEM((WIDE, 2 * PACK), f32),
            pltpu.VMEM((2, 2, REPS, SLOT, PACK), bf16),
            pltpu.SemaphoreType.DMA((8,)),
            pltpu.SemaphoreType.DMA((16,)),
            pltpu.SemaphoreType.DMA((44,)),
        ],
        compiler_params=pltpu.CompilerParams(vmem_limit_bytes=VMEM_BYTES),
        cost_estimate=pl.CostEstimate(
            flops=30_000_000_000, bytes_accessed=50_000_000, transcendentals=2_000_000
        ),
        name="mlp",
    )(here, *normed, cotangent, *parts)


def mlp_outputs_kernel(hidden, d_gate, d_up, w_down, *refs, count):
    parts = refs[:8]
    outs, d_normed = (refs[8 : 8 + count], refs[8 + count : 8 + 2 * count])
    w_gate, w_up, sem_pair = refs[8 + 2 * count :]
    step = pl.program_id(0)

    def fetches(at):
        return pair_fetches(parts, at, w_gate.at[at], w_up.at[at], sem_pair.at[at])

    @pl.when(step == 0)
    def _():
        for at in range(2):
            for copy in fetches(at):
                copy.start()

    for at in range(2):

        @pl.when(step == at)
        def _():
            for copy in fetches(at):
                copy.wait()
            gate_weights = w_gate[at].reshape(WIDE, 2 * PACK)
            up_weights = w_up[at].reshape(WIDE, 2 * PACK)
            for batch in range(count):
                rows = slice(batch * MB_TOK, batch * MB_TOK + MB_TOK)
                out_part = dot_nt(hidden[0, rows, :], w_down[0])
                normed_part = dot_nt(d_gate[0, rows, :], gate_weights) + dot_nt(
                    d_up[0, rows, :], up_weights
                )
                if at == 0:
                    outs[batch][...] = out_part
                    d_normed[batch][...] = normed_part
                else:
                    outs[batch][...] += out_part
                    d_normed[batch][...] += normed_part


def mlp_outputs(hidden, d_gate, d_up, w_down, parts):
    tokens = hidden.shape[1]
    count = tokens // MB_TOK
    outs = pl.pallas_call(
        lambda *refs: mlp_outputs_kernel(*refs, count=count),
        grid=(2,),
        in_specs=[chunk_block(tokens, 2 * PACK)] * 3
        + [chunk_block(WIDE, 2 * PACK)]
        + [anywhere()] * 8,
        out_specs=[whole_block((MB_TOK, WIDE))] * (2 * count),
        out_shape=[jax.ShapeDtypeStruct((MB_TOK, WIDE), f32)] * (2 * count),
        scratch_shapes=[
            pltpu.VMEM((2, SLOTS, SLOT, 2 * PACK), bf16),
            pltpu.VMEM((2, SLOTS, SLOT, 2 * PACK), bf16),
            pltpu.SemaphoreType.DMA((2, 8)),
        ],
        compiler_params=pltpu.CompilerParams(vmem_limit_bytes=VMEM_BYTES),
        cost_estimate=pl.CostEstimate(
            flops=15_000_000_000, bytes_accessed=35_000_000, transcendentals=0
        ),
        name="mlp_outputs",
    )(hidden, d_gate, d_up, w_down, *parts)
    return (outs[:count], outs[count:])


def attn_backward_kernel(
    here,
    cotangent,
    middle,
    d_normed_two,
    inputs,
    query_rot,
    key_both,
    value_both,
    probs_in,
    cosines,
    sines,
    *refs,
):
    parts = refs[:8]
    (
        token_grad,
        wire_in,
        wire_out,
        gain_sums,
        attn_all,
        slots,
        head_parts,
        key_parts,
        value_parts,
        d_mixed_heads,
        sems,
    ) = refs[8:]
    eighth_here, quarter_here = (here[0], here[1])
    fetches = attn_fetches(parts, attn_all, sems)
    for copy in fetches:
        copy.start()
    mid = middle[...]
    upstream = d_normed_two[...]
    scale_two = lax.rsqrt(jnp.sum(mid * mid, axis=1, keepdims=True) * (1.0 / D) + norm_epsilon)
    term_two = jnp.sum(upstream * mid * scale_two, axis=0, keepdims=True)
    for copy in fetches:
        copy.wait()
    gain_one, gain_two = (gain_row(attn_all, 0), gain_row(attn_all, 1))
    weighted = upstream * gain_two
    inner = jnp.sum(weighted * mid, axis=1, keepdims=True) * (1.0 / D)
    d_middle = (
        cotangent[...].astype(f32)
        + scale_two * weighted
        - mid * scale_two * scale_two * scale_two * inner
    )
    for s in range(SLOTS):
        slots[s] = d_middle[:, s * SLOT : s * SLOT + SLOT]

    def slot_at(eighth):
        return slots[slot_of(eighth ^ eighth_here)]

    for quarter in range(REPS):
        first = (quarter ^ quarter_here) * 2
        tiles = laid(
            [([slot_at(first)], 0, 16, USED), ([slot_at(first + 1)], 0, 16 + USED, USED)], MB_TOK, 2
        )
        wire_out[:, quarter * 256 : quarter * 256 + 256] = joined(tiles).astype(bf16)
    output_columns = joined([block_columns(attn_all, q, 384, 640) for q in range(REPS)])
    d_mixed = dot_nt(wire_out[...], output_columns)
    for s in range(SLOTS):
        slots[s] = d_mixed[:, s * SLOT : s * SLOT + SLOT]
    tiles = laid([([slot_at(e)], 0, USED * e, USED) for e in range(SLOTS)], MB_TOK, 8)
    for c in range(8):
        d_mixed_heads[:, c * 128 : c * 128 + 128] = tiles[c].astype(bf16)
    for j in range(KV_HEADS):
        at = slice(j * 128, j * 128 + 128)
        for part in (2, 1, 0):
            keys = 128 * (part + 1)
            rows = slice(part * 128, part * 128 + 128)

            def three(ref):
                return jnp.concatenate(
                    [
                        only_half(ref[rows, (h // 2) * 128 : (h // 2) * 128 + 128], h % 2)
                        for h in range(3 * j, 3 * j + 3)
                    ],
                    axis=0,
                )

            queries = three(query_rot)
            d_mix = three(d_mixed_heads)
            probs = probs_in[j, :, probs_at(part) : probs_at(part) + keys]
            probs_f = probs.astype(f32)
            d_probs = dot_nt(d_mix, value_both[0:keys, at])
            product = probs_f * d_probs
            d_scores = product - probs_f * jnp.sum(product, axis=1, keepdims=True)
            d_scores = d_scores.astype(bf16)
            d_query = dot_nn(d_scores, key_both[0:keys, at])
            for g in range(GROUP):
                head_parts[3 * j + g, rows, :] = d_query[g * 128 : g * 128 + 128]
            d_key = dot_tn(d_scores, queries)
            d_value = dot_tn(probs, d_mix)
            if part == 2:
                key_parts[j] = d_key
                value_parts[j] = d_value
            else:
                key_parts[j, 0:keys, :] += d_key
                value_parts[j, 0:keys, :] += d_value

    low = lane_index((MB_TOK, 128)) < 64
    cosine, sine = (cosines[...], sines[...])
    empty = jnp.zeros((MB_TOK, 128), f32)

    def paired_heads(parts_of, count, c):
        return jnp.where(low, parts_of(2 * c), parts_of(2 * c + 1) if 2 * c + 1 < count else empty)

    def summed(ref):
        return lambda j: ref[j] + pltpu.roll(ref[j], 64, 1)

    query_tiles = [
        turned(paired_heads(lambda h: head_parts[h], HEADS, c) * HEAD**-0.5, cosine, -sine)
        for c in range(8)
    ]
    key_tiles = [
        turned(paired_heads(summed(key_parts), KV_HEADS, c) * HEAD**-0.5, cosine, -sine)
        for c in range(3)
    ]
    value_tiles = [paired_heads(summed(value_parts), KV_HEADS, c) for c in range(3)]
    for r in range(REPS):
        tiles = laid(
            [
                (query_tiles, 240 * r, 0, 240),
                (key_tiles, 80 * r, 240, 80),
                (value_tiles, 80 * r, 320, 80),
            ],
            MB_TOK,
            4,
        )
        wire_in[r ^ quarter_here] = joined(tiles).astype(bf16)
    d_normed = sum(
        dot_nt(wire_in[quarter], block_columns(attn_all, quarter, 0, 512))
        for quarter in range(REPS)
    )
    values = inputs[...].astype(f32)
    scale = lax.rsqrt(jnp.sum(values * values, axis=1, keepdims=True) * (1.0 / D) + norm_epsilon)
    weighted = d_normed * gain_one
    inner = jnp.sum(weighted * values, axis=1, keepdims=True) * (1.0 / D)
    term_one = jnp.sum(d_normed * values * scale, axis=0, keepdims=True)
    total = d_middle + scale * weighted - values * scale * scale * scale * inner
    token_grad[...] = total.astype(bf16)
    gain_sums[0:1, :] = term_one
    gain_sums[1:2, :] = term_two


def attn_grads_kernel(*refs, count):
    normed, mixed, wires_in, wires_out, gain_parts = [
        refs[n * count : n * count + count] for n in range(5)
    ]
    arrays = refs[5 * count : 5 * count + 2]
    gain_sums = sum(part[0:8, :] for part in gain_parts)

    def stacked(parts, *at):
        return jnp.concatenate([part[at] for part in parts], axis=0)

    normed_turned = stacked(normed, ...).T
    mixed_turned = stacked(mixed, ...).T
    wire_out = stacked(wires_out, ...)
    row = lax.broadcasted_iota(jnp.int32, (SLOTS, 16, SLOT), 1)
    gain_rows = jnp.zeros((SLOTS, 16, SLOT), f32)
    for which in range(2):
        spots = [
            gain_sums[which : which + 1, s * SLOT : s * SLOT + SLOT].reshape(1, 1, SLOT)
            for s in range(SLOTS)
        ]
        gain_rows = jnp.where(row == 8 + which, jnp.concatenate(spots, axis=0), gain_rows)
    for quarter in range(REPS):
        first = dot_nn(normed_turned, stacked(wires_in, quarter))
        second = dot_nn(mixed_turned, wire_out[:, quarter * 256 : quarter * 256 + 256])
        block = jnp.concatenate(
            [first[:, 0:384], first[:, 384:512] + second[:, 0:128], second[:, 128:256]], axis=1
        ).reshape(SLOTS, SLOT, PACK)
        y, core = (quarter >> 1, quarter & 1)
        low_rows = block[:, 0:ROWS_A, :].astype(bf16)
        high_rows = block[:, ROWS_A:SLOT, :].astype(bf16)
        target = arrays[core]
        target[0, y, :, :, :] = low_rows
        tail = (block[:, 112:SLOT, 0:SLOT] + gain_rows).astype(bf16)
        for side in range(2):
            slots = slice(side * 4, side * 4 + 4)
            target[1, side, y * 4 : y * 4 + 4, :, :] = high_rows[slots]
            target[1, side, y * 4 : y * 4 + 4, 48:64, 0:SLOT] = tail[slots]


def attn_backward(
    batch,
    here,
    cotangent,
    middle,
    d_normed_two,
    inputs,
    query_rot,
    key_both,
    value_both,
    probs,
    tables,
    parts,
):
    one = [middle, d_normed_two]
    own = [query_rot, key_both, value_both, probs]
    outs = [
        ((MB_TOK, WIDE), bf16),
        ((REPS, MB_TOK, 512), bf16),
        ((MB_TOK, REPS * 256), bf16),
        ((8, WIDE), f32),
    ]
    return pl.pallas_call(
        attn_backward_kernel,
        grid=(1,),
        in_specs=[in_scalars(), batch_block(batch, WIDE)]
        + [whole_block(array.shape) for array in one]
        + [batch_block(batch, WIDE)]
        + [whole_block(array.shape) for array in own]
        + [batch_block(batch, 128)] * 2
        + [anywhere()] * 8,
        out_specs=[whole_block(out[0]) for out in outs],
        out_shape=[jax.ShapeDtypeStruct(*out) for out in outs],
        scratch_shapes=[
            pltpu.VMEM((REPS, SLOTS, SLOT, PACK), bf16),
            pltpu.VMEM((SLOTS, MB_TOK, SLOT), f32),
            pltpu.VMEM((HEADS, MB_TOK, 128), f32),
            pltpu.VMEM((KV_HEADS, MB_TOK, 128), f32),
            pltpu.VMEM((KV_HEADS, MB_TOK, 128), f32),
            pltpu.VMEM((MB_TOK, WIDE), bf16),
            pltpu.SemaphoreType.DMA((12,)),
        ],
        compiler_params=pltpu.CompilerParams(vmem_limit_bytes=VMEM_BYTES),
        cost_estimate=pl.CostEstimate(
            flops=12_000_000_000, bytes_accessed=20_000_000, transcendentals=0
        ),
        name="attn_backward",
    )(here, cotangent, *one, inputs, *own, *tables, *parts)


def attn_grads(normed, mixed, wires_in, wires_out, gain_parts):
    count = len(normed)
    half = jax.ShapeDtypeStruct((2, 2, SLOTS, ROWS_A, PACK), bf16)
    arrays = (*normed, *mixed, *wires_in, *wires_out, *gain_parts)
    return pl.pallas_call(
        lambda *refs: attn_grads_kernel(*refs, count=count),
        grid=(1,),
        in_specs=[whole_block(array.shape) for array in arrays],
        out_specs=[whole_block(half.shape)] * 2,
        out_shape=[half] * 2,
        compiler_params=pltpu.CompilerParams(vmem_limit_bytes=VMEM_BYTES),
        cost_estimate=pl.CostEstimate(
            flops=8_000_000_000, bytes_accessed=14_000_000, transcendentals=0
        ),
        name="attn_grads",
    )(*arrays)


X_SIDE = ("fsdp", 1)
Y_SIDE = ("rep", 2)
CORE = ("rep", 1)


def swap_with(values, step):
    axis, mask = step
    count = lax.axis_size(axis)
    return lax.ppermute(values, axis, [(i, i ^ mask) for i in range(count)])


def after(values, *done):
    return lax.optimization_barrier((values, done))[0]


def sent_along_z(block):
    return [swap_with(block, ("fsdp", 2 * k)) for k in range(1, 4)]


def along_z(block, came):
    return jnp.stack([block] + list(came))


def sides_of(side_first):
    return (X_SIDE, Y_SIDE) if side_first else (Y_SIDE, X_SIDE)


def sent_along_first(four, side_first):
    return swap_with(four, sides_of(side_first)[0])


def along_first(four, side_first):
    return jnp.concatenate([four, sent_along_first(four, side_first)])


def along_second(eight, side_first):
    return swap_with(eight, sides_of(side_first)[1])


def along_core(eight, across):
    return (eight, swap_with(eight, CORE), across, swap_with(across, CORE))


def added(left, right):
    return (left.astype(f32) + right.astype(f32)).astype(bf16)


class Reduction:
    def __init__(self, kept, came, which, side_first):
        self.kept = kept
        self.came = came
        self.which = which
        self.first, self.second = sides_of(side_first)
        self.out = added(kept[which, 1], came[which, 1])

    def sent_second(self):
        return swap_with(self.out, self.second)

    def over_second(self, came):
        self.second_came = came
        kept, before = after((self.kept, self.came), came)
        terms = (kept[self.which, 0, 4:8], before[self.which, 0, 4:8], came[4:8])
        self.out = sum(term.astype(f32) for term in terms).astype(bf16)

    def sent_first(self):
        return swap_with(self.out, self.first)

    def over_first(self, came):
        kept, before, second, came = after((self.kept, self.came, self.second_came, came), came)
        self.blocks = [
            sum(
                term.astype(f32)
                for term in (kept[self.which, 0, k], before[self.which, 0, k], second[k], came[k])
            ).astype(bf16)
            for k in range(4)
        ]


def z_stage(one, two):
    blocks = [jnp.concatenate([one.blocks[k], two.blocks[k]], axis=0) for k in range(4)]
    return (blocks[0], [swap_with(blocks[k], ("fsdp", 2 * k)) for k in range(1, 4)])


def z_sum(kept, came):
    return sum((block.astype(f32) for block in came), kept.astype(f32))


def split_parts(blocks, side_first):
    rows, columns = blocks.shape[2:]
    grid = blocks.reshape(4, 2, 2, 2, rows, columns)
    parts = []
    for second in range(2):
        for core in range(2):
            if side_first:
                part = grid[:, :, second, core].transpose(1, 0, 2, 3)
            else:
                part = grid[:, second, :, core].transpose(1, 0, 2, 3)
            parts.append(part.reshape(SLOTS, rows, columns))
    return parts


def eight_parts(first_blocks, second_blocks):
    return (*split_parts(first_blocks, True), *split_parts(second_blocks, False))


def join_parts(kept, sent, side_first):
    rows, columns = kept.shape[2:]
    grid = jnp.stack([kept, sent]).reshape(2, 2, 2, 4, rows, columns)
    grid = grid.transpose(3, 2, 1, 0, 4, 5) if side_first else grid.transpose(3, 1, 2, 0, 4, 5)
    return grid.reshape(SLOTS, REPS, rows, columns)


def attn_block(w_query, w_key, w_value, w_output, attn_gain, mlp_gain):
    matrices = jnp.concatenate([w_query, w_key, w_value, w_output], axis=1)
    gains = jnp.stack([attn_gain, mlp_gain])
    gains = jnp.pad(gains, ((0, SLOT - USED - 2), (0, PACK - USED)))
    return jnp.concatenate([matrices, gains], axis=0)


def down_block(w_down):
    halves = w_down.T.reshape(2, USED, HALF_PACK)
    halves = jnp.concatenate([halves[0], halves[1]], axis=1)
    return jnp.pad(halves, ((0, SLOT - USED), (0, 0)))


def mlp_block(w_gate, w_up, w_down):
    taller = ((0, SLOT - USED), (0, 0))
    return jnp.concatenate([jnp.pad(w_gate, taller), jnp.pad(w_up, taller), down_block(w_down)])


def down_of(block):
    halves = jnp.stack([block[:USED, :HALF_PACK], block[:USED, HALF_PACK:]])
    return halves.reshape(2 * USED, HALF_PACK).T


def whole(shard):
    return lax.all_gather(lax.all_gather(shard, "rep", axis=1, tiled=True), "fsdp", axis=0, tiled=True)


def cut(matrix, eighth, quarter):
    rows, columns = (matrix.shape[0] // SLOTS, matrix.shape[1] // REPS)
    return matrix[
        eighth * rows : eighth * rows + rows, quarter * columns : quarter * columns + columns
    ]


def every_block(make):
    return jnp.stack(
        [jnp.stack([make(e, q) for q in range(REPS)]) for e in range(SLOTS)]
    )


def owned(blocks):
    eighths, quarters, rows, columns = blocks.shape
    matrix = blocks.transpose(0, 2, 1, 3).reshape(eighths * rows, quarters * columns)
    part = lax.psum_scatter(matrix, "fsdp", scatter_dimension=0, tiled=True)
    return lax.psum_scatter(part, "rep", scatter_dimension=1, tiled=True).astype(f32)


def per_device(
    tokens,
    lengths,
    attn_gain,
    w_query,
    w_key,
    w_value,
    w_output,
    mlp_gain,
    w_gate,
    w_up,
    w_down,
    cotangent,
):
    paired = lax.axis_size("fsdp") == SLOTS and lax.axis_size("rep") == REPS
    if paired:
        eighth_here = lax.axis_index("fsdp").astype(jnp.int32)
        quarter_here = lax.axis_index("rep").astype(jnp.int32)
    else:
        eighth_here = jnp.int32(0)
        quarter_here = jnp.int32(0)
    here = jnp.stack([eighth_here, quarter_here])
    spread = spreading(eighth_here)
    segments, positions = jax.vmap(layout)(lengths)
    segments = (segments.reshape(-1, 1), segments.reshape(-1, 1, MB_TOK))
    tables = rope_tables(positions.reshape(-1))
    inputs = jnp.dot(tokens, spread, preferred_element_type=f32).astype(bf16)
    upstream = jnp.dot(cotangent, spread, preferred_element_type=f32).astype(bf16)
    batches = range(tokens.shape[0] // MB_TOK)
    forward_inputs = [inputs for _ in batches]

    if paired:
        attn_pack = attn_block(w_query, w_key, w_value, w_output, attn_gain, mlp_gain)
        pack = mlp_block(w_gate, w_up, w_down)
        attn_four = along_z(attn_pack, sent_along_z(attn_pack))
        three, four, attn_four = lax.optimization_barrier((pack[:ROWS_W], pack[ROWS_W:], attn_four))
        three_came = sent_along_z(three)
        one, two = (attn_four[:, :ROWS_A], attn_four[:, ROWS_A:])
        came = (sent_along_first(one, True), sent_along_first(two, False))
        three_came, came, four = lax.optimization_barrier((three_came, came, four))
        one, two = (jnp.concatenate([one, came[0]]), jnp.concatenate([two, came[1]]))
        four_came = sent_along_z(four)
        across = (along_second(one, True), along_second(two, False))
        four_came, across, inputs, upstream, tables, segments, here = lax.optimization_barrier(
            (four_came, across, inputs, upstream, tables, segments, here)
        )
        three, four = (along_z(three, three_came), along_z(four, four_came))
        attn_parts = (*along_core(one, across[0]), *along_core(two, across[1]))
        came = (sent_along_first(three, True), sent_along_first(four, False))
        came = after(came, attn_parts)
        three, four = (jnp.concatenate([three, came[0]]), jnp.concatenate([four, came[1]]))
        across = (along_second(three, True), along_second(four, False))
        near = (swap_with(three, CORE), swap_with(four, CORE))
        forward_inputs[0] = after(inputs, three, four)
    else:
        gain_one, gain_two = (
            lax.all_gather(attn_gain, "fsdp", axis=0, tiled=True).reshape(SLOTS, USED),
            lax.all_gather(mlp_gain, "fsdp", axis=0, tiled=True).reshape(SLOTS, USED),
        )
        mats = [whole(w) for w in (w_query, w_key, w_value, w_output, w_gate, w_up, w_down)]
        attn_blocks = every_block(
            lambda e, q: attn_block(*[cut(m, e, q) for m in mats[:4]], gain_one[e], gain_two[e])
        )
        attn_parts = eight_parts(attn_blocks[:, :, :ROWS_A], attn_blocks[:, :, ROWS_A:])
        mlp_blocks = every_block(
            lambda e, q: mlp_block(cut(mats[4], e, q), cut(mats[5], e, q), cut(mats[6], e, q))
        )
        mlp_parts = eight_parts(mlp_blocks[:, :, :ROWS_W], mlp_blocks[:, :, ROWS_W:])

    made = []
    for batch in batches:
        made.append(attn_forward(batch, here, forward_inputs[batch], attn_parts, tables, segments))
        if paired and batch == 0:
            forward_inputs[-1] = after(inputs, near, made[0][-1])
    normed, query_rot, key_both, value_both, probs, mixed, middle, normed_two = zip(*made)
    if paired:
        across = after(across, normed_two[-1])
        far = (swap_with(across[0], CORE), swap_with(across[1], CORE))
        mlp_parts = (three, near[0], across[0], far[0], four, near[1], across[1], far[1])
    hidden, d_gate, d_up, w_down_all, kept, sent = mlp(
        here, normed_two, upstream, mlp_parts
    )
    mlp_out, d_normed_two = mlp_outputs(hidden, d_gate, d_up, w_down_all, mlp_parts)
    d_normed_two = list(d_normed_two)
    if paired:
        came = swap_with(sent, CORE)
        gate_sums = [Reduction(kept, came, which, which == 0) for which in range(2)]
        up_sums = [Reduction(kept, came, 2 + which, which == 0) for which in range(2)]
        d_normed_two[0] = after(d_normed_two[0], gate_sums[0].out, gate_sums[1].out)
    back = []
    for batch in batches:
        back.append(
            attn_backward(
                batch,
                here,
                upstream,
                middle[batch],
                d_normed_two[batch],
                inputs,
                query_rot[batch],
                key_both[batch],
                value_both[batch],
                probs[batch],
                tables,
                attn_parts,
            )
        )
        if paired and batch == 0:
            for part in gate_sums:
                part.over_second(part.sent_second())
            for part in up_sums:
                part.out = after(part.out, gate_sums[0].out, gate_sums[1].out)
            d_normed_two[-1] = after(d_normed_two[-1], up_sums[0].out, up_sums[1].out)
    token_rows, wires_in, wires_out, gain_parts = zip(*back)
    if paired:
        for part in up_sums:
            part.over_second(part.sent_second())
        for part in gate_sums:
            part.over_first(part.sent_first())
        wires_in = after(
            wires_in, up_sums[0].out, up_sums[1].out, gate_sums[0].blocks, gate_sums[1].blocks
        )
    attn_kept, attn_sent = attn_grads(
        normed, mixed, wires_in, wires_out, gain_parts
    )
    if paired:
        up_came = [part.sent_first() for part in up_sums]
        gate_kept, gate_came = z_stage(*gate_sums)
        up_came, gate_came, attn_sent = lax.optimization_barrier((up_came, gate_came, attn_sent))
        came = swap_with(attn_sent, CORE)
        for part, part_came in zip(up_sums, up_came):
            part.over_first(part_came)
        one, two = [Reduction(attn_kept, came, which, which == 0) for which in range(2)]
        up_kept, up_came = z_stage(*up_sums)
        across = (one.sent_second(), two.sent_second())
        up_first, up_second, up_last = up_came
        up_first, up_second, across = lax.optimization_barrier((up_first, up_second, across))
        one.over_second(across[0])
        two.over_second(across[1])
        came = (one.sent_first(), two.sent_first())
        came, up_last = lax.optimization_barrier((came, up_last))
        tail = came
        one.over_first(came[0])
        two.over_first(came[1])
        gate_sum = z_sum(gate_kept, gate_came)
        up_sum = z_sum(up_kept, (up_first, up_second, up_last))
        attn_sum = z_sum(*z_stage(one, two))
        gain_sums = (attn_sum[USED, :USED], attn_sum[USED + 1, :USED])
        attn_sum = attn_sum[:USED]
        grads = [
            attn_sum[:, 0:240],
            attn_sum[:, 240:320],
            attn_sum[:, 320:400],
            attn_sum[:, 400:640],
            gate_sum[:USED],
            up_sum[:USED],
            down_of(jnp.concatenate([gate_sum[SLOT:], up_sum[SLOT:]], axis=0)),
        ]
    else:
        tail = (attn_kept,)
        attn_blocks = jnp.concatenate(
            [join_parts(attn_kept[k], attn_sent[k], k == 0) for k in range(2)], axis=2
        )
        gain_sums = tuple(
            lax.psum(
                lax.psum_scatter(
                    attn_blocks[:, 0, USED + which, :USED].astype(f32).reshape(D),
                    "fsdp",
                    scatter_dimension=0,
                    tiled=True,
                ),
                "rep",
            )
            for which in range(2)
        )
        attn_blocks = attn_blocks[:, :, :USED]
        gate_blocks, up_blocks = [
            jnp.concatenate(
                [join_parts(kept[k], sent[k], k % 2 == 0) for k in (which, which + 1)], axis=2
            )
            for which in (0, 2)
        ]
        down_blocks = jnp.concatenate([gate_blocks[:, :, SLOT:], up_blocks[:, :, SLOT:]], axis=2)
        grads = [
            owned(attn_blocks[..., 0:240]),
            owned(attn_blocks[..., 240:320]),
            owned(attn_blocks[..., 320:400]),
            owned(attn_blocks[..., 400:640]),
            owned(gate_blocks[:, :, :USED]),
            owned(up_blocks[:, :, :USED]),
            owned(jax.vmap(jax.vmap(down_of))(down_blocks)),
        ]
    middle, mlp_out, token_rows = after((middle, mlp_out, token_rows), *tail)
    output_rows = jnp.concatenate(
        [(middle[batch] + mlp_out[batch]).astype(bf16) for batch in batches], axis=0
    )
    output = jnp.dot(output_rows, spread.T, preferred_element_type=f32).astype(bf16)
    token_grad = jnp.dot(
        jnp.concatenate(token_rows, axis=0), spread.T, preferred_element_type=f32
    ).astype(bf16)
    return (
        output,
        token_grad,
        gain_sums[0],
        grads[0],
        grads[1],
        grads[2],
        grads[3],
        gain_sums[1],
        grads[4],
        grads[5],
        grads[6],
    )


def solution(mesh):
    placed = (
        P(("fsdp", "rep"), None),
        P(("fsdp", "rep"), None),
        P("fsdp"),
        P("fsdp", "rep"),
        P("fsdp", "rep"),
        P("fsdp", "rep"),
        P("fsdp", "rep"),
        P("fsdp"),
        P("fsdp", "rep"),
        P("fsdp", "rep"),
        P("fsdp", "rep"),
        P(("fsdp", "rep"), None),
    )
    return jax.shard_map(
        per_device,
        mesh=mesh,
        in_specs=placed,
        out_specs=(
            P(("fsdp", "rep"), None),
            P(("fsdp", "rep"), None),
            P("fsdp"),
            P("fsdp", "rep"),
            P("fsdp", "rep"),
            P("fsdp", "rep"),
            P("fsdp", "rep"),
            P("fsdp"),
            P("fsdp", "rep"),
            P("fsdp", "rep"),
            P("fsdp", "rep"),
        ),
        check_vma=False,
    )
```
